32 devices in a mesh: groups: 2 (over x), row: 16 (over z, y, core).
Axes of the slice: x: 2, y: 2, z: 4, core: 2. Of those that a mesh axis runs over, the one named last changes fastest.
Arguments:
- basis: float32 [8192, 128], P(('groups', 'row')), parts along dimension 0, may hold values from -6 to 6
- springs: float32 [8192], P(('groups', 'row')), parts along dimension 0, may hold values from 0.25 to 8
- tangent_blocks: float32 [4096, 4096], P(('groups', 'row')), parts along dimension 0, may hold values from -0.375 to 0.375
- tile_rows: int32 [4096], P(('groups', 'row')), parts along dimension 0, may hold values from 0 to 3
- tile_owner: int32 [4096, 1], P(('groups', 'row')), parts along dimension 0, may hold values from 0 to 15, as said below
- tile_offset: int32 [4096], P(('groups', 'row')), parts along dimension 0, may hold values from 0 to 3
- tile_count: int32 [32], P(('groups', 'row')), parts along dimension 0, may hold values from 32 to 128, as said below
Outputs:
- stiff_image: float32 [8192, 128], P(('groups', 'row')), parts along dimension 0
- reduced: float32 [256, 128], P('groups'), parts along dimension 0
The draws below stay inside these ranges and needn't reach their ends.
There are 2 independent parts, one for each index of `groups`. The reference program is written for one: setup_inputs(seed, part) draws one part's arguments, and reference() takes and returns one part's arrays. A program takes and returns all parts, laid end to end along the dimension named above; each array names one. Nothing has to cross between parts.
Inputs may be any that keep to these rules, and one draw needn't show every extreme that they name: The first tile_count[d] slots of device d are live; some device has exactly 128. `tile_owner`: the slab is closed into a shell: every slot of device d names owner (d + o) mod 16 with o one of 0, 1, -1, 4, -4, 5, -5, 8. Among the slots of one device no owner appears more than 32 times, and owner d itself appears exactly 32 times in every device.
All inputs are finite; a program needn't handle non-finite values.
Results may differ from the reference program's by a relative error of at most 0.0003.
Values sent between devices are 32-bit elements; how exact they have to be, the bound alone decides.
No kernel may reach another device: no remote copies, remote signals or barrier semaphores. Data moves between devices by JAX's collectives and lax.ppermute only.
A program may use at most 128 MiB of HBM per device.

```python
import math
import jax
import jax.numpy as jnp
from jax import lax

B = 64
MODES = 128
BR_DEV = 4
CAP = 128
MOST = 32
NB = 64
NDOF = 4096
SLOTS = 2048
N_ROW = 16


def draw_tile_count(key, part):
    first_key, second_key = jax.random.split(jax.random.fold_in(key, 17))
    counts = jax.random.randint(first_key, (N_ROW,), CAP // 4, CAP + 1)
    fullest = jax.random.randint(second_key, (), 0, N_ROW)
    return jnp.where(jnp.arange(N_ROW) == fullest, CAP, counts).astype(jnp.int32)


def draw_tile_owner(key, part):
    base_key = jax.random.fold_in(key, 29)
    steps_list = jnp.array([0, 1, -1, 4, -4, 5, -5, N_ROW // 2], dtype=jnp.int32)
    slot_ids = jnp.arange(CAP, dtype=jnp.int32)
    pattern = jnp.where(slot_ids < MOST, 0, 1 + (slot_ids - MOST) % 7).astype(jnp.int32)

    def one_device(device):
        order = jax.random.permutation(jax.random.fold_in(base_key, device), CAP)
        links = pattern[order]
        return ((device + steps_list[links]) % N_ROW).astype(jnp.int32)
    owners = jax.vmap(one_device)(jnp.arange(N_ROW, dtype=jnp.int32))
    return owners.reshape(SLOTS, 1).astype(jnp.int32)


def set_ends(entries, rng, smallest, top_value):
    extent = entries.shape
    place = [jax.random.randint(jax.random.fold_in(rng, axis), (), 0, extent[axis]) for axis in range(len(extent))]
    entries = entries.at[tuple(place)].set(smallest)
    longest = extent.index(max(extent))
    place[longest] = (place[longest] + 1) % extent[longest]
    return entries.at[tuple(place)].set(top_value)


def steps_of(key, extent, cuts, smallest, high):
    def one(axis_at, parts):
        heights = jax.random.uniform(jax.random.fold_in(jax.random.fold_in(key, 6), axis_at), (parts,), jnp.float32, smallest / len(cuts), high / len(cuts))
        return jnp.repeat(jnp.exp(heights), extent[axis_at] // parts).reshape((-1,) + (1,) * (len(extent) - axis_at - 1))

    factor_of = one(*cuts[0])
    for cut in cuts[1:]:
        factor_of = factor_of * one(*cut)
    return factor_of


def scatter_about(rng, shape, scale, reach, shards=(), kind=jnp.bfloat16):
    factor_of = steps_of(rng, shape, shards, -0.22, 0.18) if shards else 1.0
    drawn = jax.random.normal(rng, shape, jnp.float32) * scale * factor_of
    return jnp.minimum(jnp.maximum(drawn, -reach), reach).astype(kind)


def setup_inputs(seed: int = 0, part: int = 0) -> dict:
    streams_of = jax.random.split(jax.random.key(seed), 8)
    own_keys = jax.random.split(jax.random.fold_in(streams_of[7], part), 8)
    return {
        "basis": scatter_about(own_keys[0], (NDOF, MODES), 1.0, 6.0, ((0, 16),), jnp.float32),
        "springs": jnp.clip(jnp.exp(math.log(8.0) - 3.465736 * jax.random.uniform(own_keys[1], (NDOF,), jnp.float32) ** steps_of(own_keys[1], (NDOF,), ((0, 16),), -0.2, 0.2)), 0.25, 8.0),
        "tangent_blocks": scatter_about(own_keys[2], (SLOTS, B * B), 0.025, 0.375, ((0, 16),), jnp.float32),
        "tile_rows": set_ends(jax.random.randint(own_keys[3], (SLOTS,), 0, BR_DEV), jax.random.fold_in(own_keys[3], 1), 0, BR_DEV - 1).astype(jnp.int32),
        "tile_owner": draw_tile_owner(jax.random.fold_in(jax.random.fold_in(streams_of[7], part), 71), part),
        "tile_offset": set_ends(jax.random.randint(own_keys[5], (SLOTS,), 0, BR_DEV), jax.random.fold_in(own_keys[5], 1), 0, BR_DEV - 1).astype(jnp.int32),
        "tile_count": draw_tile_count(jax.random.fold_in(jax.random.fold_in(streams_of[7], part), 71), part),
    }


def reference(basis, springs, tangent_blocks, tile_rows, tile_owner, tile_offset, tile_count):
    basis_blocks = basis.reshape(NB, B, MODES)
    square_blocks = tangent_blocks.reshape(SLOTS, B, B)
    owner_ids = tile_owner[:, 0]
    devices = jnp.arange(N_ROW, dtype=jnp.int32)

    def one_device(device):
        first_slot = (device * CAP).astype(jnp.int32)
        blocks = lax.dynamic_slice_in_dim(square_blocks, first_slot, CAP, 0)
        rows_here = lax.dynamic_slice_in_dim(tile_rows, first_slot, CAP, 0)
        owners_here = lax.dynamic_slice_in_dim(owner_ids, first_slot, CAP, 0)
        offsets_here = lax.dynamic_slice_in_dim(tile_offset, first_slot, CAP, 0)
        columns = (owners_here * BR_DEV + offsets_here).astype(jnp.int32)
        picked = basis_blocks[columns]
        products = jnp.einsum('sij,sjk->sik', blocks, picked, precision=lax.Precision.HIGHEST)
        live_slot = (jnp.arange(CAP, dtype=jnp.int32) < tile_count[device]).astype(jnp.float32)
        row_select = (rows_here[None, :] == jnp.arange(BR_DEV, dtype=jnp.int32)[:, None]).astype(jnp.float32) * live_slot[None, :]
        return jnp.dot(row_select, products.reshape(CAP, B * MODES), precision=lax.Precision.HIGHEST)

    summed = lax.map(one_device, devices)
    stiff_image = springs[:, None] * basis + summed.reshape(NDOF, MODES)
    reduced = jnp.einsum('rm,rn->mn', basis, stiff_image, precision=lax.Precision.HIGHEST) / NDOF
    return stiff_image, reduced
```

```python
import functools

import jax
import jax.numpy as jnp
from jax import lax
from jax.experimental import pallas as pl
from jax.experimental.pallas import tpu as pltpu
from jax.sharding import PartitionSpec as P

B = 64
MODES = 128
BR_DEV = 4
CAP = 128
LINKS = 8
HALF = B // 2
ROWS = BR_DEV * B


def split(x):
    high = x.astype(jnp.bfloat16)
    return high, (x - high.astype(jnp.float32)).astype(jnp.bfloat16)


def dot3(a_high, a_low, b_high, b_low):
    dot = functools.partial(jnp.dot, preferred_element_type=jnp.float32)
    return dot(a_high, b_high) + (dot(a_low, b_high) + dot(a_high, b_low))


def assemble(place_ref, count_ref, blocks_ref, basis_ref, high_ref, low_ref, turned_high_ref, turned_low_ref, slots, dense):
    @pl.loop(0, CAP // 8)
    def _(group):
        eight = blocks_ref[pl.ds(pl.multiple_of(group * 8, 8), 8), :]
        for t in range(HALF):
            slots[pl.ds(group * (8 * HALF) + t, 8, stride=HALF), :] = eight[:, t * 128:(t + 1) * 128]

    dense[...] = jnp.zeros_like(dense)

    @pl.loop(0, count_ref[0])
    def _(s):
        target = pl.ds(pl.multiple_of(place_ref[s] * HALF, HALF), HALF)
        dense[target, :] += slots[pl.ds(pl.multiple_of(s * HALF, HALF), HALF), :]

    left = lax.broadcasted_iota(jnp.int32, (HALF, 128), 1) < B

    @pl.loop(0, LINKS)
    def _(link):
        for r in range(BR_DEV):
            for pair in range(BR_DEV // 2):
                start = ((link * BR_DEV + r) * BR_DEV + 2 * pair) * HALF
                first = dense[pl.ds(pl.multiple_of(start, HALF), HALF), :]
                second = dense[pl.ds(pl.multiple_of(start + HALF, HALF), HALF), :]
                even = jnp.where(left, first, pltpu.roll(second, B, 1))
                odd = jnp.where(left, pltpu.roll(first, B, 1), second)
                for h, part in enumerate((even, odd)):
                    high, low = split(part)
                    rows = slice(r * B + h * HALF, r * B + (h + 1) * HALF)
                    high_ref[link, rows, pair * 128:(pair + 1) * 128] = high
                    low_ref[link, rows, pair * 128:(pair + 1) * 128] = low

    high, low = split(basis_ref[...].T)
    turned_high_ref[...] = high
    turned_low_ref[...] = low


def project(scale, high_ref, low_ref, turned_high_ref, turned_low_ref, base_ref, *refs):
    basis_refs, (stiff_ref, partial_ref) = refs[:LINKS], refs[LINKS:]
    total = jnp.zeros((ROWS, MODES), jnp.float32)
    for link in range(LINKS):
        b_high, b_low = split(basis_refs[link][...])
        total += dot3(high_ref[link], low_ref[link], b_high, b_low)
    for r in range(BR_DEV):
        for h in range(2):
            rows = pl.ds(r * B + h, HALF, stride=2)
            start = r * B + h * HALF
            stiff_ref[rows, :] = base_ref[rows, :] + total[start:start + HALF, :]
    s_high, s_low = split(stiff_ref[...])
    partial_ref[...] = dot3(turned_high_ref[...], turned_low_ref[...], s_high, s_low) * scale


def shards(basis, springs, tangent_blocks, tile_rows, tile_owner, tile_offset, tile_count):
    n = lax.axis_size("row")
    me = lax.axis_index("row")
    steps = (0, 1, n - 1, 4, n - 4, 5, n - 5, n // 2)
    held = [basis]
    for step in steps[1:]:
        held.append(lax.ppermute(basis, "row", [((d + step) % n, d) for d in range(n)]))

    away = (tile_owner[:, 0] - me + n) % n
    link = jnp.zeros_like(away)
    for k, step in enumerate(steps):
        link = jnp.where(away == step, k, link)
    place = (link * BR_DEV + tile_rows) * BR_DEV + tile_offset

    smem = pl.BlockSpec(memory_space=pltpu.SMEM)
    vmem = pl.BlockSpec(memory_space=pltpu.VMEM)
    half = jnp.bfloat16
    high, low, turned_high, turned_low = pl.pallas_call(
        assemble,
        out_shape=(
            jax.ShapeDtypeStruct((LINKS, ROWS, ROWS), half),
            jax.ShapeDtypeStruct((LINKS, ROWS, ROWS), half),
            jax.ShapeDtypeStruct((MODES, ROWS), half),
            jax.ShapeDtypeStruct((MODES, ROWS), half),
        ),
        in_specs=[smem, smem, vmem, vmem],
        out_specs=(vmem,) * 4,
        scratch_shapes=[pltpu.VMEM((CAP * HALF, 128), jnp.float32), pltpu.VMEM((CAP * HALF, 128), jnp.float32)],
        compiler_params=pltpu.CompilerParams(vmem_limit_bytes=32 * 2**20),
        cost_estimate=pl.CostEstimate(flops=10_000_000, bytes_accessed=12_000_000, transcendentals=0),
        name="assemble",
    )(place, tile_count, tangent_blocks, basis)

    base = springs[:, None] * basis
    stiff_image, partial = pl.pallas_call(
        functools.partial(project, 1.0 / (basis.shape[0] * n)),
        out_shape=(
            jax.ShapeDtypeStruct((ROWS, MODES), jnp.float32),
            jax.ShapeDtypeStruct((MODES, MODES), jnp.float32),
        ),
        in_specs=[vmem] * (5 + LINKS),
        out_specs=(vmem,) * 2,
        compiler_params=pltpu.CompilerParams(vmem_limit_bytes=32 * 2**20),
        cost_estimate=pl.CostEstimate(flops=6 * 67_000_000, bytes_accessed=4_000_000, transcendentals=0),
        name="project",
    )(high, low, turned_high, turned_low, base, *held)

    pieces = partial.reshape(n, MODES // n, MODES)
    mine = lax.all_to_all(pieces, "row", 0, 0).sum(axis=0)
    whole = lax.all_to_all(jnp.broadcast_to(mine[None], pieces.shape), "row", 0, 0)
    return (stiff_image, whole.reshape(MODES, MODES))


def solution(mesh):
    in_specs = (
        P(("groups", "row"), None),
        P(("groups", "row")),
        P(("groups", "row"), None),
        P(("groups", "row")),
        P(("groups", "row"), None),
        P(("groups", "row")),
        P(("groups", "row")),
    )
    out_specs = (P(("groups", "row"), None), P("groups", None))
    return jax.shard_map(shards, mesh=mesh, in_specs=in_specs, out_specs=out_specs, check_vma=False)
```

```python
import functools

import jax
import jax.numpy as jnp
from jax import lax
from jax.experimental import pallas as pl
from jax.experimental.pallas import tpu as pltpu
from jax.sharding import PartitionSpec as P

B = 64
MODES = 128
BR_DEV = 4
CAP = 128
LINKS = 8
HALF = B // 2
ROWS = BR_DEV * B


def split(x):
    high = x.astype(jnp.bfloat16)
    return high, (x - high.astype(jnp.float32)).astype(jnp.bfloat16)


def dot3(a_high, a_low, b_high, b_low):
    dot = functools.partial(jnp.dot, preferred_element_type=jnp.float32)
    return dot(a_high, b_high) + (dot(a_low, b_high) + dot(a_high, b_low))


def assemble(place_ref, count_ref, blocks_ref, basis_ref, high_ref, low_ref, turned_high_ref, turned_low_ref, slots, dense):
    @pl.loop(0, CAP // 8)
    def _(group):
        eight = blocks_ref[pl.ds(pl.multiple_of(group * 8, 8), 8), :]
        for t in range(HALF):
            slots[pl.ds(group * (8 * HALF) + t, 8, stride=HALF), :] = eight[:, t * 128:(t + 1) * 128]

    dense[...] = jnp.zeros_like(dense)

    @pl.loop(0, count_ref[0])
    def _(s):
        target = pl.ds(pl.multiple_of(place_ref[s] * HALF, HALF), HALF)
        dense[target, :] += slots[pl.ds(pl.multiple_of(s * HALF, HALF), HALF), :]

    left = lax.broadcasted_iota(jnp.int32, (HALF, 128), 1) < B

    @pl.loop(0, LINKS)
    def _(link):
        for r in range(BR_DEV):
            for pair in range(BR_DEV // 2):
                start = ((link * BR_DEV + r) * BR_DEV + 2 * pair) * HALF
                first = dense[pl.ds(pl.multiple_of(start, HALF), HALF), :]
                second = dense[pl.ds(pl.multiple_of(start + HALF, HALF), HALF), :]
                even = jnp.where(left, first, pltpu.roll(second, B, 1))
                odd = jnp.where(left, pltpu.roll(first, B, 1), second)
                for h, part in enumerate((even, odd)):
                    high, low = split(part)
                    rows = slice(r * B + h * HALF, r * B + (h + 1) * HALF)
                    high_ref[link, rows, pair * 128:(pair + 1) * 128] = high
                    low_ref[link, rows, pair * 128:(pair + 1) * 128] = low

    high, low = split(basis_ref[...].T)
    turned_high_ref[...] = high
    turned_low_ref[...] = low


def project(scale, high_ref, low_ref, turned_high_ref, turned_low_ref, base_ref, *refs):
    basis_refs, (stiff_ref, partial_ref) = refs[:LINKS], refs[LINKS:]
    total = jnp.zeros((ROWS, MODES), jnp.float32)
    for link in range(LINKS):
        b_high, b_low = split(basis_refs[link][...])
        total += dot3(high_ref[link], low_ref[link], b_high, b_low)
    for r in range(BR_DEV):
        for h in range(2):
            rows = pl.ds(r * B + h, HALF, stride=2)
            start = r * B + h * HALF
            stiff_ref[rows, :] = base_ref[rows, :] + total[start:start + HALF, :]
    s_high, s_low = split(stiff_ref[...])
    partial_ref[...] = dot3(turned_high_ref[...], turned_low_ref[...], s_high, s_low) * scale


def shards(basis, springs, tangent_blocks, tile_rows, tile_owner, tile_offset, tile_count):
    n = lax.axis_size("row")
    me = lax.axis_index("row")
    steps = (0, 1, n - 1, 4, n - 4, 5, n - 5, n // 2)
    held = [basis]
    for step in steps[1:]:
        held.append(lax.ppermute(basis, "row", [((d + step) % n, d) for d in range(n)]))

    away = (tile_owner[:, 0] - me + n) % n
    link = jnp.zeros_like(away)
    for k, step in enumerate(steps):
        link = jnp.where(away == step, k, link)
    place = (link * BR_DEV + tile_rows) * BR_DEV + tile_offset

    smem = pl.BlockSpec(memory_space=pltpu.SMEM)
    vmem = pl.BlockSpec(memory_space=pltpu.VMEM)
    half = jnp.bfloat16
    high, low, turned_high, turned_low = pl.pallas_call(
        assemble,
        out_shape=(
            jax.ShapeDtypeStruct((LINKS, ROWS, ROWS), half),
            jax.ShapeDtypeStruct((LINKS, ROWS, ROWS), half),
            jax.ShapeDtypeStruct((MODES, ROWS), half),
            jax.ShapeDtypeStruct((MODES, ROWS), half),
        ),
        in_specs=[smem, smem, vmem, vmem],
        out_specs=(vmem,) * 4,
        scratch_shapes=[pltpu.VMEM((CAP * HALF, 128), jnp.float32), pltpu.VMEM((CAP * HALF, 128), jnp.float32)],
        compiler_params=pltpu.CompilerParams(vmem_limit_bytes=32 * 2**20),
        cost_estimate=pl.CostEstimate(flops=10_000_000, bytes_accessed=12_000_000, transcendentals=0),
        name="assemble",
    )(place, tile_count, tangent_blocks, basis)

    base = springs[:, None] * basis
    stiff_image, partial = pl.pallas_call(
        functools.partial(project, 1.0 / (basis.shape[0] * n)),
        out_shape=(
            jax.ShapeDtypeStruct((ROWS, MODES), jnp.float32),
            jax.ShapeDtypeStruct((MODES, MODES), jnp.float32),
        ),
        in_specs=[vmem] * (5 + LINKS),
        out_specs=(vmem,) * 2,
        compiler_params=pltpu.CompilerParams(vmem_limit_bytes=32 * 2**20),
        cost_estimate=pl.CostEstimate(flops=6 * 67_000_000, bytes_accessed=4_000_000, transcendentals=0),
        name="project",
    )(high, low, turned_high, turned_low, base, *held)

    reduced = partial
    apart = 1
    while apart < n:
        reduced += lax.ppermute(reduced, "row", [(d, d ^ apart) for d in range(n)])
        apart *= 2
    return (stiff_image, reduced)


def solution(mesh):
    in_specs = (
        P(("groups", "row"), None),
        P(("groups", "row")),
        P(("groups", "row"), None),
        P(("groups", "row")),
        P(("groups", "row"), None),
        P(("groups", "row")),
        P(("groups", "row")),
    )
    out_specs = (P(("groups", "row"), None), P("groups", None))
    return jax.shard_map(shards, mesh=mesh, in_specs=in_specs, out_specs=out_specs, check_vma=False)
```

```python
import functools

import jax
import jax.numpy as jnp
from jax import lax
from jax.experimental import pallas as pl
from jax.experimental.pallas import tpu as pltpu
from jax.sharding import PartitionSpec as P

B = 64
MODES = 128
BR_DEV = 4
CAP = 128
LINKS = 8
LATE = 3
HALF = B // 2
ROWS = BR_DEV * B


def split(x):
    high = x.astype(jnp.bfloat16)
    return high, (x - high.astype(jnp.float32)).astype(jnp.bfloat16)


def dot3(a_high, a_low, b_high, b_low):
    dot = functools.partial(jnp.dot, preferred_element_type=jnp.float32)
    return dot(a_high, b_high) + (dot(a_low, b_high) + dot(a_high, b_low))


def assemble(place_ref, count_ref, blocks_ref, basis_ref, high_ref, low_ref, turned_high_ref, turned_low_ref, slots, dense):
    @pl.loop(0, CAP // 8)
    def _(group):
        eight = blocks_ref[pl.ds(pl.multiple_of(group * 8, 8), 8), :]
        for t in range(HALF):
            slots[pl.ds(group * (8 * HALF) + t, 8, stride=HALF), :] = eight[:, t * 128:(t + 1) * 128]

    dense[...] = jnp.zeros_like(dense)

    @pl.loop(0, count_ref[0])
    def _(s):
        target = pl.ds(pl.multiple_of(place_ref[s] * HALF, HALF), HALF)
        dense[target, :] += slots[pl.ds(pl.multiple_of(s * HALF, HALF), HALF), :]

    left = lax.broadcasted_iota(jnp.int32, (HALF, 128), 1) < B

    @pl.loop(0, LINKS)
    def _(link):
        for r in range(BR_DEV):
            for pair in range(BR_DEV // 2):
                start = ((link * BR_DEV + r) * BR_DEV + 2 * pair) * HALF
                first = dense[pl.ds(pl.multiple_of(start, HALF), HALF), :]
                second = dense[pl.ds(pl.multiple_of(start + HALF, HALF), HALF), :]
                even = jnp.where(left, first, pltpu.roll(second, B, 1))
                odd = jnp.where(left, pltpu.roll(first, B, 1), second)
                for h, part in enumerate((even, odd)):
                    high, low = split(part)
                    rows = slice(r * B + h * HALF, r * B + (h + 1) * HALF)
                    high_ref[link, rows, pair * 128:(pair + 1) * 128] = high
                    low_ref[link, rows, pair * 128:(pair + 1) * 128] = low

    high, low = split(basis_ref[...].T)
    turned_high_ref[...] = high
    turned_low_ref[...] = low


def project_early(high_ref, low_ref, springs_ref, own_ref, *refs):
    basis_refs, total_ref = refs[:-1], refs[-1]
    total = jnp.zeros((ROWS, MODES), jnp.float32)
    for link, ref in enumerate((own_ref,) + basis_refs):
        b_high, b_low = split(ref[...])
        total += dot3(high_ref[link], low_ref[link], b_high, b_low)
    for r in range(BR_DEV):
        for h in range(2):
            rows = pl.ds(r * B + h, HALF, stride=2)
            start = r * B + h * HALF
            total_ref[rows, :] = springs_ref[rows, :] * own_ref[rows, :] + total[start:start + HALF, :]


def project_late(scale, high_ref, low_ref, turned_high_ref, turned_low_ref, total_ref, *refs):
    basis_refs, (stiff_ref, partial_ref) = refs[:LATE], refs[LATE:]
    total = jnp.zeros((ROWS, MODES), jnp.float32)
    for k, ref in enumerate(basis_refs):
        b_high, b_low = split(ref[...])
        total += dot3(high_ref[LINKS - LATE + k], low_ref[LINKS - LATE + k], b_high, b_low)
    for r in range(BR_DEV):
        for h in range(2):
            rows = pl.ds(r * B + h, HALF, stride=2)
            start = r * B + h * HALF
            stiff_ref[rows, :] = total_ref[rows, :] + total[start:start + HALF, :]
    s_high, s_low = split(stiff_ref[...])
    partial_ref[...] = dot3(turned_high_ref[...], turned_low_ref[...], s_high, s_low) * scale


def shards(basis, springs, tangent_blocks, tile_rows, tile_owner, tile_offset, tile_count):
    n = lax.axis_size("row")
    me = lax.axis_index("row")
    steps = (0, 1, n - 1, 4, n - 4, n // 2, 5, n - 5)

    def fetch(block, step):
        return lax.ppermute(block, "row", [((d + step) % n, d) for d in range(n)])

    above, below = fetch(basis, 4), fetch(basis, n - 4)
    across = fetch(basis, n // 2)
    after, before = fetch(basis, 1), fetch(basis, n - 1)
    far_above, far_below = fetch(above, 1), fetch(below, n - 1)

    away = (tile_owner[:, 0] - me + n) % n
    link = jnp.zeros_like(away)
    for k, step in enumerate(steps):
        link = jnp.where(away == step, k, link)
    place = (link * BR_DEV + tile_rows) * BR_DEV + tile_offset

    smem = pl.BlockSpec(memory_space=pltpu.SMEM)
    vmem = pl.BlockSpec(memory_space=pltpu.VMEM)
    half = jnp.bfloat16
    high, low, turned_high, turned_low = pl.pallas_call(
        assemble,
        out_shape=(
            jax.ShapeDtypeStruct((LINKS, ROWS, ROWS), half),
            jax.ShapeDtypeStruct((LINKS, ROWS, ROWS), half),
            jax.ShapeDtypeStruct((MODES, ROWS), half),
            jax.ShapeDtypeStruct((MODES, ROWS), half),
        ),
        in_specs=[smem, smem, vmem, vmem],
        out_specs=(vmem,) * 4,
        scratch_shapes=[pltpu.VMEM((CAP * HALF, 128), jnp.float32), pltpu.VMEM((CAP * HALF, 128), jnp.float32)],
        compiler_params=pltpu.CompilerParams(vmem_limit_bytes=32 * 2**20),
        cost_estimate=pl.CostEstimate(flops=10_000_000, bytes_accessed=12_000_000, transcendentals=0),
        name="assemble",
    )(place, tile_count, tangent_blocks, basis)

    total = pl.pallas_call(
        project_early,
        out_shape=jax.ShapeDtypeStruct((ROWS, MODES), jnp.float32),
        in_specs=[vmem] * (3 + LINKS - LATE),
        out_specs=vmem,
        compiler_params=pltpu.CompilerParams(vmem_limit_bytes=32 * 2**20),
        cost_estimate=pl.CostEstimate(flops=4 * 67_000_000, bytes_accessed=2_500_000, transcendentals=0),
        name="project_early",
    )(high, low, springs[:, None], basis, after, before, above, below)
    stiff_image, partial = pl.pallas_call(
        functools.partial(project_late, 1.0 / (basis.shape[0] * n)),
        out_shape=(
            jax.ShapeDtypeStruct((ROWS, MODES), jnp.float32),
            jax.ShapeDtypeStruct((MODES, MODES), jnp.float32),
        ),
        in_specs=[vmem] * (5 + LATE),
        out_specs=(vmem,) * 2,
        compiler_params=pltpu.CompilerParams(vmem_limit_bytes=32 * 2**20),
        cost_estimate=pl.CostEstimate(flops=2 * 67_000_000, bytes_accessed=1_500_000, transcendentals=0),
        name="project_late",
    )(high, low, turned_high, turned_low, total, across, far_above, far_below)

    reduced = partial
    apart = 1
    while apart < n:
        reduced += lax.ppermute(reduced, "row", [(d, d ^ apart) for d in range(n)])
        apart *= 2
    return (stiff_image, reduced)


def solution(mesh):
    in_specs = (
        P(("groups", "row"), None),
        P(("groups", "row")),
        P(("groups", "row"), None),
        P(("groups", "row")),
        P(("groups", "row"), None),
        P(("groups", "row")),
        P(("groups", "row")),
    )
    out_specs = (P(("groups", "row"), None), P("groups", None))
    return jax.shard_map(shards, mesh=mesh, in_specs=in_specs, out_specs=out_specs, check_vma=False)
```

```python
import functools

import jax
import jax.numpy as jnp
from jax import lax
from jax.experimental import pallas as pl
from jax.experimental.pallas import tpu as pltpu
from jax.sharding import PartitionSpec as P

B = 64
MODES = 128
BR_DEV = 4
CAP = 128
LINKS = 8
LATE = 3
HALF = B // 2
ROWS = BR_DEV * B


def split(x):
    high = x.astype(jnp.bfloat16)
    return high, (x - high.astype(jnp.float32)).astype(jnp.bfloat16)


def dot3(a_high, a_low, b_high, b_low):
    dot = functools.partial(jnp.dot, preferred_element_type=jnp.float32)
    return dot(a_high, b_high) + (dot(a_low, b_high) + dot(a_high, b_low))


def halves():
    for r in range(BR_DEV):
        for h in range(2):
            yield pl.ds(r * B + h, HALF, stride=2), slice(r * B + h * HALF, r * B + (h + 1) * HALF)


def assemble(place_ref, count_ref, blocks_ref, basis_ref, high_ref, low_ref, turned_high_ref, turned_low_ref, weight_high_ref, weight_low_ref, slots, dense, sorted_basis):
    dense[...] = jnp.zeros_like(dense)
    for rows, target in halves():
        sorted_basis[target, :] = basis_ref[rows, :]
    turned_high, turned_low = split(sorted_basis[...].T)
    turned_high_ref[...] = turned_high
    turned_low_ref[...] = turned_low

    @pl.loop(0, CAP // 8)
    def _(group):
        eight = blocks_ref[pl.ds(pl.multiple_of(group * 8, 8), 8), :]
        for t in range(HALF):
            slots[pl.ds(group * (8 * HALF) + t, 8, stride=HALF), :] = eight[:, t * 128:(t + 1) * 128]

    @pl.loop(0, count_ref[0])
    def _(s):
        target = pl.ds(pl.multiple_of(place_ref[s] * HALF, HALF), HALF)
        dense[target, :] += slots[pl.ds(pl.multiple_of(s * HALF, HALF), HALF), :]

    left = lax.broadcasted_iota(jnp.int32, (HALF, 128), 1) < B

    @pl.loop(0, LINKS)
    def _(link):
        for r in range(BR_DEV):
            for pair in range(BR_DEV // 2):
                start = ((link * BR_DEV + r) * BR_DEV + 2 * pair) * HALF
                first = dense[pl.ds(pl.multiple_of(start, HALF), HALF), :]
                second = dense[pl.ds(pl.multiple_of(start + HALF, HALF), HALF), :]
                even = jnp.where(left, first, pltpu.roll(second, B, 1))
                odd = jnp.where(left, pltpu.roll(first, B, 1), second)
                for h, part in enumerate((even, odd)):
                    high, low = split(part)
                    rows = slice(r * B + h * HALF, r * B + (h + 1) * HALF)
                    high_ref[link, rows, pair * 128:(pair + 1) * 128] = high
                    low_ref[link, rows, pair * 128:(pair + 1) * 128] = low

    for k in range(LATE):
        link = LINKS - LATE + k
        high, low = split(dot3(turned_high, turned_low, high_ref[link], low_ref[link]))
        weight_high_ref[k] = high
        weight_low_ref[k] = low


def project_early(high_ref, low_ref, turned_high_ref, turned_low_ref, springs_ref, own_ref, *refs):
    basis_refs, (total_ref, partial_ref) = refs[:-2], refs[-2:]
    total = jnp.zeros((ROWS, MODES), jnp.float32)
    for link, ref in enumerate((own_ref,) + basis_refs):
        b_high, b_low = split(ref[...])
        total += dot3(high_ref[link], low_ref[link], b_high, b_low)
    for part in range(ROWS // MODES):
        rows = slice(part * MODES, (part + 1) * MODES)
        column = jnp.broadcast_to(springs_ref[:, rows], (MODES, MODES)).T
        total_ref[rows, :] = column * own_ref[rows, :]
    for rows, target in halves():
        total_ref[rows, :] += total[target, :]
    sorted_total = jnp.concatenate([total_ref[rows, :] for rows, _ in halves()], axis=0)
    partial_ref[...] = dot3(turned_high_ref[...], turned_low_ref[...], *split(sorted_total))


def reduce_late(scale, weight_high_ref, weight_low_ref, early_ref, *refs):
    basis_refs, partial_ref = refs[:LATE], refs[LATE]
    total = early_ref[...]
    for k, ref in enumerate(basis_refs):
        total += dot3(weight_high_ref[k], weight_low_ref[k], *split(ref[...]))
    partial_ref[...] = total * scale


def project_late(high_ref, low_ref, total_ref, *refs):
    basis_refs, stiff_ref = refs[:LATE], refs[LATE]
    total = jnp.zeros((ROWS, MODES), jnp.float32)
    for k, ref in enumerate(basis_refs):
        b_high, b_low = split(ref[...])
        total += dot3(high_ref[LINKS - LATE + k], low_ref[LINKS - LATE + k], b_high, b_low)
    for rows, target in halves():
        stiff_ref[rows, :] = total_ref[rows, :] + total[target, :]


def shards(basis, springs, tangent_blocks, tile_rows, tile_owner, tile_offset, tile_count):
    n = lax.axis_size("row")
    me = lax.axis_index("row")
    steps = (0, 1, n - 1, 4, n - 4, n // 2, 5, n - 5)

    def fetch(block, step):
        return lax.ppermute(block, "row", [((d + step) % n, d) for d in range(n)])

    above, below = fetch(basis, 4), fetch(basis, n - 4)
    across = fetch(basis, n // 2)
    after, before = fetch(basis, 1), fetch(basis, n - 1)
    far_above, far_below = fetch(above, 1), fetch(below, n - 1)

    away = (tile_owner[:, 0] - me + n) % n
    link = jnp.zeros_like(away)
    for k, step in enumerate(steps):
        link = jnp.where(away == step, k, link)
    place = (link * BR_DEV + tile_rows) * BR_DEV + tile_offset

    smem = pl.BlockSpec(memory_space=pltpu.SMEM)
    vmem = pl.BlockSpec(memory_space=pltpu.VMEM)
    half, full = jnp.bfloat16, jnp.float32
    params = pltpu.CompilerParams(vmem_limit_bytes=32 * 2**20)

    high, low, turned_high, turned_low, weight_high, weight_low = pl.pallas_call(
        assemble,
        out_shape=(
            jax.ShapeDtypeStruct((LINKS, ROWS, ROWS), half),
            jax.ShapeDtypeStruct((LINKS, ROWS, ROWS), half),
            jax.ShapeDtypeStruct((MODES, ROWS), half),
            jax.ShapeDtypeStruct((MODES, ROWS), half),
            jax.ShapeDtypeStruct((LATE, MODES, ROWS), half),
            jax.ShapeDtypeStruct((LATE, MODES, ROWS), half),
        ),
        in_specs=[smem, smem, vmem, vmem],
        out_specs=(vmem,) * 6,
        scratch_shapes=[
            pltpu.VMEM((CAP * HALF, 128), full),
            pltpu.VMEM((CAP * HALF, 128), full),
            pltpu.VMEM((ROWS, MODES), full),
        ],
        compiler_params=params,
        cost_estimate=pl.CostEstimate(flops=10_000_000, bytes_accessed=12_000_000, transcendentals=0),
        name="assemble",
    )(place, tile_count, tangent_blocks, basis)

    total, early = pl.pallas_call(
        project_early,
        out_shape=(jax.ShapeDtypeStruct((ROWS, MODES), full), jax.ShapeDtypeStruct((MODES, MODES), full)),
        in_specs=[vmem] * (5 + LINKS - LATE),
        out_specs=(vmem,) * 2,
        compiler_params=params,
        cost_estimate=pl.CostEstimate(flops=20_000_000_000, bytes_accessed=2_500_000, transcendentals=0),
        name="project_early",
    )(high, low, turned_high, turned_low, springs.reshape(1, ROWS), basis, after, before, above, below)

    partial = pl.pallas_call(
        functools.partial(reduce_late, 1.0 / (basis.shape[0] * n)),
        out_shape=jax.ShapeDtypeStruct((MODES, MODES), full),
        in_specs=[vmem] * (3 + LATE),
        out_specs=vmem,
        compiler_params=params,
        cost_estimate=pl.CostEstimate(flops=80_000_000, bytes_accessed=700_000, transcendentals=0),
        name="reduce_late",
    )(weight_high, weight_low, early, across, far_above, far_below)

    stiff_image = pl.pallas_call(
        project_late,
        out_shape=jax.ShapeDtypeStruct((ROWS, MODES), full),
        in_specs=[vmem] * (3 + LATE),
        out_specs=vmem,
        compiler_params=params,
        cost_estimate=pl.CostEstimate(flops=160_000_000, bytes_accessed=1_500_000, transcendentals=0),
        name="project_late",
    )(high, low, total, across, far_above, far_below)

    reduced = partial
    apart = 1
    while apart < n:
        reduced += lax.ppermute(reduced, "row", [(d, d ^ apart) for d in range(n)])
        apart *= 2
    return (stiff_image, reduced)


def solution(mesh):
    in_specs = (
        P(("groups", "row"), None),
        P(("groups", "row")),
        P(("groups", "row"), None),
        P(("groups", "row")),
        P(("groups", "row"), None),
        P(("groups", "row")),
        P(("groups", "row")),
    )
    out_specs = (P(("groups", "row"), None), P("groups", None))
    return jax.shard_map(shards, mesh=mesh, in_specs=in_specs, out_specs=out_specs, check_vma=False)
```

```python
import functools

import jax
import jax.numpy as jnp
from jax import lax
from jax.experimental import pallas as pl
from jax.experimental.pallas import tpu as pltpu
from jax.sharding import PartitionSpec as P

B = 64
MODES = 128
BR_DEV = 4
CAP = 128
LINKS = 8
LATE = 3
HALF = B // 2
ROWS = BR_DEV * B


def split(x):
    high = x.astype(jnp.bfloat16)
    return high, (x - high.astype(jnp.float32)).astype(jnp.bfloat16)


def dot3(a_high, a_low, b_high, b_low):
    dot = functools.partial(jnp.dot, preferred_element_type=jnp.float32)
    return dot(a_high, b_high) + (dot(a_low, b_high) + dot(a_high, b_low))


def halves():
    for r in range(BR_DEV):
        for h in range(2):
            yield pl.ds(r * B + h, HALF, stride=2), slice(r * B + h * HALF, r * B + (h + 1) * HALF)


def assemble(place_ref, count_ref, blocks_ref, basis_ref, high_ref, low_ref, turned_high_ref, turned_low_ref, weight_high_ref, weight_low_ref, slots, dense, sorted_basis):
    dense[...] = jnp.zeros_like(dense)
    for rows, target in halves():
        sorted_basis[target, :] = basis_ref[rows, :]
    turned_high, turned_low = split(sorted_basis[...].T)
    turned_high_ref[...] = turned_high
    turned_low_ref[...] = turned_low

    @pl.loop(0, CAP // 8)
    def _(group):
        eight = blocks_ref[pl.ds(pl.multiple_of(group * 8, 8), 8), :]
        for t in range(HALF):
            slots[pl.ds(group * (8 * HALF) + t, 8, stride=HALF), :] = eight[:, t * 128:(t + 1) * 128]

    @pl.loop(0, count_ref[0])
    def _(s):
        target = pl.ds(pl.multiple_of(place_ref[s] * HALF, HALF), HALF)
        dense[target, :] += slots[pl.ds(pl.multiple_of(s * HALF, HALF), HALF), :]

    left = lax.broadcasted_iota(jnp.int32, (HALF, 128), 1) < B

    @pl.loop(0, LINKS)
    def _(link):
        for r in range(BR_DEV):
            for pair in range(BR_DEV // 2):
                start = ((link * BR_DEV + r) * BR_DEV + 2 * pair) * HALF
                first = dense[pl.ds(pl.multiple_of(start, HALF), HALF), :]
                second = dense[pl.ds(pl.multiple_of(start + HALF, HALF), HALF), :]
                even = jnp.where(left, first, pltpu.roll(second, B, 1))
                odd = jnp.where(left, pltpu.roll(first, B, 1), second)
                for h, part in enumerate((even, odd)):
                    high, low = split(part)
                    rows = slice(r * B + h * HALF, r * B + (h + 1) * HALF)
                    high_ref[link, rows, pair * 128:(pair + 1) * 128] = high
                    low_ref[link, rows, pair * 128:(pair + 1) * 128] = low

    for k in range(LATE):
        link = LINKS - LATE + k
        high, low = split(dot3(turned_high, turned_low, high_ref[link], low_ref[link]))
        weight_high_ref[k] = high
        weight_low_ref[k] = low


def project_early(high_ref, low_ref, turned_high_ref, turned_low_ref, springs_ref, own_ref, *refs):
    basis_refs, (total_ref, partial_ref) = refs[:-2], refs[-2:]
    total = jnp.zeros((ROWS, MODES), jnp.float32)
    for link, ref in enumerate((own_ref,) + basis_refs):
        b_high, b_low = split(ref[...])
        total += dot3(high_ref[link], low_ref[link], b_high, b_low)
    for part in range(ROWS // MODES):
        rows = slice(part * MODES, (part + 1) * MODES)
        column = jnp.broadcast_to(springs_ref[:, rows], (MODES, MODES)).T
        total_ref[rows, :] = column * own_ref[rows, :]
    for rows, target in halves():
        total_ref[rows, :] += total[target, :]
    sorted_total = jnp.concatenate([total_ref[rows, :] for rows, _ in halves()], axis=0)
    partial_ref[...] = dot3(turned_high_ref[...], turned_low_ref[...], *split(sorted_total))


def reduce_late(scale, core_ref, weight_high_ref, weight_low_ref, early_ref, *refs):
    basis_refs, (kept_ref, sent_ref, partial) = refs[:LATE], refs[LATE:]
    total = early_ref[...]
    for k, ref in enumerate(basis_refs):
        total += dot3(weight_high_ref[k], weight_low_ref[k], *split(ref[...]))
    partial[...] = total * scale
    half = MODES // 2
    kept_ref[...] = partial[pl.ds(pl.multiple_of(core_ref[0] * half, half), half), :]
    sent_ref[...] = partial[pl.ds(pl.multiple_of((1 - core_ref[0]) * half, half), half), :]


def join(core_ref, mine_ref, other_ref, whole_ref):
    half = MODES // 2
    whole_ref[pl.ds(pl.multiple_of(core_ref[0] * half, half), half), :] = mine_ref[...]
    whole_ref[pl.ds(pl.multiple_of((1 - core_ref[0]) * half, half), half), :] = other_ref[...]


def project_late(high_ref, low_ref, total_ref, *refs):
    basis_refs, stiff_ref = refs[:LATE], refs[LATE]
    total = jnp.zeros((ROWS, MODES), jnp.float32)
    for k, ref in enumerate(basis_refs):
        b_high, b_low = split(ref[...])
        total += dot3(high_ref[LINKS - LATE + k], low_ref[LINKS - LATE + k], b_high, b_low)
    for rows, target in halves():
        stiff_ref[rows, :] = total_ref[rows, :] + total[target, :]


def shards(basis, springs, tangent_blocks, tile_rows, tile_owner, tile_offset, tile_count):
    n = lax.axis_size("row")
    me = lax.axis_index("row")
    steps = (0, 1, n - 1, 4, n - 4, n // 2, 5, n - 5)

    def fetch(block, step):
        return lax.ppermute(block, "row", [((d + step) % n, d) for d in range(n)])

    above, below = fetch(basis, 4), fetch(basis, n - 4)
    across = fetch(basis, n // 2)
    after, before = fetch(basis, 1), fetch(basis, n - 1)
    far_above, far_below = fetch(above, 1), fetch(below, n - 1)

    away = (tile_owner[:, 0] - me + n) % n
    link = jnp.zeros_like(away)
    for k, step in enumerate(steps):
        link = jnp.where(away == step, k, link)
    place = (link * BR_DEV + tile_rows) * BR_DEV + tile_offset

    smem = pl.BlockSpec(memory_space=pltpu.SMEM)
    vmem = pl.BlockSpec(memory_space=pltpu.VMEM)
    half, full = jnp.bfloat16, jnp.float32
    params = pltpu.CompilerParams(vmem_limit_bytes=32 * 2**20)

    high, low, turned_high, turned_low, weight_high, weight_low = pl.pallas_call(
        assemble,
        out_shape=(
            jax.ShapeDtypeStruct((LINKS, ROWS, ROWS), half),
            jax.ShapeDtypeStruct((LINKS, ROWS, ROWS), half),
            jax.ShapeDtypeStruct((MODES, ROWS), half),
            jax.ShapeDtypeStruct((MODES, ROWS), half),
            jax.ShapeDtypeStruct((LATE, MODES, ROWS), half),
            jax.ShapeDtypeStruct((LATE, MODES, ROWS), half),
        ),
        in_specs=[smem, smem, vmem, vmem],
        out_specs=(vmem,) * 6,
        scratch_shapes=[
            pltpu.VMEM((CAP * HALF, 128), full),
            pltpu.VMEM((CAP * HALF, 128), full),
            pltpu.VMEM((ROWS, MODES), full),
        ],
        compiler_params=params,
        cost_estimate=pl.CostEstimate(flops=10_000_000, bytes_accessed=12_000_000, transcendentals=0),
        name="assemble",
    )(place, tile_count, tangent_blocks, basis)

    total, early = pl.pallas_call(
        project_early,
        out_shape=(jax.ShapeDtypeStruct((ROWS, MODES), full), jax.ShapeDtypeStruct((MODES, MODES), full)),
        in_specs=[vmem] * (5 + LINKS - LATE),
        out_specs=(vmem,) * 2,
        compiler_params=params,
        cost_estimate=pl.CostEstimate(flops=300_000_000, bytes_accessed=2_500_000, transcendentals=0),
        name="project_early",
    )(high, low, turned_high, turned_low, springs.reshape(1, ROWS), basis, after, before, above, below)

    core = (me % 2).reshape(1)
    piece = jax.ShapeDtypeStruct((MODES // 2, MODES), full)
    kept, sent = pl.pallas_call(
        functools.partial(reduce_late, 1.0 / (basis.shape[0] * n)),
        out_shape=(piece, piece),
        in_specs=[smem] + [vmem] * (3 + LATE),
        out_specs=(vmem,) * 2,
        scratch_shapes=[pltpu.VMEM((MODES, MODES), full)],
        compiler_params=params,
        cost_estimate=pl.CostEstimate(flops=80_000_000, bytes_accessed=700_000, transcendentals=0),
        name="reduce_late",
    )(core, weight_high, weight_low, early, across, far_above, far_below)

    stiff_image = pl.pallas_call(
        project_late,
        out_shape=jax.ShapeDtypeStruct((ROWS, MODES), full),
        in_specs=[vmem] * (3 + LATE),
        out_specs=vmem,
        compiler_params=params,
        cost_estimate=pl.CostEstimate(flops=160_000_000, bytes_accessed=1_500_000, transcendentals=0),
        name="project_late",
    )(high, low, total, across, far_above, far_below)

    def swap(block, apart):
        return lax.ppermute(block, "row", [(d, d ^ apart) for d in range(n)])

    mine = kept + swap(sent, 1)
    apart = 2
    while apart < n:
        mine += swap(mine, apart)
        apart *= 2
    reduced = pl.pallas_call(
        join,
        out_shape=jax.ShapeDtypeStruct((MODES, MODES), full),
        in_specs=[smem, vmem, vmem],
        out_specs=vmem,
        compiler_params=params,
        cost_estimate=pl.CostEstimate(flops=0, bytes_accessed=130_000, transcendentals=0),
        name="join",
    )(core, mine, swap(mine, 1))
    return (stiff_image, reduced)


def solution(mesh):
    in_specs = (
        P(("groups", "row"), None),
        P(("groups", "row")),
        P(("groups", "row"), None),
        P(("groups", "row")),
        P(("groups", "row"), None),
        P(("groups", "row")),
        P(("groups", "row")),
    )
    out_specs = (P(("groups", "row"), None), P("groups", None))
    return jax.shard_map(shards, mesh=mesh, in_specs=in_specs, out_specs=out_specs, check_vma=False)
```

```python
import functools

import jax
import jax.numpy as jnp
from jax import lax
from jax.experimental import pallas as pl
from jax.experimental.pallas import tpu as pltpu
from jax.sharding import PartitionSpec as P

B = 64
MODES = 128
BR_DEV = 4
CAP = 128
LINKS = 8
LATE = 3
HALF = B // 2
ROWS = BR_DEV * B


def split(x):
    high = x.astype(jnp.bfloat16)
    return high, (x - high.astype(jnp.float32)).astype(jnp.bfloat16)


def dot3(a_high, a_low, b_high, b_low):
    dot = functools.partial(jnp.dot, preferred_element_type=jnp.float32)
    return dot(a_high, b_high) + (dot(a_low, b_high) + dot(a_high, b_low))


def halves():
    for r in range(BR_DEV):
        for h in range(2):
            yield pl.ds(r * B + h, HALF, stride=2), slice(r * B + h * HALF, r * B + (h + 1) * HALF)


def assemble(place_ref, count_ref, blocks_ref, basis_ref, high_ref, low_ref, turned_high_ref, turned_low_ref, weight_high_ref, weight_low_ref, slots, dense, sorted_basis):
    dense[...] = jnp.zeros_like(dense)
    for rows, target in halves():
        sorted_basis[target, :] = basis_ref[rows, :]
    turned_high, turned_low = split(sorted_basis[...].T)
    turned_high_ref[...] = turned_high
    turned_low_ref[...] = turned_low

    @pl.loop(0, CAP // 8)
    def _(group):
        eight = blocks_ref[pl.ds(pl.multiple_of(group * 8, 8), 8), :]
        for t in range(HALF):
            slots[pl.ds(group * (8 * HALF) + t, 8, stride=HALF), :] = eight[:, t * 128:(t + 1) * 128]

    @pl.loop(0, count_ref[0])
    def _(s):
        target = pl.ds(pl.multiple_of(place_ref[s] * HALF, HALF), HALF)
        dense[target, :] += slots[pl.ds(pl.multiple_of(s * HALF, HALF), HALF), :]

    left = lax.broadcasted_iota(jnp.int32, (HALF, 128), 1) < B

    @pl.loop(0, LINKS)
    def _(link):
        for r in range(BR_DEV):
            for pair in range(BR_DEV // 2):
                start = ((link * BR_DEV + r) * BR_DEV + 2 * pair) * HALF
                first = dense[pl.ds(pl.multiple_of(start, HALF), HALF), :]
                second = dense[pl.ds(pl.multiple_of(start + HALF, HALF), HALF), :]
                even = jnp.where(left, first, pltpu.roll(second, B, 1))
                odd = jnp.where(left, pltpu.roll(first, B, 1), second)
                for h, part in enumerate((even, odd)):
                    high, low = split(part)
                    rows = slice(r * B + h * HALF, r * B + (h + 1) * HALF)
                    high_ref[link, rows, pair * 128:(pair + 1) * 128] = high
                    low_ref[link, rows, pair * 128:(pair + 1) * 128] = low

    for k in range(LATE):
        link = LINKS - LATE + k
        high, low = split(dot3(turned_high, turned_low, high_ref[link], low_ref[link]))
        weight_high_ref[k] = high
        weight_low_ref[k] = low


def project_early(high_ref, low_ref, turned_high_ref, turned_low_ref, springs_ref, own_ref, *refs):
    basis_refs, (total_ref, partial_ref) = refs[:-2], refs[-2:]
    total = jnp.zeros((ROWS, MODES), jnp.float32)
    for link, ref in enumerate((own_ref,) + basis_refs):
        b_high, b_low = split(ref[...])
        total += dot3(high_ref[link], low_ref[link], b_high, b_low)
    for part in range(ROWS // MODES):
        rows = slice(part * MODES, (part + 1) * MODES)
        column = jnp.broadcast_to(springs_ref[:, rows], (MODES, MODES)).T
        total_ref[rows, :] = column * own_ref[rows, :]
    for rows, target in halves():
        total_ref[rows, :] += total[target, :]
    sorted_total = jnp.concatenate([total_ref[rows, :] for rows, _ in halves()], axis=0)
    partial_ref[...] = dot3(turned_high_ref[...], turned_low_ref[...], *split(sorted_total))


def reduce_late(scale, weight_high_ref, weight_low_ref, early_ref, *refs):
    basis_refs, partial_ref = refs[:LATE], refs[LATE]
    total = early_ref[...]
    for k, ref in enumerate(basis_refs):
        total += dot3(weight_high_ref[k], weight_low_ref[k], *split(ref[...]))
    partial_ref[...] = total * scale


def add_after(first_ref, second_ref, done_ref, sum_ref):
    sum_ref[...] = first_ref[...] + second_ref[...]


def choose(core_ref, odd_ref, even_ref, whole_ref):
    @pl.when(core_ref[0] == 1)
    def _():
        whole_ref[...] = odd_ref[...]

    @pl.when(core_ref[0] == 0)
    def _():
        whole_ref[...] = even_ref[...]


def project_late(high_ref, low_ref, total_ref, *refs):
    basis_refs, (stiff_ref, done_ref) = refs[:LATE], refs[LATE:]
    total = jnp.zeros((ROWS, MODES), jnp.float32)
    for k, ref in enumerate(basis_refs):
        b_high, b_low = split(ref[...])
        total += dot3(high_ref[LINKS - LATE + k], low_ref[LINKS - LATE + k], b_high, b_low)
    for rows, target in halves():
        stiff_ref[rows, :] = total_ref[rows, :] + total[target, :]
    done_ref[...] = jnp.zeros_like(done_ref)


def shards(basis, springs, tangent_blocks, tile_rows, tile_owner, tile_offset, tile_count):
    n = lax.axis_size("row")
    me = lax.axis_index("row")
    steps = (0, 1, n - 1, 4, n - 4, n // 2, 5, n - 5)

    def fetch(block, step):
        return lax.ppermute(block, "row", [((d + step) % n, d) for d in range(n)])

    above, below = fetch(basis, 4), fetch(basis, n - 4)
    across = fetch(basis, n // 2)
    after, before = fetch(basis, 1), fetch(basis, n - 1)
    far_above, far_below = fetch(above, 1), fetch(below, n - 1)

    away = (tile_owner[:, 0] - me + n) % n
    link = jnp.zeros_like(away)
    for k, step in enumerate(steps):
        link = jnp.where(away == step, k, link)
    place = (link * BR_DEV + tile_rows) * BR_DEV + tile_offset

    smem = pl.BlockSpec(memory_space=pltpu.SMEM)
    vmem = pl.BlockSpec(memory_space=pltpu.VMEM)
    half, full = jnp.bfloat16, jnp.float32
    params = pltpu.CompilerParams(vmem_limit_bytes=32 * 2**20)

    high, low, turned_high, turned_low, weight_high, weight_low = pl.pallas_call(
        assemble,
        out_shape=(
            jax.ShapeDtypeStruct((LINKS, ROWS, ROWS), half),
            jax.ShapeDtypeStruct((LINKS, ROWS, ROWS), half),
            jax.ShapeDtypeStruct((MODES, ROWS), half),
            jax.ShapeDtypeStruct((MODES, ROWS), half),
            jax.ShapeDtypeStruct((LATE, MODES, ROWS), half),
            jax.ShapeDtypeStruct((LATE, MODES, ROWS), half),
        ),
        in_specs=[smem, smem, vmem, vmem],
        out_specs=(vmem,) * 6,
        scratch_shapes=[
            pltpu.VMEM((CAP * HALF, 128), full),
            pltpu.VMEM((CAP * HALF, 128), full),
            pltpu.VMEM((ROWS, MODES), full),
        ],
        compiler_params=params,
        cost_estimate=pl.CostEstimate(flops=10_000_000, bytes_accessed=12_000_000, transcendentals=0),
        name="assemble",
    )(place, tile_count, tangent_blocks, basis)

    total, early = pl.pallas_call(
        project_early,
        out_shape=(jax.ShapeDtypeStruct((ROWS, MODES), full), jax.ShapeDtypeStruct((MODES, MODES), full)),
        in_specs=[vmem] * (5 + LINKS - LATE),
        out_specs=(vmem,) * 2,
        compiler_params=params,
        cost_estimate=pl.CostEstimate(flops=300_000_000, bytes_accessed=2_500_000, transcendentals=0),
        name="project_early",
    )(high, low, turned_high, turned_low, springs.reshape(1, ROWS), basis, after, before, above, below)

    square = jax.ShapeDtypeStruct((MODES, MODES), full)
    partial = pl.pallas_call(
        functools.partial(reduce_late, 1.0 / (basis.shape[0] * n)),
        out_shape=square,
        in_specs=[vmem] * (3 + LATE),
        out_specs=vmem,
        compiler_params=params,
        cost_estimate=pl.CostEstimate(flops=80_000_000, bytes_accessed=700_000, transcendentals=0),
        name="reduce_late",
    )(weight_high, weight_low, early, across, far_above, far_below)

    stiff_image, done = pl.pallas_call(
        project_late,
        out_shape=(jax.ShapeDtypeStruct((ROWS, MODES), full), jax.ShapeDtypeStruct((8, 128), full)),
        in_specs=[vmem] * (3 + LATE),
        out_specs=(vmem,) * 2,
        compiler_params=params,
        cost_estimate=pl.CostEstimate(flops=160_000_000, bytes_accessed=1_500_000, transcendentals=0),
        name="project_late",
    )(high, low, total, across, far_above, far_below)

    def swap(block, apart):
        return lax.ppermute(block, "row", [(d, d ^ apart) for d in range(1, n, 2)])

    mine = partial + lax.ppermute(partial, "row", [(d, d + 1) for d in range(0, n, 2)])
    apart = 2
    if n.bit_length() % 2:
        mine = pl.pallas_call(
            add_after,
            out_shape=square,
            in_specs=[vmem] * 3,
            out_specs=vmem,
            compiler_params=params,
            name="add_after",
        )(mine, swap(mine, apart), done)
        apart *= 2
    while apart < n:
        pair = mine + swap(mine, apart)
        mine = pair + (swap(mine, 2 * apart) + swap(mine, 3 * apart))
        apart *= 4
    back = lax.ppermute(mine, "row", [(d, d - 1) for d in range(1, n, 2)])
    reduced = pl.pallas_call(
        choose,
        out_shape=square,
        in_specs=[smem, vmem, vmem],
        out_specs=vmem,
        compiler_params=params,
        cost_estimate=pl.CostEstimate(flops=0, bytes_accessed=130_000, transcendentals=0),
        name="choose",
    )((me % 2).reshape(1), mine, back)
    return (stiff_image, reduced)


def solution(mesh):
    in_specs = (
        P(("groups", "row"), None),
        P(("groups", "row")),
        P(("groups", "row"), None),
        P(("groups", "row")),
        P(("groups", "row"), None),
        P(("groups", "row")),
        P(("groups", "row")),
    )
    out_specs = (P(("groups", "row"), None), P("groups", None))
    return jax.shard_map(shards, mesh=mesh, in_specs=in_specs, out_specs=out_specs, check_vma=False)
```

```python
import functools

import jax
import jax.numpy as jnp
from jax import lax
from jax.experimental import pallas as pl
from jax.experimental.pallas import tpu as pltpu
from jax.sharding import PartitionSpec as P

B = 64
MODES = 128
BR_DEV = 4
CAP = 128
LINKS = 8
LATE = 3
HALF = B // 2
ROWS = BR_DEV * B


def split(x):
    high = x.astype(jnp.bfloat16)
    return high, (x - high.astype(jnp.float32)).astype(jnp.bfloat16)


def dot3(a_high, a_low, b_high, b_low):
    dot = functools.partial(jnp.dot, preferred_element_type=jnp.float32)
    return dot(a_high, b_high) + (dot(a_low, b_high) + dot(a_high, b_low))


def halves():
    for r in range(BR_DEV):
        for h in range(2):
            yield pl.ds(r * B + h, HALF, stride=2), slice(r * B + h * HALF, r * B + (h + 1) * HALF)


def assemble(place_ref, count_ref, blocks_ref, basis_ref, high_ref, low_ref, turned_high_ref, turned_low_ref, weight_high_ref, weight_low_ref, slots, dense, sorted_basis):
    dense[...] = jnp.zeros_like(dense)
    for rows, target in halves():
        sorted_basis[target, :] = basis_ref[rows, :]
    turned_high, turned_low = split(sorted_basis[...].T)
    turned_high_ref[...] = turned_high
    turned_low_ref[...] = turned_low

    @pl.loop(0, CAP // 8)
    def _(group):
        eight = blocks_ref[pl.ds(pl.multiple_of(group * 8, 8), 8), :]
        for t in range(HALF):
            slots[pl.ds(group * (8 * HALF) + t, 8, stride=HALF), :] = eight[:, t * 128:(t + 1) * 128]

    @pl.loop(0, count_ref[0])
    def _(s):
        target = pl.ds(pl.multiple_of(place_ref[s] * HALF, HALF), HALF)
        dense[target, :] += slots[pl.ds(pl.multiple_of(s * HALF, HALF), HALF), :]

    left = lax.broadcasted_iota(jnp.int32, (HALF, 128), 1) < B

    @pl.loop(0, LINKS)
    def _(link):
        for r in range(BR_DEV):
            for pair in range(BR_DEV // 2):
                start = ((link * BR_DEV + r) * BR_DEV + 2 * pair) * HALF
                first = dense[pl.ds(pl.multiple_of(start, HALF), HALF), :]
                second = dense[pl.ds(pl.multiple_of(start + HALF, HALF), HALF), :]
                even = jnp.where(left, first, pltpu.roll(second, B, 1))
                odd = jnp.where(left, pltpu.roll(first, B, 1), second)
                for h, part in enumerate((even, odd)):
                    high, low = split(part)
                    rows = slice(r * B + h * HALF, r * B + (h + 1) * HALF)
                    high_ref[link, rows, pair * 128:(pair + 1) * 128] = high
                    low_ref[link, rows, pair * 128:(pair + 1) * 128] = low

    for k in range(LATE):
        link = LINKS - LATE + k
        high, low = split(dot3(turned_high, turned_low, high_ref[link], low_ref[link]))
        weight_high_ref[k] = high
        weight_low_ref[k] = low


def project_early(high_ref, low_ref, turned_high_ref, turned_low_ref, springs_ref, own_ref, *refs):
    basis_refs, (total_ref, partial_ref) = refs[:-2], refs[-2:]
    total = jnp.zeros((ROWS, MODES), jnp.float32)
    for link, ref in enumerate((own_ref,) + basis_refs):
        b_high, b_low = split(ref[...])
        total += dot3(high_ref[link], low_ref[link], b_high, b_low)
    for part in range(ROWS // MODES):
        rows = slice(part * MODES, (part + 1) * MODES)
        column = jnp.broadcast_to(springs_ref[:, rows], (MODES, MODES)).T
        total_ref[rows, :] = column * own_ref[rows, :]
    for rows, target in halves():
        total_ref[rows, :] += total[target, :]
    sorted_total = jnp.concatenate([total_ref[rows, :] for rows, _ in halves()], axis=0)
    partial_ref[...] = dot3(turned_high_ref[...], turned_low_ref[...], *split(sorted_total))


def reduce_late(scale, weight_high_ref, weight_low_ref, early_ref, *refs):
    basis_refs, partial_ref = refs[:LATE], refs[LATE]
    total = early_ref[...]
    for k, ref in enumerate(basis_refs):
        total += dot3(weight_high_ref[k], weight_low_ref[k], *split(ref[...]))
    partial_ref[...] = total * scale


def add_after(first_ref, second_ref, done_ref, sum_ref):
    sum_ref[...] = first_ref[...] + second_ref[...]


def choose(core_ref, odd_ref, even_ref, whole_ref):
    @pl.when(core_ref[0] == 1)
    def _():
        whole_ref[...] = odd_ref[...]

    @pl.when(core_ref[0] == 0)
    def _():
        whole_ref[...] = even_ref[...]


def project_late(high_ref, low_ref, total_ref, *refs):
    basis_refs, (stiff_ref, done_ref) = refs[:LATE], refs[LATE:]
    total = jnp.zeros((ROWS, MODES), jnp.float32)
    for k, ref in enumerate(basis_refs):
        b_high, b_low = split(ref[...])
        total += dot3(high_ref[LINKS - LATE + k], low_ref[LINKS - LATE + k], b_high, b_low)
    for rows, target in halves():
        stiff_ref[rows, :] = total_ref[rows, :] + total[target, :]
    done_ref[...] = jnp.zeros_like(done_ref)


def shards(basis, springs, tangent_blocks, tile_rows, tile_owner, tile_offset, tile_count):
    n = lax.axis_size("row")
    me = lax.axis_index("row")
    steps = (0, 1, n - 1, 4, n - 4, n // 2, 5, n - 5)

    def fetch(block, step):
        return lax.ppermute(block, "row", [((d + step) % n, d) for d in range(n)])

    above, below = fetch(basis, 4), fetch(basis, n - 4)
    across = fetch(basis, n // 2)
    after, before = fetch(basis, 1), fetch(basis, n - 1)
    far_above, far_below = fetch(above, 1), fetch(below, n - 1)

    away = (tile_owner[:, 0] - me + n) % n
    link = jnp.zeros_like(away)
    for k, step in enumerate(steps):
        link = jnp.where(away == step, k, link)
    place = (link * BR_DEV + tile_rows) * BR_DEV + tile_offset

    smem = pl.BlockSpec(memory_space=pltpu.SMEM)
    vmem = pl.BlockSpec(memory_space=pltpu.VMEM)
    half, full = jnp.bfloat16, jnp.float32
    params = pltpu.CompilerParams(vmem_limit_bytes=32 * 2**20)

    high, low, turned_high, turned_low, weight_high, weight_low = pl.pallas_call(
        assemble,
        out_shape=(
            jax.ShapeDtypeStruct((LINKS, ROWS, ROWS), half),
            jax.ShapeDtypeStruct((LINKS, ROWS, ROWS), half),
            jax.ShapeDtypeStruct((MODES, ROWS), half),
            jax.ShapeDtypeStruct((MODES, ROWS), half),
            jax.ShapeDtypeStruct((LATE, MODES, ROWS), half),
            jax.ShapeDtypeStruct((LATE, MODES, ROWS), half),
        ),
        in_specs=[smem, smem, vmem, vmem],
        out_specs=(vmem,) * 6,
        scratch_shapes=[
            pltpu.VMEM((CAP * HALF, 128), full),
            pltpu.VMEM((CAP * HALF, 128), full),
            pltpu.VMEM((ROWS, MODES), full),
        ],
        compiler_params=params,
        cost_estimate=pl.CostEstimate(flops=10_000_000, bytes_accessed=12_000_000, transcendentals=0),
        name="assemble",
    )(place, tile_count, tangent_blocks, basis)

    total, early = pl.pallas_call(
        project_early,
        out_shape=(jax.ShapeDtypeStruct((ROWS, MODES), full), jax.ShapeDtypeStruct((MODES, MODES), full)),
        in_specs=[vmem] * (5 + LINKS - LATE),
        out_specs=(vmem,) * 2,
        compiler_params=params,
        cost_estimate=pl.CostEstimate(flops=300_000_000, bytes_accessed=2_500_000, transcendentals=0),
        name="project_early",
    )(high, low, turned_high, turned_low, springs.reshape(1, ROWS), basis, after, before, above, below)

    square = jax.ShapeDtypeStruct((MODES, MODES), full)
    partial = pl.pallas_call(
        functools.partial(reduce_late, 1.0 / (basis.shape[0] * n)),
        out_shape=square,
        in_specs=[vmem] * (3 + LATE),
        out_specs=vmem,
        compiler_params=params,
        cost_estimate=pl.CostEstimate(flops=80_000_000, bytes_accessed=700_000, transcendentals=0),
        name="reduce_late",
    )(weight_high, weight_low, early, across, far_above, far_below)

    stiff_image, done = pl.pallas_call(
        project_late,
        out_shape=(jax.ShapeDtypeStruct((ROWS, MODES), full), jax.ShapeDtypeStruct((8, 128), full)),
        in_specs=[vmem] * (3 + LATE),
        out_specs=(vmem,) * 2,
        compiler_params=params,
        cost_estimate=pl.CostEstimate(flops=160_000_000, bytes_accessed=1_500_000, transcendentals=0),
        name="project_late",
    )(high, low, total, across, far_above, far_below)

    def swap(block, apart):
        return lax.ppermute(block, "row", [(d, d ^ apart if apart == 1 or d % 2 else d) for d in range(n)])

    mine = partial + swap(partial, 1)
    mine = pl.pallas_call(
        add_after,
        out_shape=square,
        in_specs=[vmem] * 3,
        out_specs=vmem,
        compiler_params=params,
        name="add_after",
    )(mine, swap(mine, 2), done)
    apart = 4
    while apart < n:
        mine += swap(mine, apart)
        apart *= 2
    back = swap(mine, 1)
    reduced = pl.pallas_call(
        choose,
        out_shape=square,
        in_specs=[smem, vmem, vmem],
        out_specs=vmem,
        compiler_params=params,
        cost_estimate=pl.CostEstimate(flops=0, bytes_accessed=130_000, transcendentals=0),
        name="choose",
    )((me % 2).reshape(1), mine, back)
    return (stiff_image, reduced)


def solution(mesh):
    in_specs = (
        P(("groups", "row"), None),
        P(("groups", "row")),
        P(("groups", "row"), None),
        P(("groups", "row")),
        P(("groups", "row"), None),
        P(("groups", "row")),
        P(("groups", "row")),
    )
    out_specs = (P(("groups", "row"), None), P("groups", None))
    return jax.shard_map(shards, mesh=mesh, in_specs=in_specs, out_specs=out_specs, check_vma=False)
```

```python
import functools

import jax
import jax.numpy as jnp
from jax import lax
from jax.experimental import pallas as pl
from jax.experimental.pallas import tpu as pltpu
from jax.sharding import PartitionSpec as P

B = 64
MODES = 128
BR_DEV = 4
CAP = 128
LINKS = 8
LATE = 3
HALF = B // 2
ROWS = BR_DEV * B


def split(x):
    high = x.astype(jnp.bfloat16)
    return high, (x - high.astype(jnp.float32)).astype(jnp.bfloat16)


def dot3(a_high, a_low, b_high, b_low):
    dot = functools.partial(jnp.dot, preferred_element_type=jnp.float32)
    return dot(a_high, b_high) + (dot(a_low, b_high) + dot(a_high, b_low))


def halves():
    for r in range(BR_DEV):
        for h in range(2):
            yield pl.ds(r * B + h, HALF, stride=2), slice(r * B + h * HALF, r * B + (h + 1) * HALF)


def assemble(place_ref, count_ref, blocks_ref, basis_ref, high_ref, low_ref, turned_high_ref, turned_low_ref, weight_high_ref, weight_low_ref, slots, dense, sorted_basis):
    dense[...] = jnp.zeros_like(dense)
    for rows, target in halves():
        sorted_basis[target, :] = basis_ref[rows, :]
    turned_high, turned_low = split(sorted_basis[...].T)
    turned_high_ref[...] = turned_high
    turned_low_ref[...] = turned_low

    @pl.loop(0, CAP // 8)
    def _(group):
        eight = blocks_ref[pl.ds(pl.multiple_of(group * 8, 8), 8), :]
        for t in range(HALF):
            slots[pl.ds(group * (8 * HALF) + t, 8, stride=HALF), :] = eight[:, t * 128:(t + 1) * 128]

    @pl.loop(0, count_ref[0])
    def _(s):
        target = pl.ds(pl.multiple_of(place_ref[s] * HALF, HALF), HALF)
        dense[target, :] += slots[pl.ds(pl.multiple_of(s * HALF, HALF), HALF), :]

    left = lax.broadcasted_iota(jnp.int32, (HALF, 128), 1) < B

    @pl.loop(0, LINKS)
    def _(link):
        for r in range(BR_DEV):
            for pair in range(BR_DEV // 2):
                start = ((link * BR_DEV + r) * BR_DEV + 2 * pair) * HALF
                first = dense[pl.ds(pl.multiple_of(start, HALF), HALF), :]
                second = dense[pl.ds(pl.multiple_of(start + HALF, HALF), HALF), :]
                even = jnp.where(left, first, pltpu.roll(second, B, 1))
                odd = jnp.where(left, pltpu.roll(first, B, 1), second)
                for h, part in enumerate((even, odd)):
                    high, low = split(part)
                    rows = slice(r * B + h * HALF, r * B + (h + 1) * HALF)
                    high_ref[link, rows, pair * 128:(pair + 1) * 128] = high
                    low_ref[link, rows, pair * 128:(pair + 1) * 128] = low

    for k in range(LATE):
        link = LINKS - LATE + k
        high, low = split(dot3(turned_high, turned_low, high_ref[link], low_ref[link]))
        weight_high_ref[k] = high
        weight_low_ref[k] = low


def project_early(high_ref, low_ref, turned_high_ref, turned_low_ref, springs_ref, own_ref, *refs):
    basis_refs, (total_ref, partial_ref) = refs[:-2], refs[-2:]
    total = jnp.zeros((ROWS, MODES), jnp.float32)
    for link, ref in enumerate((own_ref,) + basis_refs):
        b_high, b_low = split(ref[...])
        total += dot3(high_ref[link], low_ref[link], b_high, b_low)
    for part in range(ROWS // MODES):
        rows = slice(part * MODES, (part + 1) * MODES)
        column = jnp.broadcast_to(springs_ref[:, rows], (MODES, MODES)).T
        total_ref[rows, :] = column * own_ref[rows, :]
    for rows, target in halves():
        total_ref[rows, :] += total[target, :]
    sorted_total = jnp.concatenate([total_ref[rows, :] for rows, _ in halves()], axis=0)
    partial_ref[...] = dot3(turned_high_ref[...], turned_low_ref[...], *split(sorted_total))


def reduce_late(scale, side_ref, weight_high_ref, weight_low_ref, early_ref, *refs):
    basis_refs, (kept_ref, sent_ref, partial) = refs[:LATE], refs[LATE:]
    total = early_ref[...]
    for k, ref in enumerate(basis_refs):
        total += dot3(weight_high_ref[k], weight_low_ref[k], *split(ref[...]))
    partial[...] = total * scale
    half = MODES // 2
    kept_ref[...] = partial[pl.ds(pl.multiple_of(side_ref[0] * half, half), half), :]
    sent_ref[...] = partial[pl.ds(pl.multiple_of((1 - side_ref[0]) * half, half), half), :]


def add_after(first_ref, second_ref, done_ref, sum_ref):
    sum_ref[...] = first_ref[...] + second_ref[...]


def join(side_ref, mine_ref, other_ref, whole_ref):
    half = MODES // 2
    whole_ref[pl.ds(pl.multiple_of(side_ref[0] * half, half), half), :] = mine_ref[...]
    whole_ref[pl.ds(pl.multiple_of((1 - side_ref[0]) * half, half), half), :] = other_ref[...]


def project_late(high_ref, low_ref, total_ref, *refs):
    basis_refs, (stiff_ref, done_ref) = refs[:LATE], refs[LATE:]
    total = jnp.zeros((ROWS, MODES), jnp.float32)
    for k, ref in enumerate(basis_refs):
        b_high, b_low = split(ref[...])
        total += dot3(high_ref[LINKS - LATE + k], low_ref[LINKS - LATE + k], b_high, b_low)
    for rows, target in halves():
        stiff_ref[rows, :] = total_ref[rows, :] + total[target, :]
    done_ref[...] = jnp.zeros_like(done_ref)


def shards(basis, springs, tangent_blocks, tile_rows, tile_owner, tile_offset, tile_count):
    n = lax.axis_size("row")
    me = lax.axis_index("row")
    steps = (0, 1, n - 1, 4, n - 4, n // 2, 5, n - 5)

    def fetch(block, step):
        return lax.ppermute(block, "row", [((d + step) % n, d) for d in range(n)])

    above, below = fetch(basis, 4), fetch(basis, n - 4)
    across = fetch(basis, n // 2)
    after, before = fetch(basis, 1), fetch(basis, n - 1)
    far_above, far_below = fetch(above, 1), fetch(below, n - 1)

    away = (tile_owner[:, 0] - me + n) % n
    link = jnp.zeros_like(away)
    for k, step in enumerate(steps):
        link = jnp.where(away == step, k, link)
    place = (link * BR_DEV + tile_rows) * BR_DEV + tile_offset

    smem = pl.BlockSpec(memory_space=pltpu.SMEM)
    vmem = pl.BlockSpec(memory_space=pltpu.VMEM)
    half, full = jnp.bfloat16, jnp.float32
    params = pltpu.CompilerParams(vmem_limit_bytes=32 * 2**20)

    high, low, turned_high, turned_low, weight_high, weight_low = pl.pallas_call(
        assemble,
        out_shape=(
            jax.ShapeDtypeStruct((LINKS, ROWS, ROWS), half),
            jax.ShapeDtypeStruct((LINKS, ROWS, ROWS), half),
            jax.ShapeDtypeStruct((MODES, ROWS), half),
            jax.ShapeDtypeStruct((MODES, ROWS), half),
            jax.ShapeDtypeStruct((LATE, MODES, ROWS), half),
            jax.ShapeDtypeStruct((LATE, MODES, ROWS), half),
        ),
        in_specs=[smem, smem, vmem, vmem],
        out_specs=(vmem,) * 6,
        scratch_shapes=[
            pltpu.VMEM((CAP * HALF, 128), full),
            pltpu.VMEM((CAP * HALF, 128), full),
            pltpu.VMEM((ROWS, MODES), full),
        ],
        compiler_params=params,
        cost_estimate=pl.CostEstimate(flops=10_000_000, bytes_accessed=12_000_000, transcendentals=0),
        name="assemble",
    )(place, tile_count, tangent_blocks, basis)

    total, early = pl.pallas_call(
        project_early,
        out_shape=(jax.ShapeDtypeStruct((ROWS, MODES), full), jax.ShapeDtypeStruct((MODES, MODES), full)),
        in_specs=[vmem] * (5 + LINKS - LATE),
        out_specs=(vmem,) * 2,
        compiler_params=params,
        cost_estimate=pl.CostEstimate(flops=300_000_000, bytes_accessed=2_500_000, transcendentals=0),
        name="project_early",
    )(high, low, turned_high, turned_low, springs.reshape(1, ROWS), basis, after, before, above, below)

    side = me
    for shift in (8, 4, 2, 1):
        side = side ^ (side >> shift)
    side = (side & 1).reshape(1)
    piece = jax.ShapeDtypeStruct((MODES // 2, MODES), full)
    kept, sent = pl.pallas_call(
        functools.partial(reduce_late, 1.0 / (basis.shape[0] * n)),
        out_shape=(piece, piece),
        in_specs=[smem] + [vmem] * (3 + LATE),
        out_specs=(vmem,) * 2,
        scratch_shapes=[pltpu.VMEM((MODES, MODES), full)],
        compiler_params=params,
        cost_estimate=pl.CostEstimate(flops=80_000_000, bytes_accessed=700_000, transcendentals=0),
        name="reduce_late",
    )(side, weight_high, weight_low, early, across, far_above, far_below)

    stiff_image, done = pl.pallas_call(
        project_late,
        out_shape=(jax.ShapeDtypeStruct((ROWS, MODES), full), jax.ShapeDtypeStruct((8, 128), full)),
        in_specs=[vmem] * (3 + LATE),
        out_specs=(vmem,) * 2,
        compiler_params=params,
        cost_estimate=pl.CostEstimate(flops=160_000_000, bytes_accessed=1_500_000, transcendentals=0),
        name="project_late",
    )(high, low, total, across, far_above, far_below)

    def swap(block, apart):
        return lax.ppermute(block, "row", [(d, d ^ apart) for d in range(n)])

    mine = kept + swap(sent, 1)
    mine = pl.pallas_call(
        add_after,
        out_shape=piece,
        in_specs=[vmem] * 3,
        out_specs=vmem,
        compiler_params=params,
        name="add_after",
    )(mine, swap(mine, 3), done)
    apart = 4
    while apart < n:
        mine += swap(mine, apart + 1)
        apart *= 2
    reduced = pl.pallas_call(
        join,
        out_shape=jax.ShapeDtypeStruct((MODES, MODES), full),
        in_specs=[smem, vmem, vmem],
        out_specs=vmem,
        compiler_params=params,
        cost_estimate=pl.CostEstimate(flops=0, bytes_accessed=130_000, transcendentals=0),
        name="join",
    )(side, mine, swap(mine, 1))
    return (stiff_image, reduced)


def solution(mesh):
    in_specs = (
        P(("groups", "row"), None),
        P(("groups", "row")),
        P(("groups", "row"), None),
        P(("groups", "row")),
        P(("groups", "row"), None),
        P(("groups", "row")),
        P(("groups", "row")),
    )
    out_specs = (P(("groups", "row"), None), P("groups", None))
    return jax.shard_map(shards, mesh=mesh, in_specs=in_specs, out_specs=out_specs, check_vma=False)
```

```python
import functools

import jax
import jax.numpy as jnp
from jax import lax
from jax.experimental import pallas as pl
from jax.experimental.pallas import tpu as pltpu
from jax.sharding import PartitionSpec as P

B = 64
MODES = 128
BR_DEV = 4
CAP = 128
LINKS = 8
LATE = 3
HALF = B // 2
ROWS = BR_DEV * B


def split(x):
    high = x.astype(jnp.bfloat16)
    return high, (x - high.astype(jnp.float32)).astype(jnp.bfloat16)


def dot3(a_high, a_low, b_high, b_low):
    dot = functools.partial(jnp.dot, preferred_element_type=jnp.float32)
    return dot(a_high, b_high) + (dot(a_low, b_high) + dot(a_high, b_low))


def halves():
    for r in range(BR_DEV):
        for h in range(2):
            yield pl.ds(r * B + h, HALF, stride=2), slice(r * B + h * HALF, r * B + (h + 1) * HALF)


def sum_slots(place_ref, blocks_ref, basis_ref, dense_ref, turned_high_ref, turned_low_ref, sorted_basis):
    dense_ref[...] = jnp.zeros_like(dense_ref)

    @pl.loop(0, CAP // 8)
    def _(group):
        for k in range(8):
            block = blocks_ref[pl.ds(group * (8 * HALF) + k, HALF, stride=8), :]
            target = pl.ds(pl.multiple_of(place_ref[group * 8 + k] * HALF, HALF), HALF)
            dense_ref[target, :] += block

    for rows, target in halves():
        sorted_basis[target, :] = basis_ref[rows, :]
    turned_high, turned_low = split(sorted_basis[...].T)
    turned_high_ref[...] = turned_high
    turned_low_ref[...] = turned_low


def pack(dense_ref, turned_high_ref, turned_low_ref, high_ref, low_ref, weight_high_ref, weight_low_ref):
    left = lax.broadcasted_iota(jnp.int32, (HALF, 128), 1) < B

    @pl.loop(0, LINKS)
    def _(link):
        for r in range(BR_DEV):
            for pair in range(BR_DEV // 2):
                start = ((link * BR_DEV + r) * BR_DEV + 2 * pair) * HALF
                first = dense_ref[pl.ds(pl.multiple_of(start, HALF), HALF), :]
                second = dense_ref[pl.ds(pl.multiple_of(start + HALF, HALF), HALF), :]
                even = jnp.where(left, first, pltpu.roll(second, B, 1))
                odd = jnp.where(left, pltpu.roll(first, B, 1), second)
                for h, part in enumerate((even, odd)):
                    high, low = split(part)
                    rows = slice(r * B + h * HALF, r * B + (h + 1) * HALF)
                    high_ref[link, rows, pair * 128:(pair + 1) * 128] = high
                    low_ref[link, rows, pair * 128:(pair + 1) * 128] = low

    for k in range(LATE):
        link = LINKS - LATE + k
        high, low = split(dot3(turned_high_ref[...], turned_low_ref[...], high_ref[link], low_ref[link]))
        weight_high_ref[k] = high
        weight_low_ref[k] = low


def project_early(high_ref, low_ref, turned_high_ref, turned_low_ref, springs_ref, *refs):
    basis_refs, (total_ref, partial_ref) = refs[:-2], refs[-2:]
    total = jnp.zeros((ROWS, MODES), jnp.float32)
    for link, ref in enumerate(basis_refs):
        b_high, b_low = split(ref[...])
        total += dot3(high_ref[link], low_ref[link], b_high, b_low)
    for part in range(ROWS // MODES):
        rows = slice(part * MODES, (part + 1) * MODES)
        column = jnp.broadcast_to(springs_ref[:, rows], (MODES, MODES)).T
        total_ref[rows, :] = column * basis_refs[0][rows, :]
    for rows, target in halves():
        total_ref[rows, :] += total[target, :]
    sorted_total = jnp.concatenate([total_ref[rows, :] for rows, _ in halves()], axis=0)
    partial_ref[...] = dot3(turned_high_ref[...], turned_low_ref[...], *split(sorted_total))


def reduce_late(scale, side_ref, weight_high_ref, weight_low_ref, early_ref, *refs):
    basis_refs, (kept_ref, sent_ref, partial) = refs[:LATE], refs[LATE:]
    total = early_ref[...]
    for k, ref in enumerate(basis_refs):
        total += dot3(weight_high_ref[k], weight_low_ref[k], *split(ref[...]))
    partial[...] = total * scale
    half = MODES // 2
    kept_ref[...] = partial[pl.ds(pl.multiple_of(side_ref[0] * half, half), half), :]
    sent_ref[...] = partial[pl.ds(pl.multiple_of((1 - side_ref[0]) * half, half), half), :]


def add_after(first_ref, second_ref, done_ref, sum_ref):
    sum_ref[...] = first_ref[...] + second_ref[...]


def join(side_ref, mine_ref, other_ref, whole_ref):
    half = MODES // 2
    whole_ref[pl.ds(pl.multiple_of(side_ref[0] * half, half), half), :] = mine_ref[...]
    whole_ref[pl.ds(pl.multiple_of((1 - side_ref[0]) * half, half), half), :] = other_ref[...]


def project_late(high_ref, low_ref, total_ref, *refs):
    basis_refs, (stiff_ref, done_ref) = refs[:LATE], refs[LATE:]
    total = jnp.zeros((ROWS, MODES), jnp.float32)
    for k, ref in enumerate(basis_refs):
        b_high, b_low = split(ref[...])
        total += dot3(high_ref[LINKS - LATE + k], low_ref[LINKS - LATE + k], b_high, b_low)
    for rows, target in halves():
        stiff_ref[rows, :] = total_ref[rows, :] + total[target, :]
    done_ref[...] = jnp.zeros_like(done_ref)


def shards(basis, springs, tangent_blocks, tile_rows, tile_owner, tile_offset, tile_count):
    n = lax.axis_size("row")
    me = lax.axis_index("row")
    steps = (0, 1, n - 1, 4, n - 4, n // 2, 5, n - 5)

    def fetch(block, step):
        return lax.ppermute(block, "row", [((d + step) % n, d) for d in range(n)])

    above, below = fetch(basis, 4), fetch(basis, n - 4)
    across = fetch(basis, n // 2)
    after, before = fetch(basis, 1), fetch(basis, n - 1)
    far_above, far_below = fetch(above, 1), fetch(below, n - 1)

    away = (tile_owner[:, 0] - me + n) % n
    link = jnp.zeros_like(away)
    for k, step in enumerate(steps):
        link = jnp.where(away == step, k, link)
    place = (link * BR_DEV + tile_rows) * BR_DEV + tile_offset
    place = jnp.where(jnp.arange(CAP, dtype=jnp.int32) < tile_count[0], place, CAP)
    blocks = tangent_blocks.reshape(CAP // 8, 8, HALF, 128).transpose(0, 2, 1, 3).reshape(CAP * HALF, 128)

    smem = pl.BlockSpec(memory_space=pltpu.SMEM)
    vmem = pl.BlockSpec(memory_space=pltpu.VMEM)
    half, full = jnp.bfloat16, jnp.float32
    params = pltpu.CompilerParams(vmem_limit_bytes=32 * 2**20)

    dense, turned_high, turned_low = pl.pallas_call(
        sum_slots,
        out_shape=(
            jax.ShapeDtypeStruct(((CAP + 1) * HALF, 128), full),
            jax.ShapeDtypeStruct((MODES, ROWS), half),
            jax.ShapeDtypeStruct((MODES, ROWS), half),
        ),
        in_specs=[smem] + [vmem] * 2,
        out_specs=(vmem,) * 3,
        scratch_shapes=[pltpu.VMEM((ROWS, MODES), full)],
        compiler_params=params,
        cost_estimate=pl.CostEstimate(flops=500_000, bytes_accessed=4_000_000, transcendentals=0),
        name="sum_slots",
    )(place, blocks, basis)

    high, low, weight_high, weight_low = pl.pallas_call(
        pack,
        out_shape=(
            jax.ShapeDtypeStruct((LINKS, ROWS, ROWS), half),
            jax.ShapeDtypeStruct((LINKS, ROWS, ROWS), half),
            jax.ShapeDtypeStruct((LATE, MODES, ROWS), half),
            jax.ShapeDtypeStruct((LATE, MODES, ROWS), half),
        ),
        in_specs=[vmem] * 3,
        out_specs=(vmem,) * 4,
        compiler_params=params,
        cost_estimate=pl.CostEstimate(flops=10_000_000_000, bytes_accessed=4_000_000, transcendentals=0),
        name="pack",
    )(dense, turned_high, turned_low)

    total, early = pl.pallas_call(
        project_early,
        out_shape=(jax.ShapeDtypeStruct((ROWS, MODES), full), jax.ShapeDtypeStruct((MODES, MODES), full)),
        in_specs=[vmem] * (5 + LINKS - LATE),
        out_specs=(vmem,) * 2,
        compiler_params=params,
        cost_estimate=pl.CostEstimate(flops=300_000_000, bytes_accessed=2_500_000, transcendentals=0),
        name="project_early",
    )(high, low, turned_high, turned_low, springs.reshape(1, ROWS), basis, after, before, above, below)

    side = me
    for shift in (8, 4, 2, 1):
        side = side ^ (side >> shift)
    side = (side & 1).reshape(1)
    piece = jax.ShapeDtypeStruct((MODES // 2, MODES), full)
    kept, sent = pl.pallas_call(
        functools.partial(reduce_late, 1.0 / (basis.shape[0] * n)),
        out_shape=(piece, piece),
        in_specs=[smem] + [vmem] * (3 + LATE),
        out_specs=(vmem,) * 2,
        scratch_shapes=[pltpu.VMEM((MODES, MODES), full)],
        compiler_params=params,
        cost_estimate=pl.CostEstimate(flops=80_000_000, bytes_accessed=700_000, transcendentals=0),
        name="reduce_late",
    )(side, weight_high, weight_low, early, across, far_above, far_below)

    stiff_image, done = pl.pallas_call(
        project_late,
        out_shape=(jax.ShapeDtypeStruct((ROWS, MODES), full), jax.ShapeDtypeStruct((8, 128), full)),
        in_specs=[vmem] * (3 + LATE),
        out_specs=(vmem,) * 2,
        compiler_params=params,
        cost_estimate=pl.CostEstimate(flops=160_000_000, bytes_accessed=1_500_000, transcendentals=0),
        name="project_late",
    )(high, low, total, across, far_above, far_below)

    def swap(block, apart):
        return lax.ppermute(block, "row", [(d, d ^ apart) for d in range(n)])

    mine = kept + swap(sent, 1)
    mine = pl.pallas_call(
        add_after,
        out_shape=piece,
        in_specs=[vmem] * 3,
        out_specs=vmem,
        compiler_params=params,
        name="add_after",
    )(mine, swap(mine, 3), done)
    apart = 4
    while apart < n:
        mine += swap(mine, apart + 1)
        apart *= 2
    reduced = pl.pallas_call(
        join,
        out_shape=jax.ShapeDtypeStruct((MODES, MODES), full),
        in_specs=[smem, vmem, vmem],
        out_specs=vmem,
        compiler_params=params,
        cost_estimate=pl.CostEstimate(flops=0, bytes_accessed=130_000, transcendentals=0),
        name="join",
    )(side, mine, swap(mine, 1))
    return (stiff_image, reduced)


def solution(mesh):
    in_specs = (
        P(("groups", "row"), None),
        P(("groups", "row")),
        P(("groups", "row"), None),
        P(("groups", "row")),
        P(("groups", "row"), None),
        P(("groups", "row")),
        P(("groups", "row")),
    )
    out_specs = (P(("groups", "row"), None), P("groups", None))
    return jax.shard_map(shards, mesh=mesh, in_specs=in_specs, out_specs=out_specs, check_vma=False)
```

```python
import functools

import jax
import jax.numpy as jnp
from jax import lax
from jax.experimental import pallas as pl
from jax.experimental.pallas import tpu as pltpu
from jax.sharding import PartitionSpec as P

B = 64
MODES = 128
BR_DEV = 4
CAP = 128
LINKS = 8
LATE = 3
HALF = B // 2
ROWS = BR_DEV * B


def split(x):
    high = x.astype(jnp.bfloat16)
    return high, (x - high.astype(jnp.float32)).astype(jnp.bfloat16)


def dot3(a_high, a_low, b_high, b_low):
    dot = functools.partial(jnp.dot, preferred_element_type=jnp.float32)
    return dot(a_high, b_high) + (dot(a_low, b_high) + dot(a_high, b_low))


def halves():
    for r in range(BR_DEV):
        for h in range(2):
            yield pl.ds(r * B + h, HALF, stride=2), slice(r * B + h * HALF, r * B + (h + 1) * HALF)


def prepare(basis_ref, held_ref):
    held_ref[...] = basis_ref[...]


def assemble(count_ref, rows_ref, owner_ref, offset_ref, blocks_ref, high_ref, low_ref, dense, placed, place, arrived):
    n = lax.axis_size("row")
    away = lax.rem(owner_ref[...].reshape(1, CAP) - lax.axis_index("row") + n, n)
    link = jnp.zeros_like(away)
    for k, step in enumerate(steps(n)):
        link = jnp.where(away == step, k, link)
    target = (link * BR_DEV + rows_ref[...].reshape(1, CAP)) * BR_DEV + offset_ref[...].reshape(1, CAP)
    slot = lax.broadcasted_iota(jnp.int32, (1, CAP), 1)
    placed[...] = jnp.where(slot < count_ref[0], target, CAP)
    copy = pltpu.make_async_copy(placed, place, arrived)
    copy.start()
    dense[...] = jnp.zeros_like(dense)
    copy.wait()

    @pl.loop(0, CAP // 8)
    def _(group):
        for k in range(8):
            block = blocks_ref[pl.ds(group * (8 * HALF) + k, HALF, stride=8), :]
            target = pl.ds(pl.multiple_of(place[0, group * 8 + k] * HALF, HALF), HALF)
            dense[target, :] += block

    left = lax.broadcasted_iota(jnp.int32, (HALF, 128), 1) < B

    @pl.loop(0, LINKS)
    def _(link):
        for r in range(BR_DEV):
            for pair in range(BR_DEV // 2):
                start = ((link * BR_DEV + r) * BR_DEV + 2 * pair) * HALF
                first = dense[pl.ds(pl.multiple_of(start, HALF), HALF), :]
                second = dense[pl.ds(pl.multiple_of(start + HALF, HALF), HALF), :]
                even = jnp.where(left, first, pltpu.roll(second, B, 1))
                odd = jnp.where(left, pltpu.roll(first, B, 1), second)
                for h, part in enumerate((even, odd)):
                    high, low = split(part)
                    rows = slice(r * B + h * HALF, r * B + (h + 1) * HALF)
                    high_ref[link, rows, pair * 128:(pair + 1) * 128] = high
                    low_ref[link, rows, pair * 128:(pair + 1) * 128] = low


def project_early(high_ref, low_ref, springs_ref, *refs):
    basis_refs, (total_ref, partial_ref, weight_high_ref, weight_low_ref, sorted_rows) = refs[:-5], refs[-5:]
    own_ref = basis_refs[0]
    for rows, target in halves():
        sorted_rows[target, :] = own_ref[rows, :]
    turned_high, turned_low = split(sorted_rows[...].T)
    for k in range(LATE):
        link = LINKS - LATE + k
        high, low = split(dot3(turned_high, turned_low, high_ref[link], low_ref[link]))
        weight_high_ref[k] = high
        weight_low_ref[k] = low
    total = jnp.zeros((ROWS, MODES), jnp.float32)
    for link, ref in enumerate(basis_refs):
        b_high, b_low = split(ref[...])
        total += dot3(high_ref[link], low_ref[link], b_high, b_low)
    for part in range(ROWS // MODES):
        rows = slice(part * MODES, (part + 1) * MODES)
        column = jnp.broadcast_to(springs_ref[:, rows], (MODES, MODES)).T
        total_ref[rows, :] = column * own_ref[rows, :]
    for rows, target in halves():
        total_ref[rows, :] += total[target, :]
        sorted_rows[target, :] = total_ref[rows, :]
    partial_ref[...] = dot3(turned_high, turned_low, *split(sorted_rows[...]))


def reduce_late(scale, side_ref, weight_high_ref, weight_low_ref, early_ref, *refs):
    basis_refs, (kept_ref, sent_ref, partial) = refs[:LATE], refs[LATE:]
    total = early_ref[...]
    for k, ref in enumerate(basis_refs):
        total += dot3(weight_high_ref[k], weight_low_ref[k], *split(ref[...]))
    partial[...] = total * scale
    half = MODES // 2
    kept_ref[...] = partial[pl.ds(pl.multiple_of(side_ref[0] * half, half), half), :]
    sent_ref[...] = partial[pl.ds(pl.multiple_of((1 - side_ref[0]) * half, half), half), :]


def add_after(first_ref, second_ref, done_ref, sum_ref):
    sum_ref[...] = first_ref[...] + second_ref[...]


def join(side_ref, mine_ref, other_ref, whole_ref):
    half = MODES // 2
    whole_ref[pl.ds(pl.multiple_of(side_ref[0] * half, half), half), :] = mine_ref[...]
    whole_ref[pl.ds(pl.multiple_of((1 - side_ref[0]) * half, half), half), :] = other_ref[...]


def project_late(high_ref, low_ref, total_ref, *refs):
    basis_refs, (stiff_ref, done_ref) = refs[:LATE], refs[LATE:]
    total = jnp.zeros((ROWS, MODES), jnp.float32)
    for k, ref in enumerate(basis_refs):
        b_high, b_low = split(ref[...])
        total += dot3(high_ref[LINKS - LATE + k], low_ref[LINKS - LATE + k], b_high, b_low)
    for rows, target in halves():
        stiff_ref[rows, :] = total_ref[rows, :] + total[target, :]
    done_ref[...] = jnp.zeros_like(done_ref)


def steps(n):
    return (0, 1, n - 1, 4, n - 4, n // 2, 5, n - 5)


def shards(basis, springs, tangent_blocks, tile_rows, tile_owner, tile_offset, tile_count):
    n = lax.axis_size("row")
    me = lax.axis_index("row")
    smem = pl.BlockSpec(memory_space=pltpu.SMEM)
    vmem = pl.BlockSpec(memory_space=pltpu.VMEM)
    half, full = jnp.bfloat16, jnp.float32
    params = pltpu.CompilerParams(vmem_limit_bytes=32 * 2**20)

    held = pl.pallas_call(
        prepare,
        out_shape=jax.ShapeDtypeStruct((ROWS, MODES), full),
        in_specs=[vmem],
        out_specs=vmem,
        compiler_params=params,
        cost_estimate=pl.CostEstimate(flops=10_000_000_000, bytes_accessed=300_000, transcendentals=0),
        name="prepare",
    )(basis)

    def fetch(block, step):
        return lax.ppermute(block, "row", [((d + step) % n, d) for d in range(n)])

    above, below = fetch(held, 4), fetch(held, n - 4)
    across = fetch(held, n // 2)
    after, before = fetch(held, 1), fetch(held, n - 1)
    far_above, far_below = fetch(above, 1), fetch(below, n - 1)

    blocks = tangent_blocks.reshape(CAP // 8, 8, HALF, 128).transpose(0, 2, 1, 3).reshape(CAP * HALF, 128)
    high, low = pl.pallas_call(
        assemble,
        out_shape=(
            jax.ShapeDtypeStruct((LINKS, ROWS, ROWS), half),
            jax.ShapeDtypeStruct((LINKS, ROWS, ROWS), half),
        ),
        in_specs=[smem] + [vmem] * 4,
        out_specs=(vmem,) * 2,
        scratch_shapes=[
            pltpu.VMEM(((CAP + 1) * HALF, 128), full),
            pltpu.VMEM((1, CAP), jnp.int32),
            pltpu.SMEM((1, CAP), jnp.int32),
            pltpu.SemaphoreType.DMA(()),
        ],
        compiler_params=params,
        cost_estimate=pl.CostEstimate(flops=10_000_000, bytes_accessed=8_000_000, transcendentals=0),
        name="assemble",
    )(tile_count, tile_rows, tile_owner[:, 0], tile_offset, blocks)

    total, early, weight_high, weight_low = pl.pallas_call(
        project_early,
        out_shape=(
            jax.ShapeDtypeStruct((ROWS, MODES), full),
            jax.ShapeDtypeStruct((MODES, MODES), full),
            jax.ShapeDtypeStruct((LATE, MODES, ROWS), half),
            jax.ShapeDtypeStruct((LATE, MODES, ROWS), half),
        ),
        in_specs=[vmem] * (3 + LINKS - LATE),
        out_specs=(vmem,) * 4,
        scratch_shapes=[pltpu.VMEM((ROWS, MODES), full)],
        compiler_params=params,
        cost_estimate=pl.CostEstimate(flops=300_000_000, bytes_accessed=2_500_000, transcendentals=0),
        name="project_early",
    )(high, low, springs.reshape(1, ROWS), held, after, before, above, below)

    side = me
    for shift in (8, 4, 2, 1):
        side = side ^ (side >> shift)
    side = (side & 1).reshape(1)
    piece = jax.ShapeDtypeStruct((MODES // 2, MODES), full)
    kept, sent = pl.pallas_call(
        functools.partial(reduce_late, 1.0 / (basis.shape[0] * n)),
        out_shape=(piece, piece),
        in_specs=[smem] + [vmem] * (3 + LATE),
        out_specs=(vmem,) * 2,
        scratch_shapes=[pltpu.VMEM((MODES, MODES), full)],
        compiler_params=params,
        cost_estimate=pl.CostEstimate(flops=80_000_000, bytes_accessed=700_000, transcendentals=0),
        name="reduce_late",
    )(side, weight_high, weight_low, early, across, far_above, far_below)

    stiff_image, done = pl.pallas_call(
        project_late,
        out_shape=(jax.ShapeDtypeStruct((ROWS, MODES), full), jax.ShapeDtypeStruct((8, 128), full)),
        in_specs=[vmem] * (3 + LATE),
        out_specs=(vmem,) * 2,
        compiler_params=params,
        cost_estimate=pl.CostEstimate(flops=160_000_000, bytes_accessed=1_500_000, transcendentals=0),
        name="project_late",
    )(high, low, total, across, far_above, far_below)

    def swap(block, apart):
        return lax.ppermute(block, "row", [(d, d ^ apart) for d in range(n)])

    mine = kept + swap(sent, 1)
    mine = pl.pallas_call(
        add_after,
        out_shape=piece,
        in_specs=[vmem] * 3,
        out_specs=vmem,
        compiler_params=params,
        name="add_after",
    )(mine, swap(mine, 3), done)
    apart = 4
    while apart < n:
        mine += swap(mine, apart + 1)
        apart *= 2
    reduced = pl.pallas_call(
        join,
        out_shape=jax.ShapeDtypeStruct((MODES, MODES), full),
        in_specs=[smem, vmem, vmem],
        out_specs=vmem,
        compiler_params=params,
        cost_estimate=pl.CostEstimate(flops=0, bytes_accessed=130_000, transcendentals=0),
        name="join",
    )(side, mine, swap(mine, 1))
    return (stiff_image, reduced)


def solution(mesh):
    in_specs = (
        P(("groups", "row"), None),
        P(("groups", "row")),
        P(("groups", "row"), None),
        P(("groups", "row")),
        P(("groups", "row"), None),
        P(("groups", "row")),
        P(("groups", "row")),
    )
    out_specs = (P(("groups", "row"), None), P("groups", None))
    return jax.shard_map(shards, mesh=mesh, in_specs=in_specs, out_specs=out_specs, check_vma=False)
```

```python
import functools

import jax
import jax.numpy as jnp
from jax import lax
from jax.experimental import pallas as pl
from jax.experimental.pallas import tpu as pltpu
from jax.sharding import PartitionSpec as P

B = 64
MODES = 128
BR_DEV = 4
CAP = 128
LINKS = 8
LATE = 3
HALF = B // 2
ROWS = BR_DEV * B


def split(x):
    high = x.astype(jnp.bfloat16)
    return high, (x - high.astype(jnp.float32)).astype(jnp.bfloat16)


def dot3(a_high, a_low, b_high, b_low):
    dot = functools.partial(jnp.dot, preferred_element_type=jnp.float32)
    return dot(a_high, b_high) + (dot(a_low, b_high) + dot(a_high, b_low))


def halves():
    for r in range(BR_DEV):
        for h in range(2):
            yield pl.ds(r * B + h, HALF, stride=2), slice(r * B + h * HALF, r * B + (h + 1) * HALF)


def prepare(basis_ref, held_ref):
    held_ref[...] = basis_ref[...]


def assemble(count_ref, rows_ref, owner_ref, offset_ref, blocks_ref, high_ref, low_ref, dense, placed, place, arrived):
    n, me = lax.axis_size("row"), lax.axis_index("row")
    away = lax.rem(owner_ref[...].reshape(1, CAP) - me + n, n)
    link = jnp.zeros_like(away)
    for k, step in enumerate(steps(n, me)):
        link = jnp.where(away == step, k, link)
    target = (link * BR_DEV + rows_ref[...].reshape(1, CAP)) * BR_DEV + offset_ref[...].reshape(1, CAP)
    slot = lax.broadcasted_iota(jnp.int32, (1, CAP), 1)
    placed[...] = jnp.where(slot < count_ref[0], target, CAP)
    copy = pltpu.make_async_copy(placed, place, arrived)
    copy.start()
    dense[...] = jnp.zeros_like(dense)
    copy.wait()

    @pl.loop(0, CAP // 8)
    def _(group):
        for k in range(8):
            block = blocks_ref[pl.ds(group * (8 * HALF) + k, HALF, stride=8), :]
            target = pl.ds(pl.multiple_of(place[0, group * 8 + k] * HALF, HALF), HALF)
            dense[target, :] += block

    left = lax.broadcasted_iota(jnp.int32, (HALF, 128), 1) < B

    @pl.loop(0, LINKS)
    def _(link):
        for r in range(BR_DEV):
            for pair in range(BR_DEV // 2):
                start = ((link * BR_DEV + r) * BR_DEV + 2 * pair) * HALF
                first = dense[pl.ds(pl.multiple_of(start, HALF), HALF), :]
                second = dense[pl.ds(pl.multiple_of(start + HALF, HALF), HALF), :]
                even = jnp.where(left, first, pltpu.roll(second, B, 1))
                odd = jnp.where(left, pltpu.roll(first, B, 1), second)
                for h, part in enumerate((even, odd)):
                    high, low = split(part)
                    rows = slice(r * B + h * HALF, r * B + (h + 1) * HALF)
                    high_ref[link, rows, pair * 128:(pair + 1) * 128] = high
                    low_ref[link, rows, pair * 128:(pair + 1) * 128] = low


def project_early(high_ref, low_ref, springs_ref, *refs):
    basis_refs, (total_ref, partial_ref, weight_high_ref, weight_low_ref, sorted_rows) = refs[:-5], refs[-5:]
    own_ref = basis_refs[0]
    for rows, target in halves():
        sorted_rows[target, :] = own_ref[rows, :]
    turned_high, turned_low = split(sorted_rows[...].T)
    for k in range(LATE):
        link = LINKS - LATE + k
        high, low = split(dot3(turned_high, turned_low, high_ref[link], low_ref[link]))
        weight_high_ref[k] = high
        weight_low_ref[k] = low
    total = jnp.zeros((ROWS, MODES), jnp.float32)
    for link, ref in enumerate(basis_refs):
        b_high, b_low = split(ref[...])
        total += dot3(high_ref[link], low_ref[link], b_high, b_low)
    for part in range(ROWS // MODES):
        rows = slice(part * MODES, (part + 1) * MODES)
        column = jnp.broadcast_to(springs_ref[:, rows], (MODES, MODES)).T
        total_ref[rows, :] = column * own_ref[rows, :]
    for rows, target in halves():
        total_ref[rows, :] += total[target, :]
        sorted_rows[target, :] = total_ref[rows, :]
    partial_ref[...] = dot3(turned_high, turned_low, *split(sorted_rows[...]))


def reduce_late(scale, side_ref, weight_high_ref, weight_low_ref, early_ref, *refs):
    basis_refs, (kept_ref, sent_ref, partial) = refs[:LATE], refs[LATE:]
    total = early_ref[...]
    for k, ref in enumerate(basis_refs):
        total += dot3(weight_high_ref[k], weight_low_ref[k], *split(ref[...]))
    partial[...] = total * scale
    half = MODES // 2
    kept_ref[...] = partial[pl.ds(pl.multiple_of(side_ref[0] * half, half), half), :]
    sent_ref[...] = partial[pl.ds(pl.multiple_of((1 - side_ref[0]) * half, half), half), :]


def add_after(first_ref, second_ref, done_ref, sum_ref):
    sum_ref[...] = first_ref[...] + second_ref[...]


def join(side_ref, mine_ref, other_ref, whole_ref):
    half = MODES // 2
    whole_ref[pl.ds(pl.multiple_of(side_ref[0] * half, half), half), :] = mine_ref[...]
    whole_ref[pl.ds(pl.multiple_of((1 - side_ref[0]) * half, half), half), :] = other_ref[...]


def project_late(high_ref, low_ref, total_ref, *refs):
    basis_refs, (stiff_ref, done_ref) = refs[:LATE], refs[LATE:]
    total = jnp.zeros((ROWS, MODES), jnp.float32)
    for k, ref in enumerate(basis_refs):
        b_high, b_low = split(ref[...])
        total += dot3(high_ref[LINKS - LATE + k], low_ref[LINKS - LATE + k], b_high, b_low)
    for rows, target in halves():
        stiff_ref[rows, :] = total_ref[rows, :] + total[target, :]
    done_ref[...] = jnp.zeros_like(done_ref)


def steps(n, me):
    even, even_four = me % 2 == 0, (me // 4) % 2 == 0

    def one_of(first, when_first):
        return jnp.where(when_first, first, n - first)

    return (
        0,
        one_of(4, even_four),
        one_of(n - 4, even_four),
        one_of(1, even),
        one_of(n - 1, even),
        n // 2,
        one_of(5, even),
        one_of(n - 5, even),
    )


def pick(first_ref, second_ref, near_ref, next_ref):
    me = lax.axis_index("row")
    straight = (me % 2 == 1) == ((me // 4) % 2 == 0)

    @pl.when(straight)
    def _():
        near_ref[...] = first_ref[...]
        next_ref[...] = second_ref[...]

    @pl.when(jnp.logical_not(straight))
    def _():
        near_ref[...] = second_ref[...]
        next_ref[...] = first_ref[...]


def shards(basis, springs, tangent_blocks, tile_rows, tile_owner, tile_offset, tile_count):
    n = lax.axis_size("row")
    me = lax.axis_index("row")
    smem = pl.BlockSpec(memory_space=pltpu.SMEM)
    vmem = pl.BlockSpec(memory_space=pltpu.VMEM)
    half, full = jnp.bfloat16, jnp.float32
    params = pltpu.CompilerParams(vmem_limit_bytes=32 * 2**20)

    held = pl.pallas_call(
        prepare,
        out_shape=jax.ShapeDtypeStruct((ROWS, MODES), full),
        in_specs=[vmem],
        out_specs=vmem,
        compiler_params=params,
        cost_estimate=pl.CostEstimate(flops=10_000_000_000, bytes_accessed=300_000, transcendentals=0),
        name="prepare",
    )(basis)

    def trade(block, partner):
        return lax.ppermute(block, "row", [(d, partner(d) % n) for d in range(n)])

    def near(d):
        return d ^ 1

    def next_chip(d):
        return d + 1 if d % 2 else d - 1

    first = trade(basis, lambda d: d - 4 if d // 4 % 2 else d + 4)
    second = trade(basis, lambda d: d + 4 if d // 4 % 2 else d - 4)
    across = trade(held, lambda d: d + n // 2)
    beside, beyond = trade(held, near), trade(held, next_chip)
    near_sent, next_sent = pl.pallas_call(
        pick,
        out_shape=(jax.ShapeDtypeStruct((ROWS, MODES), full),) * 2,
        in_specs=[vmem] * 2,
        out_specs=(vmem,) * 2,
        compiler_params=params,
        cost_estimate=pl.CostEstimate(flops=0, bytes_accessed=500_000, transcendentals=0),
        name="pick",
    )(first, second)
    far_near, far_next = trade(near_sent, near), trade(next_sent, next_chip)

    blocks = tangent_blocks.reshape(CAP // 8, 8, HALF, 128).transpose(0, 2, 1, 3).reshape(CAP * HALF, 128)
    high, low = pl.pallas_call(
        assemble,
        out_shape=(
            jax.ShapeDtypeStruct((LINKS, ROWS, ROWS), half),
            jax.ShapeDtypeStruct((LINKS, ROWS, ROWS), half),
        ),
        in_specs=[smem] + [vmem] * 4,
        out_specs=(vmem,) * 2,
        scratch_shapes=[
            pltpu.VMEM(((CAP + 1) * HALF, 128), full),
            pltpu.VMEM((1, CAP), jnp.int32),
            pltpu.SMEM((1, CAP), jnp.int32),
            pltpu.SemaphoreType.DMA(()),
        ],
        compiler_params=params,
        cost_estimate=pl.CostEstimate(flops=10_000_000, bytes_accessed=8_000_000, transcendentals=0),
        name="assemble",
    )(tile_count, tile_rows, tile_owner[:, 0], tile_offset, blocks)

    total, early, weight_high, weight_low = pl.pallas_call(
        project_early,
        out_shape=(
            jax.ShapeDtypeStruct((ROWS, MODES), full),
            jax.ShapeDtypeStruct((MODES, MODES), full),
            jax.ShapeDtypeStruct((LATE, MODES, ROWS), half),
            jax.ShapeDtypeStruct((LATE, MODES, ROWS), half),
        ),
        in_specs=[vmem] * (3 + LINKS - LATE),
        out_specs=(vmem,) * 4,
        scratch_shapes=[pltpu.VMEM((ROWS, MODES), full)],
        compiler_params=params,
        cost_estimate=pl.CostEstimate(flops=300_000_000, bytes_accessed=2_500_000, transcendentals=0),
        name="project_early",
    )(high, low, springs.reshape(1, ROWS), held, first, second, beside, beyond)

    side = me
    for shift in (8, 4, 2, 1):
        side = side ^ (side >> shift)
    side = (side & 1).reshape(1)
    piece = jax.ShapeDtypeStruct((MODES // 2, MODES), full)
    kept, sent = pl.pallas_call(
        functools.partial(reduce_late, 1.0 / (basis.shape[0] * n)),
        out_shape=(piece, piece),
        in_specs=[smem] + [vmem] * (3 + LATE),
        out_specs=(vmem,) * 2,
        scratch_shapes=[pltpu.VMEM((MODES, MODES), full)],
        compiler_params=params,
        cost_estimate=pl.CostEstimate(flops=80_000_000, bytes_accessed=700_000, transcendentals=0),
        name="reduce_late",
    )(side, weight_high, weight_low, early, across, far_near, far_next)

    stiff_image, done = pl.pallas_call(
        project_late,
        out_shape=(jax.ShapeDtypeStruct((ROWS, MODES), full), jax.ShapeDtypeStruct((8, 128), full)),
        in_specs=[vmem] * (3 + LATE),
        out_specs=(vmem,) * 2,
        compiler_params=params,
        cost_estimate=pl.CostEstimate(flops=160_000_000, bytes_accessed=1_500_000, transcendentals=0),
        name="project_late",
    )(high, low, total, across, far_near, far_next)

    def swap(block, apart):
        return lax.ppermute(block, "row", [(d, d ^ apart) for d in range(n)])

    mine = kept + swap(sent, 1)
    mine = pl.pallas_call(
        add_after,
        out_shape=piece,
        in_specs=[vmem] * 3,
        out_specs=vmem,
        compiler_params=params,
        name="add_after",
    )(mine, swap(mine, 3), done)
    apart = 4
    while apart < n:
        mine += swap(mine, apart + 1)
        apart *= 2
    reduced = pl.pallas_call(
        join,
        out_shape=jax.ShapeDtypeStruct((MODES, MODES), full),
        in_specs=[smem, vmem, vmem],
        out_specs=vmem,
        compiler_params=params,
        cost_estimate=pl.CostEstimate(flops=0, bytes_accessed=130_000, transcendentals=0),
        name="join",
    )(side, mine, swap(mine, 1))
    return (stiff_image, reduced)


def solution(mesh):
    in_specs = (
        P(("groups", "row"), None),
        P(("groups", "row")),
        P(("groups", "row"), None),
        P(("groups", "row")),
        P(("groups", "row"), None),
        P(("groups", "row")),
        P(("groups", "row")),
    )
    out_specs = (P(("groups", "row"), None), P("groups", None))
    return jax.shard_map(shards, mesh=mesh, in_specs=in_specs, out_specs=out_specs, check_vma=False)
```

```python
import functools

import jax
import jax.numpy as jnp
from jax import lax
from jax.experimental import pallas as pl
from jax.experimental.pallas import tpu as pltpu
from jax.sharding import PartitionSpec as P

B = 64
MODES = 128
BR_DEV = 4
CAP = 128
LINKS = 8
LATE = 3
HALF = B // 2
ROWS = BR_DEV * B


def split(x):
    high = x.astype(jnp.bfloat16)
    return high, (x - high.astype(jnp.float32)).astype(jnp.bfloat16)


def dot3(a_high, a_low, b_high, b_low):
    dot = functools.partial(jnp.dot, preferred_element_type=jnp.float32)
    return dot(a_high, b_high) + (dot(a_low, b_high) + dot(a_high, b_low))


def halves():
    for r in range(BR_DEV):
        for h in range(2):
            yield pl.ds(r * B + h, HALF, stride=2), slice(r * B + h * HALF, r * B + (h + 1) * HALF)


def prepare(basis_ref, held_ref):
    held_ref[...] = basis_ref[...]


def assemble(count_ref, rows_ref, owner_ref, offset_ref, blocks_ref, high_ref, low_ref, dense, placed, place, arrived):
    n, me = lax.axis_size("row"), lax.axis_index("row")
    away = lax.rem(owner_ref[...].reshape(1, CAP) - me + n, n)
    link = jnp.zeros_like(away)
    for k, step in enumerate(steps(n, me)):
        link = jnp.where(away == step, k, link)
    target = (link * BR_DEV + rows_ref[...].reshape(1, CAP)) * BR_DEV + offset_ref[...].reshape(1, CAP)
    slot = lax.broadcasted_iota(jnp.int32, (1, CAP), 1)
    placed[...] = jnp.where(slot < count_ref[0], target, CAP)
    copy = pltpu.make_async_copy(placed, place, arrived)
    copy.start()
    dense[...] = jnp.zeros_like(dense)
    copy.wait()

    @pl.loop(0, CAP // 8)
    def _(group):
        for k in range(8):
            block = blocks_ref[pl.ds(group * (8 * HALF) + k, HALF, stride=8), :]
            target = pl.ds(pl.multiple_of(place[0, group * 8 + k] * HALF, HALF), HALF)
            dense[target, :] += block

    left = lax.broadcasted_iota(jnp.int32, (HALF, 128), 1) < B

    @pl.loop(0, LINKS)
    def _(link):
        for r in range(BR_DEV):
            for pair in range(BR_DEV // 2):
                start = ((link * BR_DEV + r) * BR_DEV + 2 * pair) * HALF
                first = dense[pl.ds(pl.multiple_of(start, HALF), HALF), :]
                second = dense[pl.ds(pl.multiple_of(start + HALF, HALF), HALF), :]
                even = jnp.where(left, first, pltpu.roll(second, B, 1))
                odd = jnp.where(left, pltpu.roll(first, B, 1), second)
                for h, part in enumerate((even, odd)):
                    high, low = split(part)
                    rows = slice(r * B + h * HALF, r * B + (h + 1) * HALF)
                    high_ref[link, rows, pair * 128:(pair + 1) * 128] = high
                    low_ref[link, rows, pair * 128:(pair + 1) * 128] = low


def project_early(high_ref, low_ref, springs_ref, *refs):
    basis_refs, (total_ref, partial_ref, weight_high_ref, weight_low_ref, sorted_rows) = refs[:-5], refs[-5:]
    own_ref = basis_refs[0]
    for rows, target in halves():
        sorted_rows[target, :] = own_ref[rows, :]
    turned_high, turned_low = split(sorted_rows[...].T)
    for k in range(LATE):
        link = LINKS - LATE + k
        high, low = split(dot3(turned_high, turned_low, high_ref[link], low_ref[link]))
        weight_high_ref[k] = high
        weight_low_ref[k] = low
    total = jnp.zeros((ROWS, MODES), jnp.float32)
    for link, ref in enumerate(basis_refs):
        b_high, b_low = split(ref[...])
        total += dot3(high_ref[link], low_ref[link], b_high, b_low)
    for part in range(ROWS // MODES):
        rows = slice(part * MODES, (part + 1) * MODES)
        column = jnp.broadcast_to(springs_ref[:, rows], (MODES, MODES)).T
        total_ref[rows, :] = column * own_ref[rows, :]
    for rows, target in halves():
        total_ref[rows, :] += total[target, :]
        sorted_rows[target, :] = total_ref[rows, :]
    partial_ref[...] = dot3(turned_high, turned_low, *split(sorted_rows[...]))


def reduce_late(scale, side_ref, weight_high_ref, weight_low_ref, early_ref, *refs):
    basis_refs, (kept_ref, sent_ref, partial) = refs[:LATE], refs[LATE:]
    total = early_ref[...]
    for k, ref in enumerate(basis_refs):
        total += dot3(weight_high_ref[k], weight_low_ref[k], *split(ref[...]))
    partial[...] = total * scale
    half = MODES // 2
    kept_ref[...] = partial[pl.ds(pl.multiple_of(side_ref[0] * half, half), half), :]
    sent_ref[...] = partial[pl.ds(pl.multiple_of((1 - side_ref[0]) * half, half), half), :]


def add_after(first_ref, second_ref, done_ref, sum_ref):
    sum_ref[...] = first_ref[...] + second_ref[...]


def join(side_ref, mine_ref, other_ref, whole_ref):
    half = MODES // 2
    whole_ref[pl.ds(pl.multiple_of(side_ref[0] * half, half), half), :] = mine_ref[...]
    whole_ref[pl.ds(pl.multiple_of((1 - side_ref[0]) * half, half), half), :] = other_ref[...]


def project_late(high_ref, low_ref, total_ref, *refs):
    basis_refs, (stiff_ref, done_ref) = refs[:LATE], refs[LATE:]
    total = jnp.zeros((ROWS, MODES), jnp.float32)
    for k, ref in enumerate(basis_refs):
        b_high, b_low = split(ref[...])
        total += dot3(high_ref[LINKS - LATE + k], low_ref[LINKS - LATE + k], b_high, b_low)
    for rows, target in halves():
        stiff_ref[rows, :] = total_ref[rows, :] + total[target, :]
    done_ref[...] = jnp.zeros_like(done_ref)


def steps(n, me):
    even, even_four = me % 2 == 0, (me // 4) % 2 == 0

    def one_of(first, when_first):
        return jnp.where(when_first, first, n - first)

    return (
        0,
        one_of(n - 4, even_four),
        one_of(4, even_four),
        one_of(1, even),
        one_of(n - 1, even),
        n // 2,
        one_of(5, even),
        one_of(n - 5, even),
    )


def pick(first_ref, second_ref, near_ref, next_ref):
    me = lax.axis_index("row")
    straight = (me % 2 == 1) == ((me // 4) % 2 == 0)

    @pl.when(straight)
    def _():
        near_ref[...] = second_ref[...]
        next_ref[...] = first_ref[...]

    @pl.when(jnp.logical_not(straight))
    def _():
        near_ref[...] = first_ref[...]
        next_ref[...] = second_ref[...]


def shards(basis, springs, tangent_blocks, tile_rows, tile_owner, tile_offset, tile_count):
    n = lax.axis_size("row")
    me = lax.axis_index("row")
    smem = pl.BlockSpec(memory_space=pltpu.SMEM)
    vmem = pl.BlockSpec(memory_space=pltpu.VMEM)
    half, full = jnp.bfloat16, jnp.float32
    params = pltpu.CompilerParams(vmem_limit_bytes=32 * 2**20)

    held = pl.pallas_call(
        prepare,
        out_shape=jax.ShapeDtypeStruct((ROWS, MODES), full),
        in_specs=[vmem],
        out_specs=vmem,
        compiler_params=params,
        cost_estimate=pl.CostEstimate(flops=10_000_000_000, bytes_accessed=300_000, transcendentals=0),
        name="prepare",
    )(basis)

    def trade(block, partner):
        return lax.ppermute(block, "row", [(d, partner(d) % n) for d in range(n)])

    def near(d):
        return d ^ 1

    def next_chip(d):
        return d + 1 if d % 2 else d - 1

    def outer(d):
        return d - 4 if d // 4 % 2 else d + 4

    def inner(d):
        return d + 4 if d // 4 % 2 else d - 4

    first = trade(basis, inner)
    second = trade(basis, outer)
    across = trade(first, outer) if n == 16 else trade(held, lambda d: d + n // 2)
    beside, beyond = trade(held, near), trade(held, next_chip)
    near_sent, next_sent = pl.pallas_call(
        pick,
        out_shape=(jax.ShapeDtypeStruct((ROWS, MODES), full),) * 2,
        in_specs=[vmem] * 2,
        out_specs=(vmem,) * 2,
        compiler_params=params,
        cost_estimate=pl.CostEstimate(flops=0, bytes_accessed=500_000, transcendentals=0),
        name="pick",
    )(first, second)
    far_near, far_next = trade(near_sent, near), trade(next_sent, next_chip)

    blocks = tangent_blocks.reshape(CAP // 8, 8, HALF, 128).transpose(0, 2, 1, 3).reshape(CAP * HALF, 128)
    high, low = pl.pallas_call(
        assemble,
        out_shape=(
            jax.ShapeDtypeStruct((LINKS, ROWS, ROWS), half),
            jax.ShapeDtypeStruct((LINKS, ROWS, ROWS), half),
        ),
        in_specs=[smem] + [vmem] * 4,
        out_specs=(vmem,) * 2,
        scratch_shapes=[
            pltpu.VMEM(((CAP + 1) * HALF, 128), full),
            pltpu.VMEM((1, CAP), jnp.int32),
            pltpu.SMEM((1, CAP), jnp.int32),
            pltpu.SemaphoreType.DMA(()),
        ],
        compiler_params=params,
        cost_estimate=pl.CostEstimate(flops=10_000_000, bytes_accessed=8_000_000, transcendentals=0),
        name="assemble",
    )(tile_count, tile_rows, tile_owner[:, 0], tile_offset, blocks)

    total, early, weight_high, weight_low = pl.pallas_call(
        project_early,
        out_shape=(
            jax.ShapeDtypeStruct((ROWS, MODES), full),
            jax.ShapeDtypeStruct((MODES, MODES), full),
            jax.ShapeDtypeStruct((LATE, MODES, ROWS), half),
            jax.ShapeDtypeStruct((LATE, MODES, ROWS), half),
        ),
        in_specs=[vmem] * (3 + LINKS - LATE),
        out_specs=(vmem,) * 4,
        scratch_shapes=[pltpu.VMEM((ROWS, MODES), full)],
        compiler_params=params,
        cost_estimate=pl.CostEstimate(flops=300_000_000, bytes_accessed=2_500_000, transcendentals=0),
        name="project_early",
    )(high, low, springs.reshape(1, ROWS), held, first, second, beside, beyond)

    side = me
    for shift in (8, 4, 2, 1):
        side = side ^ (side >> shift)
    side = (side & 1).reshape(1)
    piece = jax.ShapeDtypeStruct((MODES // 2, MODES), full)
    kept, sent = pl.pallas_call(
        functools.partial(reduce_late, 1.0 / (basis.shape[0] * n)),
        out_shape=(piece, piece),
        in_specs=[smem] + [vmem] * (3 + LATE),
        out_specs=(vmem,) * 2,
        scratch_shapes=[pltpu.VMEM((MODES, MODES), full)],
        compiler_params=params,
        cost_estimate=pl.CostEstimate(flops=80_000_000, bytes_accessed=700_000, transcendentals=0),
        name="reduce_late",
    )(side, weight_high, weight_low, early, across, far_near, far_next)

    stiff_image, done = pl.pallas_call(
        project_late,
        out_shape=(jax.ShapeDtypeStruct((ROWS, MODES), full), jax.ShapeDtypeStruct((8, 128), full)),
        in_specs=[vmem] * (3 + LATE),
        out_specs=(vmem,) * 2,
        compiler_params=params,
        cost_estimate=pl.CostEstimate(flops=160_000_000, bytes_accessed=1_500_000, transcendentals=0),
        name="project_late",
    )(high, low, total, across, far_near, far_next)

    def swap(block, apart):
        return lax.ppermute(block, "row", [(d, d ^ apart) for d in range(n)])

    mine = kept + swap(sent, 1)
    mine = pl.pallas_call(
        add_after,
        out_shape=piece,
        in_specs=[vmem] * 3,
        out_specs=vmem,
        compiler_params=params,
        name="add_after",
    )(mine, swap(mine, 3), done)
    apart = 4
    while apart < n:
        mine += swap(mine, apart + 1)
        apart *= 2
    reduced = pl.pallas_call(
        join,
        out_shape=jax.ShapeDtypeStruct((MODES, MODES), full),
        in_specs=[smem, vmem, vmem],
        out_specs=vmem,
        compiler_params=params,
        cost_estimate=pl.CostEstimate(flops=0, bytes_accessed=130_000, transcendentals=0),
        name="join",
    )(side, mine, swap(mine, 1))
    return (stiff_image, reduced)


def solution(mesh):
    in_specs = (
        P(("groups", "row"), None),
        P(("groups", "row")),
        P(("groups", "row"), None),
        P(("groups", "row")),
        P(("groups", "row"), None),
        P(("groups", "row")),
        P(("groups", "row")),
    )
    out_specs = (P(("groups", "row"), None), P("groups", None))
    return jax.shard_map(shards, mesh=mesh, in_specs=in_specs, out_specs=out_specs, check_vma=False)
```

```python
import functools

import jax
import jax.numpy as jnp
from jax import lax
from jax.experimental import pallas as pl
from jax.experimental.pallas import tpu as pltpu
from jax.sharding import PartitionSpec as P

B = 64
MODES = 128
BR_DEV = 4
CAP = 128
LINKS = 8
LATE = 3
HALF = B // 2
ROWS = BR_DEV * B


def split(x):
    high = x.astype(jnp.bfloat16)
    return high, (x - high.astype(jnp.float32)).astype(jnp.bfloat16)


def dot3(a_high, a_low, b_high, b_low):
    dot = functools.partial(jnp.dot, preferred_element_type=jnp.float32)
    return dot(a_high, b_high) + (dot(a_low, b_high) + dot(a_high, b_low))


def halves():
    for r in range(BR_DEV):
        for h in range(2):
            yield pl.ds(r * B + h, HALF, stride=2), slice(r * B + h * HALF, r * B + (h + 1) * HALF)


def prepare(basis_ref, held_ref):
    held_ref[...] = basis_ref[...]


def assemble(count_ref, rows_ref, owner_ref, offset_ref, blocks_ref, high_ref, low_ref, dense, placed, place, arrived):
    n, me = lax.axis_size("row"), lax.axis_index("row")
    away = lax.rem(owner_ref[...].reshape(1, CAP) - me + n, n)
    link = jnp.zeros_like(away)
    for k, step in enumerate(steps(n, me)):
        link = jnp.where(away == step, k, link)
    target = (link * BR_DEV + rows_ref[...].reshape(1, CAP)) * BR_DEV + offset_ref[...].reshape(1, CAP)
    slot = lax.broadcasted_iota(jnp.int32, (1, CAP), 1)
    placed[...] = jnp.where(slot < count_ref[0], target, CAP)
    copy = pltpu.make_async_copy(placed, place, arrived)
    copy.start()
    dense[...] = jnp.zeros_like(dense)
    copy.wait()

    @pl.loop(0, CAP // 8)
    def _(group):
        for k in range(8):
            block = blocks_ref[pl.ds(group * (8 * HALF) + k, HALF, stride=8), :]
            target = pl.ds(pl.multiple_of(place[0, group * 8 + k] * HALF, HALF), HALF)
            dense[target, :] += block

    left = lax.broadcasted_iota(jnp.int32, (HALF, 128), 1) < B

    @pl.loop(0, LINKS)
    def _(link):
        for r in range(BR_DEV):
            for pair in range(BR_DEV // 2):
                start = ((link * BR_DEV + r) * BR_DEV + 2 * pair) * HALF
                first = dense[pl.ds(pl.multiple_of(start, HALF), HALF), :]
                second = dense[pl.ds(pl.multiple_of(start + HALF, HALF), HALF), :]
                even = jnp.where(left, first, pltpu.roll(second, B, 1))
                odd = jnp.where(left, pltpu.roll(first, B, 1), second)
                for h, part in enumerate((even, odd)):
                    high, low = split(part)
                    rows = slice(r * B + h * HALF, r * B + (h + 1) * HALF)
                    high_ref[link, rows, pair * 128:(pair + 1) * 128] = high
                    low_ref[link, rows, pair * 128:(pair + 1) * 128] = low


def project_early(high_ref, low_ref, springs_ref, *refs):
    basis_refs, (total_ref, partial_ref, weight_high_ref, weight_low_ref, sorted_rows) = refs[:-5], refs[-5:]
    own_ref = basis_refs[0]
    for rows, target in halves():
        sorted_rows[target, :] = own_ref[rows, :]
    turned_high, turned_low = split(sorted_rows[...].T)
    for k in range(LATE):
        link = LINKS - LATE + k
        high, low = split(dot3(turned_high, turned_low, high_ref[link], low_ref[link]))
        weight_high_ref[k] = high
        weight_low_ref[k] = low
    total = jnp.zeros((ROWS, MODES), jnp.float32)
    for link, ref in enumerate(basis_refs):
        b_high, b_low = split(ref[...])
        total += dot3(high_ref[link], low_ref[link], b_high, b_low)
    for part in range(ROWS // MODES):
        rows = slice(part * MODES, (part + 1) * MODES)
        column = jnp.broadcast_to(springs_ref[:, rows], (MODES, MODES)).T
        total_ref[rows, :] = column * own_ref[rows, :]
    for rows, target in halves():
        total_ref[rows, :] += total[target, :]
        sorted_rows[target, :] = total_ref[rows, :]
    partial_ref[...] = dot3(turned_high, turned_low, *split(sorted_rows[...]))


def reduce_late(scale, side_ref, weight_high_ref, weight_low_ref, early_ref, *refs):
    basis_refs, (kept_ref, sent_ref, partial) = refs[:LATE], refs[LATE:]
    total = early_ref[...]
    for k, ref in enumerate(basis_refs):
        total += dot3(weight_high_ref[k], weight_low_ref[k], *split(ref[...]))
    partial[...] = total * scale
    half = MODES // 2
    kept_ref[...] = partial[pl.ds(pl.multiple_of(side_ref[0] * half, half), half), :]
    sent_ref[...] = partial[pl.ds(pl.multiple_of((1 - side_ref[0]) * half, half), half), :]


def add_after(first_ref, second_ref, done_ref, sum_ref):
    sum_ref[...] = first_ref[...] + second_ref[...]


def join(side_ref, mine_ref, other_ref, whole_ref):
    half = MODES // 2
    whole_ref[pl.ds(pl.multiple_of(side_ref[0] * half, half), half), :] = mine_ref[...]
    whole_ref[pl.ds(pl.multiple_of((1 - side_ref[0]) * half, half), half), :] = other_ref[...]


def project_late(high_ref, low_ref, total_ref, *refs):
    basis_refs, (stiff_ref, done_ref) = refs[:LATE], refs[LATE:]
    total = jnp.zeros((ROWS, MODES), jnp.float32)
    for k, ref in enumerate(basis_refs):
        b_high, b_low = split(ref[...])
        total += dot3(high_ref[LINKS - LATE + k], low_ref[LINKS - LATE + k], b_high, b_low)
    for rows, target in halves():
        stiff_ref[rows, :] = total_ref[rows, :] + total[target, :]
    done_ref[...] = jnp.zeros_like(done_ref)


def steps(n, me):
    even, even_four = me % 2 == 0, (me // 4) % 2 == 0

    def one_of(first, when_first):
        return jnp.where(when_first, first, n - first)

    return (
        0,
        one_of(n - 4, even_four),
        one_of(4, even_four),
        one_of(1, even),
        one_of(n - 1, even),
        one_of(n - 5, even),
        n // 2,
        one_of(5, even),
    )


def pick(first_ref, second_ref, near_ref, next_ref):
    me = lax.axis_index("row")
    straight = (me % 2 == 1) == ((me // 4) % 2 == 0)

    @pl.when(straight)
    def _():
        near_ref[...] = second_ref[...]
        next_ref[...] = first_ref[...]

    @pl.when(jnp.logical_not(straight))
    def _():
        near_ref[...] = first_ref[...]
        next_ref[...] = second_ref[...]


def shards(basis, springs, tangent_blocks, tile_rows, tile_owner, tile_offset, tile_count):
    n = lax.axis_size("row")
    me = lax.axis_index("row")
    smem = pl.BlockSpec(memory_space=pltpu.SMEM)
    vmem = pl.BlockSpec(memory_space=pltpu.VMEM)
    half, full = jnp.bfloat16, jnp.float32
    params = pltpu.CompilerParams(vmem_limit_bytes=32 * 2**20)

    held = pl.pallas_call(
        prepare,
        out_shape=jax.ShapeDtypeStruct((ROWS, MODES), full),
        in_specs=[vmem],
        out_specs=vmem,
        compiler_params=params,
        cost_estimate=pl.CostEstimate(flops=10_000_000_000, bytes_accessed=300_000, transcendentals=0),
        name="prepare",
    )(basis)

    def trade(block, partner):
        return lax.ppermute(block, "row", [(d, partner(d) % n) for d in range(n)])

    def near(d):
        return d ^ 1

    def next_chip(d):
        return d + 1 if d % 2 else d - 1

    def outer(d):
        return d - 4 if d // 4 % 2 else d + 4

    def inner(d):
        return d + 4 if d // 4 % 2 else d - 4

    first = trade(basis, inner)
    second = trade(basis, outer)
    across = trade(first, outer) if n == 16 else trade(held, lambda d: d + n // 2)
    beside, beyond = trade(held, near), trade(held, next_chip)
    near_sent, next_sent = pl.pallas_call(
        pick,
        out_shape=(jax.ShapeDtypeStruct((ROWS, MODES), full),) * 2,
        in_specs=[vmem] * 2,
        out_specs=(vmem,) * 2,
        compiler_params=params,
        cost_estimate=pl.CostEstimate(flops=0, bytes_accessed=500_000, transcendentals=0),
        name="pick",
    )(first, second)
    far_next, far_near = trade(next_sent, next_chip), trade(near_sent, near)

    blocks = tangent_blocks.reshape(CAP // 8, 8, HALF, 128).transpose(0, 2, 1, 3).reshape(CAP * HALF, 128)
    high, low = pl.pallas_call(
        assemble,
        out_shape=(
            jax.ShapeDtypeStruct((LINKS, ROWS, ROWS), half),
            jax.ShapeDtypeStruct((LINKS, ROWS, ROWS), half),
        ),
        in_specs=[smem] + [vmem] * 4,
        out_specs=(vmem,) * 2,
        scratch_shapes=[
            pltpu.VMEM(((CAP + 1) * HALF, 128), full),
            pltpu.VMEM((1, CAP), jnp.int32),
            pltpu.SMEM((1, CAP), jnp.int32),
            pltpu.SemaphoreType.DMA(()),
        ],
        compiler_params=params,
        cost_estimate=pl.CostEstimate(flops=10_000_000, bytes_accessed=8_000_000, transcendentals=0),
        name="assemble",
    )(tile_count, tile_rows, tile_owner[:, 0], tile_offset, blocks)

    total, early, weight_high, weight_low = pl.pallas_call(
        project_early,
        out_shape=(
            jax.ShapeDtypeStruct((ROWS, MODES), full),
            jax.ShapeDtypeStruct((MODES, MODES), full),
            jax.ShapeDtypeStruct((LATE, MODES, ROWS), half),
            jax.ShapeDtypeStruct((LATE, MODES, ROWS), half),
        ),
        in_specs=[vmem] * (3 + LINKS - LATE),
        out_specs=(vmem,) * 4,
        scratch_shapes=[pltpu.VMEM((ROWS, MODES), full)],
        compiler_params=params,
        cost_estimate=pl.CostEstimate(flops=20_000_000_000, bytes_accessed=2_500_000, transcendentals=0),
        name="project_early",
    )(high, low, springs.reshape(1, ROWS), held, first, second, beside, beyond)

    side = me
    for shift in (8, 4, 2, 1):
        side = side ^ (side >> shift)
    side = (side & 1).reshape(1)
    piece = jax.ShapeDtypeStruct((MODES // 2, MODES), full)
    kept, sent = pl.pallas_call(
        functools.partial(reduce_late, 1.0 / (basis.shape[0] * n)),
        out_shape=(piece, piece),
        in_specs=[smem] + [vmem] * (3 + LATE),
        out_specs=(vmem,) * 2,
        scratch_shapes=[pltpu.VMEM((MODES, MODES), full)],
        compiler_params=params,
        cost_estimate=pl.CostEstimate(flops=80_000_000, bytes_accessed=700_000, transcendentals=0),
        name="reduce_late",
    )(side, weight_high, weight_low, early, far_next, across, far_near)

    stiff_image, done = pl.pallas_call(
        project_late,
        out_shape=(jax.ShapeDtypeStruct((ROWS, MODES), full), jax.ShapeDtypeStruct((8, 128), full)),
        in_specs=[vmem] * (3 + LATE),
        out_specs=(vmem,) * 2,
        compiler_params=params,
        cost_estimate=pl.CostEstimate(flops=160_000_000, bytes_accessed=1_500_000, transcendentals=0),
        name="project_late",
    )(high, low, total, far_next, across, far_near)

    def swap(block, apart):
        return lax.ppermute(block, "row", [(d, d ^ apart) for d in range(n)])

    mine = kept + swap(sent, 1)
    mine = pl.pallas_call(
        add_after,
        out_shape=piece,
        in_specs=[vmem] * 3,
        out_specs=vmem,
        compiler_params=params,
        name="add_after",
    )(mine, swap(mine, 3), done)
    apart = 4
    while apart < n:
        mine += swap(mine, apart + 1)
        apart *= 2
    reduced = pl.pallas_call(
        join,
        out_shape=jax.ShapeDtypeStruct((MODES, MODES), full),
        in_specs=[smem, vmem, vmem],
        out_specs=vmem,
        compiler_params=params,
        cost_estimate=pl.CostEstimate(flops=0, bytes_accessed=130_000, transcendentals=0),
        name="join",
    )(side, mine, swap(mine, 1))
    return (stiff_image, reduced)


def solution(mesh):
    in_specs = (
        P(("groups", "row"), None),
        P(("groups", "row")),
        P(("groups", "row"), None),
        P(("groups", "row")),
        P(("groups", "row"), None),
        P(("groups", "row")),
        P(("groups", "row")),
    )
    out_specs = (P(("groups", "row"), None), P("groups", None))
    return jax.shard_map(shards, mesh=mesh, in_specs=in_specs, out_specs=out_specs, check_vma=False)
```

```python
import functools

import jax
import jax.numpy as jnp
from jax import lax
from jax.experimental import pallas as pl
from jax.experimental.pallas import tpu as pltpu
from jax.sharding import PartitionSpec as P

B = 64
MODES = 128
BR_DEV = 4
CAP = 128
LINKS = 8
LATE = 3
HALF = B // 2
ROWS = BR_DEV * B


def split(x):
    high = x.astype(jnp.bfloat16)
    return high, (x - high.astype(jnp.float32)).astype(jnp.bfloat16)


def dot3(a_high, a_low, b_high, b_low):
    dot = functools.partial(jnp.dot, preferred_element_type=jnp.float32)
    return dot(a_high, b_high) + (dot(a_low, b_high) + dot(a_high, b_low))


def halves():
    for r in range(BR_DEV):
        for h in range(2):
            yield pl.ds(r * B + h, HALF, stride=2), slice(r * B + h * HALF, r * B + (h + 1) * HALF)


def prepare(basis_ref, held_ref):
    held_ref[...] = basis_ref[...]


def assemble(count_ref, rows_ref, owner_ref, offset_ref, blocks_ref, high_ref, low_ref, dense, placed, place, arrived):
    n, me = lax.axis_size("row"), lax.axis_index("row")
    away = lax.rem(owner_ref[...].reshape(1, CAP) - me + n, n)
    link = jnp.zeros_like(away)
    for k, step in enumerate(steps(n, me)):
        link = jnp.where(away == step, k, link)
    target = (link * BR_DEV + rows_ref[...].reshape(1, CAP)) * BR_DEV + offset_ref[...].reshape(1, CAP)
    slot = lax.broadcasted_iota(jnp.int32, (1, CAP), 1)
    placed[...] = jnp.where(slot < count_ref[0], target, CAP)
    copy = pltpu.make_async_copy(placed, place, arrived)
    copy.start()
    dense[...] = jnp.zeros_like(dense)
    copy.wait()

    @pl.loop(0, CAP // 8)
    def _(group):
        for k in range(8):
            block = blocks_ref[pl.ds(group * (8 * HALF) + k, HALF, stride=8), :]
            target = pl.ds(pl.multiple_of(place[0, group * 8 + k] * HALF, HALF), HALF)
            dense[target, :] += block

    left = lax.broadcasted_iota(jnp.int32, (HALF, 128), 1) < B

    @pl.loop(0, LINKS)
    def _(link):
        for r in range(BR_DEV):
            for pair in range(BR_DEV // 2):
                start = ((link * BR_DEV + r) * BR_DEV + 2 * pair) * HALF
                first = dense[pl.ds(pl.multiple_of(start, HALF), HALF), :]
                second = dense[pl.ds(pl.multiple_of(start + HALF, HALF), HALF), :]
                even = jnp.where(left, first, pltpu.roll(second, B, 1))
                odd = jnp.where(left, pltpu.roll(first, B, 1), second)
                for h, part in enumerate((even, odd)):
                    high, low = split(part)
                    rows = slice(r * B + h * HALF, r * B + (h + 1) * HALF)
                    high_ref[link, rows, pair * 128:(pair + 1) * 128] = high
                    low_ref[link, rows, pair * 128:(pair + 1) * 128] = low


def project_early(high_ref, low_ref, springs_ref, *refs):
    basis_refs, (total_ref, partial_ref, weight_high_ref, weight_low_ref, sorted_rows) = refs[:-5], refs[-5:]
    own_ref = basis_refs[0]
    for rows, target in halves():
        sorted_rows[target, :] = own_ref[rows, :]
    turned_high, turned_low = split(sorted_rows[...].T)
    for k in range(LATE):
        link = LINKS - LATE + k
        high, low = split(dot3(turned_high, turned_low, high_ref[link], low_ref[link]))
        weight_high_ref[k] = high
        weight_low_ref[k] = low
    total = jnp.zeros((ROWS, MODES), jnp.float32)
    for link, ref in enumerate(basis_refs):
        b_high, b_low = split(ref[...])
        total += dot3(high_ref[link], low_ref[link], b_high, b_low)
    for part in range(ROWS // MODES):
        rows = slice(part * MODES, (part + 1) * MODES)
        column = jnp.broadcast_to(springs_ref[:, rows], (MODES, MODES)).T
        total_ref[rows, :] = column * own_ref[rows, :]
    for rows, target in halves():
        total_ref[rows, :] += total[target, :]
        sorted_rows[target, :] = total_ref[rows, :]
    partial_ref[...] = dot3(turned_high, turned_low, *split(sorted_rows[...]))


def reduce_late(scale, side_ref, weight_high_ref, weight_low_ref, early_ref, *refs):
    basis_refs, (kept_ref, sent_ref, partial) = refs[:LATE], refs[LATE:]
    total = early_ref[...]
    for k, ref in enumerate(basis_refs):
        total += dot3(weight_high_ref[k], weight_low_ref[k], *split(ref[...]))
    partial[...] = total * scale
    half = MODES // 2
    kept_ref[...] = partial[pl.ds(pl.multiple_of(side_ref[0] * half, half), half), :]
    sent_ref[...] = partial[pl.ds(pl.multiple_of((1 - side_ref[0]) * half, half), half), :]


def add_after(first_ref, second_ref, done_ref, sum_ref):
    sum_ref[...] = first_ref[...] + second_ref[...]


def join(side_ref, mine_ref, other_ref, whole_ref):
    half = MODES // 2
    whole_ref[pl.ds(pl.multiple_of(side_ref[0] * half, half), half), :] = mine_ref[...]
    whole_ref[pl.ds(pl.multiple_of((1 - side_ref[0]) * half, half), half), :] = other_ref[...]


def project_late(high_ref, low_ref, total_ref, *refs):
    basis_refs, (stiff_ref, done_ref) = refs[:LATE], refs[LATE:]
    total = jnp.zeros((ROWS, MODES), jnp.float32)
    for k, ref in enumerate(basis_refs):
        b_high, b_low = split(ref[...])
        total += dot3(high_ref[LINKS - LATE + k], low_ref[LINKS - LATE + k], b_high, b_low)
    for rows, target in halves():
        stiff_ref[rows, :] = total_ref[rows, :] + total[target, :]
    done_ref[...] = jnp.zeros_like(done_ref)


def steps(n, me):
    even, even_four = me % 2 == 0, (me // 4) % 2 == 0

    def one_of(first, when_first):
        return jnp.where(when_first, first, n - first)

    return (
        0,
        one_of(n - 4, even_four),
        one_of(4, even_four),
        one_of(1, even),
        one_of(n - 1, even),
        n // 2,
        one_of(n - 5, even),
        one_of(5, even),
    )


def pick(first_ref, second_ref, outer_ref, next_ref, near_ref):
    outer_ref[...] = first_ref[...]
    me = lax.axis_index("row")
    straight = (me % 2 == 1) == ((me // 4) % 2 == 0)

    @pl.when(straight)
    def _():
        near_ref[...] = second_ref[...]
        next_ref[...] = first_ref[...]

    @pl.when(jnp.logical_not(straight))
    def _():
        near_ref[...] = first_ref[...]
        next_ref[...] = second_ref[...]


def shards(basis, springs, tangent_blocks, tile_rows, tile_owner, tile_offset, tile_count):
    n = lax.axis_size("row")
    me = lax.axis_index("row")
    smem = pl.BlockSpec(memory_space=pltpu.SMEM)
    vmem = pl.BlockSpec(memory_space=pltpu.VMEM)
    half, full = jnp.bfloat16, jnp.float32
    params = pltpu.CompilerParams(vmem_limit_bytes=32 * 2**20)

    held = pl.pallas_call(
        prepare,
        out_shape=jax.ShapeDtypeStruct((ROWS, MODES), full),
        in_specs=[vmem],
        out_specs=vmem,
        compiler_params=params,
        cost_estimate=pl.CostEstimate(flops=10_000_000_000, bytes_accessed=300_000, transcendentals=0),
        name="prepare",
    )(basis)

    def trade(block, partner):
        return lax.ppermute(block, "row", [(d, partner(d) % n) for d in range(n)])

    def near(d):
        return d ^ 1

    def next_chip(d):
        return d + 1 if d % 2 else d - 1

    def outer(d):
        return d - 4 if d // 4 % 2 else d + 4

    def inner(d):
        return d + 4 if d // 4 % 2 else d - 4

    first = trade(basis, inner)
    second = trade(basis, outer)
    beside, beyond = trade(held, near), trade(held, next_chip)
    outer_sent, next_sent, near_sent = pl.pallas_call(
        pick,
        out_shape=(jax.ShapeDtypeStruct((ROWS, MODES), full),) * 3,
        in_specs=[vmem] * 2,
        out_specs=(vmem,) * 3,
        compiler_params=params,
        cost_estimate=pl.CostEstimate(flops=0, bytes_accessed=700_000, transcendentals=0),
        name="pick",
    )(first, second)
    across = trade(outer_sent, outer) if n == 16 else trade(held, lambda d: d + n // 2)
    far_next, far_near = trade(next_sent, next_chip), trade(near_sent, near)

    blocks = tangent_blocks.reshape(CAP // 8, 8, HALF, 128).transpose(0, 2, 1, 3).reshape(CAP * HALF, 128)
    high, low = pl.pallas_call(
        assemble,
        out_shape=(
            jax.ShapeDtypeStruct((LINKS, ROWS, ROWS), half),
            jax.ShapeDtypeStruct((LINKS, ROWS, ROWS), half),
        ),
        in_specs=[smem] + [vmem] * 4,
        out_specs=(vmem,) * 2,
        scratch_shapes=[
            pltpu.VMEM(((CAP + 1) * HALF, 128), full),
            pltpu.VMEM((1, CAP), jnp.int32),
            pltpu.SMEM((1, CAP), jnp.int32),
            pltpu.SemaphoreType.DMA(()),
        ],
        compiler_params=params,
        cost_estimate=pl.CostEstimate(flops=10_000_000, bytes_accessed=8_000_000, transcendentals=0),
        name="assemble",
    )(tile_count, tile_rows, tile_owner[:, 0], tile_offset, blocks)

    total, early, weight_high, weight_low = pl.pallas_call(
        project_early,
        out_shape=(
            jax.ShapeDtypeStruct((ROWS, MODES), full),
            jax.ShapeDtypeStruct((MODES, MODES), full),
            jax.ShapeDtypeStruct((LATE, MODES, ROWS), half),
            jax.ShapeDtypeStruct((LATE, MODES, ROWS), half),
        ),
        in_specs=[vmem] * (3 + LINKS - LATE),
        out_specs=(vmem,) * 4,
        scratch_shapes=[pltpu.VMEM((ROWS, MODES), full)],
        compiler_params=params,
        cost_estimate=pl.CostEstimate(flops=20_000_000_000, bytes_accessed=2_500_000, transcendentals=0),
        name="project_early",
    )(high, low, springs.reshape(1, ROWS), held, first, second, beside, beyond)

    side = me
    for shift in (8, 4, 2, 1):
        side = side ^ (side >> shift)
    side = (side & 1).reshape(1)
    piece = jax.ShapeDtypeStruct((MODES // 2, MODES), full)
    kept, sent = pl.pallas_call(
        functools.partial(reduce_late, 1.0 / (basis.shape[0] * n)),
        out_shape=(piece, piece),
        in_specs=[smem] + [vmem] * (3 + LATE),
        out_specs=(vmem,) * 2,
        scratch_shapes=[pltpu.VMEM((MODES, MODES), full)],
        compiler_params=params,
        cost_estimate=pl.CostEstimate(flops=80_000_000, bytes_accessed=700_000, transcendentals=0),
        name="reduce_late",
    )(side, weight_high, weight_low, early, across, far_next, far_near)

    stiff_image, done = pl.pallas_call(
        project_late,
        out_shape=(jax.ShapeDtypeStruct((ROWS, MODES), full), jax.ShapeDtypeStruct((8, 128), full)),
        in_specs=[vmem] * (3 + LATE),
        out_specs=(vmem,) * 2,
        compiler_params=params,
        cost_estimate=pl.CostEstimate(flops=160_000_000, bytes_accessed=1_500_000, transcendentals=0),
        name="project_late",
    )(high, low, total, across, far_next, far_near)

    def swap(block, apart):
        return lax.ppermute(block, "row", [(d, d ^ apart) for d in range(n)])

    mine = kept + swap(sent, 1)
    mine = pl.pallas_call(
        add_after,
        out_shape=piece,
        in_specs=[vmem] * 3,
        out_specs=vmem,
        compiler_params=params,
        name="add_after",
    )(mine, swap(mine, 3), done)
    apart = 4
    while apart < n:
        mine += swap(mine, apart + 1)
        apart *= 2
    reduced = pl.pallas_call(
        join,
        out_shape=jax.ShapeDtypeStruct((MODES, MODES), full),
        in_specs=[smem, vmem, vmem],
        out_specs=vmem,
        compiler_params=params,
        cost_estimate=pl.CostEstimate(flops=0, bytes_accessed=130_000, transcendentals=0),
        name="join",
    )(side, mine, swap(mine, 1))
    return (stiff_image, reduced)


def solution(mesh):
    in_specs = (
        P(("groups", "row"), None),
        P(("groups", "row")),
        P(("groups", "row"), None),
        P(("groups", "row")),
        P(("groups", "row"), None),
        P(("groups", "row")),
        P(("groups", "row")),
    )
    out_specs = (P(("groups", "row"), None), P("groups", None))
    return jax.shard_map(shards, mesh=mesh, in_specs=in_specs, out_specs=out_specs, check_vma=False)
```

```python
import functools

import jax
import jax.numpy as jnp
from jax import lax
from jax.experimental import pallas as pl
from jax.experimental.pallas import tpu as pltpu
from jax.sharding import PartitionSpec as P

B = 64
MODES = 128
BR_DEV = 4
CAP = 128
LINKS = 8
LATE = 3
HALF = B // 2
ROWS = BR_DEV * B


def split(x):
    high = x.astype(jnp.bfloat16)
    return high, (x - high.astype(jnp.float32)).astype(jnp.bfloat16)


def dot3(a_high, a_low, b_high, b_low):
    dot = functools.partial(jnp.dot, preferred_element_type=jnp.float32)
    return dot(a_high, b_high) + (dot(a_low, b_high) + dot(a_high, b_low))


def halves():
    for r in range(BR_DEV):
        for h in range(2):
            yield pl.ds(r * B + h, HALF, stride=2), slice(r * B + h * HALF, r * B + (h + 1) * HALF)


def prepare(basis_ref, held_ref):
    held_ref[...] = basis_ref[...]


def assemble(count_ref, rows_ref, owner_ref, offset_ref, blocks_ref, held_ref, high_ref, low_ref, again_ref, dense, placed, place, arrived):
    n, me = lax.axis_size("row"), lax.axis_index("row")
    away = lax.rem(owner_ref[...].reshape(1, CAP) - me + n, n)
    link = jnp.zeros_like(away)
    for k, step in enumerate(steps(n, me)):
        link = jnp.where(away == step, k, link)
    target = (link * BR_DEV + rows_ref[...].reshape(1, CAP)) * BR_DEV + offset_ref[...].reshape(1, CAP)
    slot = lax.broadcasted_iota(jnp.int32, (1, CAP), 1)
    placed[...] = jnp.where(slot < count_ref[0], target, CAP)
    copy = pltpu.make_async_copy(placed, place, arrived)
    copy.start()
    dense[...] = jnp.zeros_like(dense)
    again_ref[...] = held_ref[...]
    copy.wait()

    @pl.loop(0, CAP // 8)
    def _(group):
        for k in range(8):
            block = blocks_ref[pl.ds(group * (8 * HALF) + k, HALF, stride=8), :]
            target = pl.ds(pl.multiple_of(place[0, group * 8 + k] * HALF, HALF), HALF)
            dense[target, :] += block

    left = lax.broadcasted_iota(jnp.int32, (HALF, 128), 1) < B

    @pl.loop(0, LINKS)
    def _(link):
        for r in range(BR_DEV):
            for pair in range(BR_DEV // 2):
                start = ((link * BR_DEV + r) * BR_DEV + 2 * pair) * HALF
                first = dense[pl.ds(pl.multiple_of(start, HALF), HALF), :]
                second = dense[pl.ds(pl.multiple_of(start + HALF, HALF), HALF), :]
                even = jnp.where(left, first, pltpu.roll(second, B, 1))
                odd = jnp.where(left, pltpu.roll(first, B, 1), second)
                for h, part in enumerate((even, odd)):
                    high, low = split(part)
                    rows = slice(r * B + h * HALF, r * B + (h + 1) * HALF)
                    high_ref[link, rows, pair * 128:(pair + 1) * 128] = high
                    low_ref[link, rows, pair * 128:(pair + 1) * 128] = low


def project_early(high_ref, low_ref, springs_ref, *refs):
    basis_refs, (total_ref, partial_ref, weight_high_ref, weight_low_ref, sorted_rows) = refs[:-5], refs[-5:]
    own_ref = basis_refs[0]
    for rows, target in halves():
        sorted_rows[target, :] = own_ref[rows, :]
    turned_high, turned_low = split(sorted_rows[...].T)
    for k in range(LATE):
        link = LINKS - LATE + k
        high, low = split(dot3(turned_high, turned_low, high_ref[link], low_ref[link]))
        weight_high_ref[k] = high
        weight_low_ref[k] = low
    total = jnp.zeros((ROWS, MODES), jnp.float32)
    for link, ref in enumerate(basis_refs):
        b_high, b_low = split(ref[...])
        total += dot3(high_ref[link], low_ref[link], b_high, b_low)
    for part in range(ROWS // MODES):
        rows = slice(part * MODES, (part + 1) * MODES)
        column = jnp.broadcast_to(springs_ref[:, rows], (MODES, MODES)).T
        total_ref[rows, :] = column * own_ref[rows, :]
    for rows, target in halves():
        total_ref[rows, :] += total[target, :]
        sorted_rows[target, :] = total_ref[rows, :]
    partial_ref[...] = dot3(turned_high, turned_low, *split(sorted_rows[...]))


def reduce_late(scale, side_ref, weight_high_ref, weight_low_ref, early_ref, *refs):
    basis_refs, (kept_ref, sent_ref, partial) = refs[:LATE], refs[LATE:]
    total = early_ref[...]
    for k, ref in enumerate(basis_refs):
        total += dot3(weight_high_ref[k], weight_low_ref[k], *split(ref[...]))
    partial[...] = total * scale
    half = MODES // 2
    kept_ref[...] = partial[pl.ds(pl.multiple_of(side_ref[0] * half, half), half), :]
    sent_ref[...] = partial[pl.ds(pl.multiple_of((1 - side_ref[0]) * half, half), half), :]


def add_after(first_ref, second_ref, done_ref, sum_ref):
    sum_ref[...] = first_ref[...] + second_ref[...]


def join(side_ref, mine_ref, other_ref, whole_ref):
    half = MODES // 2
    whole_ref[pl.ds(pl.multiple_of(side_ref[0] * half, half), half), :] = mine_ref[...]
    whole_ref[pl.ds(pl.multiple_of((1 - side_ref[0]) * half, half), half), :] = other_ref[...]


def project_late(high_ref, low_ref, total_ref, *refs):
    basis_refs, (stiff_ref, done_ref) = refs[:LATE], refs[LATE:]
    total = jnp.zeros((ROWS, MODES), jnp.float32)
    for k, ref in enumerate(basis_refs):
        b_high, b_low = split(ref[...])
        total += dot3(high_ref[LINKS - LATE + k], low_ref[LINKS - LATE + k], b_high, b_low)
    for rows, target in halves():
        stiff_ref[rows, :] = total_ref[rows, :] + total[target, :]
    done_ref[...] = jnp.zeros_like(done_ref)


def steps(n, me):
    even, even_four = me % 2 == 0, (me // 4) % 2 == 0

    def one_of(first, when_first):
        return jnp.where(when_first, first, n - first)

    return (
        0,
        one_of(n - 4, even_four),
        one_of(4, even_four),
        one_of(1, even),
        one_of(n - 1, even),
        one_of(n - 5, even),
        n // 2,
        one_of(5, even),
    )


def pick(first_ref, second_ref, next_ref, outer_ref, near_ref):
    outer_ref[...] = first_ref[...]
    me = lax.axis_index("row")
    straight = (me % 2 == 1) == ((me // 4) % 2 == 0)

    @pl.when(straight)
    def _():
        near_ref[...] = second_ref[...]
        next_ref[...] = first_ref[...]

    @pl.when(jnp.logical_not(straight))
    def _():
        near_ref[...] = first_ref[...]
        next_ref[...] = second_ref[...]


def shards(basis, springs, tangent_blocks, tile_rows, tile_owner, tile_offset, tile_count):
    n = lax.axis_size("row")
    me = lax.axis_index("row")
    smem = pl.BlockSpec(memory_space=pltpu.SMEM)
    vmem = pl.BlockSpec(memory_space=pltpu.VMEM)
    half, full = jnp.bfloat16, jnp.float32
    params = pltpu.CompilerParams(vmem_limit_bytes=32 * 2**20)

    held = pl.pallas_call(
        prepare,
        out_shape=jax.ShapeDtypeStruct((ROWS, MODES), full),
        in_specs=[vmem],
        out_specs=vmem,
        compiler_params=params,
        cost_estimate=pl.CostEstimate(flops=10_000_000_000, bytes_accessed=300_000, transcendentals=0),
        name="prepare",
    )(basis)

    def trade(block, partner):
        return lax.ppermute(block, "row", [(d, partner(d) % n) for d in range(n)])

    def near(d):
        return d ^ 1

    def next_chip(d):
        return d + 1 if d % 2 else d - 1

    def outer(d):
        return d - 4 if d // 4 % 2 else d + 4

    def inner(d):
        return d + 4 if d // 4 % 2 else d - 4

    first = trade(basis, inner)
    second = trade(basis, outer)
    next_sent, outer_sent, near_sent = pl.pallas_call(
        pick,
        out_shape=(jax.ShapeDtypeStruct((ROWS, MODES), full),) * 3,
        in_specs=[vmem] * 2,
        out_specs=(vmem,) * 3,
        compiler_params=params,
        cost_estimate=pl.CostEstimate(flops=0, bytes_accessed=700_000, transcendentals=0),
        name="pick",
    )(first, second)
    across = trade(outer_sent, outer) if n == 16 else trade(held, lambda d: d + n // 2)
    far_next, far_near = trade(next_sent, next_chip), trade(near_sent, near)

    blocks = tangent_blocks.reshape(CAP // 8, 8, HALF, 128).transpose(0, 2, 1, 3).reshape(CAP * HALF, 128)
    high, low, again = pl.pallas_call(
        assemble,
        out_shape=(
            jax.ShapeDtypeStruct((LINKS, ROWS, ROWS), half),
            jax.ShapeDtypeStruct((LINKS, ROWS, ROWS), half),
            jax.ShapeDtypeStruct((ROWS, MODES), full),
        ),
        in_specs=[smem] + [vmem] * 5,
        out_specs=(vmem,) * 3,
        scratch_shapes=[
            pltpu.VMEM(((CAP + 1) * HALF, 128), full),
            pltpu.VMEM((1, CAP), jnp.int32),
            pltpu.SMEM((1, CAP), jnp.int32),
            pltpu.SemaphoreType.DMA(()),
        ],
        compiler_params=params,
        cost_estimate=pl.CostEstimate(flops=10_000_000, bytes_accessed=8_000_000, transcendentals=0),
        name="assemble",
    )(tile_count, tile_rows, tile_owner[:, 0], tile_offset, blocks, held)
    beside, beyond = trade(again, near), trade(again, next_chip)

    total, early, weight_high, weight_low = pl.pallas_call(
        project_early,
        out_shape=(
            jax.ShapeDtypeStruct((ROWS, MODES), full),
            jax.ShapeDtypeStruct((MODES, MODES), full),
            jax.ShapeDtypeStruct((LATE, MODES, ROWS), half),
            jax.ShapeDtypeStruct((LATE, MODES, ROWS), half),
        ),
        in_specs=[vmem] * (3 + LINKS - LATE),
        out_specs=(vmem,) * 4,
        scratch_shapes=[pltpu.VMEM((ROWS, MODES), full)],
        compiler_params=params,
        cost_estimate=pl.CostEstimate(flops=20_000_000_000, bytes_accessed=2_500_000, transcendentals=0),
        name="project_early",
    )(high, low, springs.reshape(1, ROWS), again, first, second, beside, beyond)

    side = me
    for shift in (8, 4, 2, 1):
        side = side ^ (side >> shift)
    side = (side & 1).reshape(1)
    piece = jax.ShapeDtypeStruct((MODES // 2, MODES), full)
    kept, sent = pl.pallas_call(
        functools.partial(reduce_late, 1.0 / (basis.shape[0] * n)),
        out_shape=(piece, piece),
        in_specs=[smem] + [vmem] * (3 + LATE),
        out_specs=(vmem,) * 2,
        scratch_shapes=[pltpu.VMEM((MODES, MODES), full)],
        compiler_params=params,
        cost_estimate=pl.CostEstimate(flops=80_000_000, bytes_accessed=700_000, transcendentals=0),
        name="reduce_late",
    )(side, weight_high, weight_low, early, far_next, across, far_near)

    stiff_image, done = pl.pallas_call(
        project_late,
        out_shape=(jax.ShapeDtypeStruct((ROWS, MODES), full), jax.ShapeDtypeStruct((8, 128), full)),
        in_specs=[vmem] * (3 + LATE),
        out_specs=(vmem,) * 2,
        compiler_params=params,
        cost_estimate=pl.CostEstimate(flops=160_000_000, bytes_accessed=1_500_000, transcendentals=0),
        name="project_late",
    )(high, low, total, far_next, across, far_near)

    def swap(block, apart):
        return lax.ppermute(block, "row", [(d, d ^ apart) for d in range(n)])

    mine = kept + swap(sent, 1)
    mine = pl.pallas_call(
        add_after,
        out_shape=piece,
        in_specs=[vmem] * 3,
        out_specs=vmem,
        compiler_params=params,
        name="add_after",
    )(mine, swap(mine, 3), done)
    apart = 4
    while apart < n:
        mine += swap(mine, apart + 1)
        apart *= 2
    reduced = pl.pallas_call(
        join,
        out_shape=jax.ShapeDtypeStruct((MODES, MODES), full),
        in_specs=[smem, vmem, vmem],
        out_specs=vmem,
        compiler_params=params,
        cost_estimate=pl.CostEstimate(flops=0, bytes_accessed=130_000, transcendentals=0),
        name="join",
    )(side, mine, swap(mine, 1))
    return (stiff_image, reduced)


def solution(mesh):
    in_specs = (
        P(("groups", "row"), None),
        P(("groups", "row")),
        P(("groups", "row"), None),
        P(("groups", "row")),
        P(("groups", "row"), None),
        P(("groups", "row")),
        P(("groups", "row")),
    )
    out_specs = (P(("groups", "row"), None), P("groups", None))
    return jax.shard_map(shards, mesh=mesh, in_specs=in_specs, out_specs=out_specs, check_vma=False)
```

```python
import functools

import jax
import jax.numpy as jnp
from jax import lax
from jax.experimental import pallas as pl
from jax.experimental.pallas import tpu as pltpu
from jax.sharding import PartitionSpec as P

B = 64
MODES = 128
BR_DEV = 4
CAP = 128
LINKS = 8
LATE = 3
HALF = B // 2
ROWS = BR_DEV * B


def split(x):
    high = x.astype(jnp.bfloat16)
    return high, (x - high.astype(jnp.float32)).astype(jnp.bfloat16)


def dot3(a_high, a_low, b_high, b_low):
    dot = functools.partial(jnp.dot, preferred_element_type=jnp.float32)
    return dot(a_high, b_high) + (dot(a_low, b_high) + dot(a_high, b_low))


def halves():
    for r in range(BR_DEV):
        for h in range(2):
            yield pl.ds(r * B + h, HALF, stride=2), slice(r * B + h * HALF, r * B + (h + 1) * HALF)


def prepare(token_ref):
    token_ref[...] = jnp.zeros_like(token_ref)


def assemble(count_ref, rows_ref, owner_ref, offset_ref, blocks_ref, basis_ref, token_ref, high_ref, low_ref, held_ref, dense, placed, place, arrived):
    n, me = lax.axis_size("row"), lax.axis_index("row")
    away = lax.rem(owner_ref[...].reshape(1, CAP) - me + n, n)
    link = jnp.zeros_like(away)
    for k, step in enumerate(steps(n, me)):
        link = jnp.where(away == step, k, link)
    target = (link * BR_DEV + rows_ref[...].reshape(1, CAP)) * BR_DEV + offset_ref[...].reshape(1, CAP)
    slot = lax.broadcasted_iota(jnp.int32, (1, CAP), 1)
    placed[...] = jnp.where(slot < count_ref[0], target, CAP)
    copy = pltpu.make_async_copy(placed, place, arrived)
    copy.start()
    dense[...] = jnp.zeros_like(dense)
    held_ref[...] = basis_ref[...]
    copy.wait()

    @pl.loop(0, CAP // 8)
    def _(group):
        for k in range(8):
            block = blocks_ref[pl.ds(group * (8 * HALF) + k, HALF, stride=8), :]
            target = pl.ds(pl.multiple_of(place[0, group * 8 + k] * HALF, HALF), HALF)
            dense[target, :] += block

    left = lax.broadcasted_iota(jnp.int32, (HALF, 128), 1) < B

    @pl.loop(0, LINKS)
    def _(link):
        for r in range(BR_DEV):
            for pair in range(BR_DEV // 2):
                start = ((link * BR_DEV + r) * BR_DEV + 2 * pair) * HALF
                first = dense[pl.ds(pl.multiple_of(start, HALF), HALF), :]
                second = dense[pl.ds(pl.multiple_of(start + HALF, HALF), HALF), :]
                even = jnp.where(left, first, pltpu.roll(second, B, 1))
                odd = jnp.where(left, pltpu.roll(first, B, 1), second)
                for h, part in enumerate((even, odd)):
                    high, low = split(part)
                    rows = slice(r * B + h * HALF, r * B + (h + 1) * HALF)
                    high_ref[link, rows, pair * 128:(pair + 1) * 128] = high
                    low_ref[link, rows, pair * 128:(pair + 1) * 128] = low


def project_early(high_ref, low_ref, springs_ref, *refs):
    basis_refs, (total_ref, partial_ref, weight_high_ref, weight_low_ref, sorted_rows) = refs[:-5], refs[-5:]
    own_ref = basis_refs[0]
    for rows, target in halves():
        sorted_rows[target, :] = own_ref[rows, :]
    turned_high, turned_low = split(sorted_rows[...].T)
    for k in range(LATE):
        link = LINKS - LATE + k
        high, low = split(dot3(turned_high, turned_low, high_ref[link], low_ref[link]))
        weight_high_ref[k] = high
        weight_low_ref[k] = low
    total = jnp.zeros((ROWS, MODES), jnp.float32)
    for link, ref in enumerate(basis_refs):
        b_high, b_low = split(ref[...])
        total += dot3(high_ref[link], low_ref[link], b_high, b_low)
    for part in range(ROWS // MODES):
        rows = slice(part * MODES, (part + 1) * MODES)
        column = jnp.broadcast_to(springs_ref[:, rows], (MODES, MODES)).T
        total_ref[rows, :] = column * own_ref[rows, :]
    for rows, target in halves():
        total_ref[rows, :] += total[target, :]
        sorted_rows[target, :] = total_ref[rows, :]
    partial_ref[...] = dot3(turned_high, turned_low, *split(sorted_rows[...]))


def reduce_late(scale, side_ref, weight_high_ref, weight_low_ref, early_ref, *refs):
    basis_refs, (kept_ref, sent_ref, partial) = refs[:LATE], refs[LATE:]
    total = early_ref[...]
    for k, ref in enumerate(basis_refs):
        total += dot3(weight_high_ref[k], weight_low_ref[k], *split(ref[...]))
    partial[...] = total * scale
    half = MODES // 2
    kept_ref[...] = partial[pl.ds(pl.multiple_of(side_ref[0] * half, half), half), :]
    sent_ref[...] = partial[pl.ds(pl.multiple_of((1 - side_ref[0]) * half, half), half), :]


def add_after(first_ref, second_ref, done_ref, sum_ref):
    sum_ref[...] = first_ref[...] + second_ref[...]


def join(side_ref, mine_ref, other_ref, whole_ref):
    half = MODES // 2
    whole_ref[pl.ds(pl.multiple_of(side_ref[0] * half, half), half), :] = mine_ref[...]
    whole_ref[pl.ds(pl.multiple_of((1 - side_ref[0]) * half, half), half), :] = other_ref[...]


def project_late(high_ref, low_ref, total_ref, *refs):
    basis_refs, (stiff_ref, done_ref) = refs[:LATE], refs[LATE:]
    total = jnp.zeros((ROWS, MODES), jnp.float32)
    for k, ref in enumerate(basis_refs):
        b_high, b_low = split(ref[...])
        total += dot3(high_ref[LINKS - LATE + k], low_ref[LINKS - LATE + k], b_high, b_low)
    for rows, target in halves():
        stiff_ref[rows, :] = total_ref[rows, :] + total[target, :]
    done_ref[...] = jnp.zeros_like(done_ref)


def steps(n, me):
    even, even_four = me % 2 == 0, (me // 4) % 2 == 0

    def one_of(first, when_first):
        return jnp.where(when_first, first, n - first)

    return (
        0,
        one_of(n - 4, even_four),
        one_of(4, even_four),
        one_of(1, even),
        one_of(n - 1, even),
        one_of(n - 5, even),
        n // 2,
        one_of(5, even),
    )


def pick(first_ref, second_ref, next_ref, outer_ref, near_ref):
    outer_ref[...] = first_ref[...]
    me = lax.axis_index("row")
    straight = (me % 2 == 1) == ((me // 4) % 2 == 0)

    @pl.when(straight)
    def _():
        near_ref[...] = second_ref[...]
        next_ref[...] = first_ref[...]

    @pl.when(jnp.logical_not(straight))
    def _():
        near_ref[...] = first_ref[...]
        next_ref[...] = second_ref[...]


def shards(basis, springs, tangent_blocks, tile_rows, tile_owner, tile_offset, tile_count):
    n = lax.axis_size("row")
    me = lax.axis_index("row")
    smem = pl.BlockSpec(memory_space=pltpu.SMEM)
    vmem = pl.BlockSpec(memory_space=pltpu.VMEM)
    half, full = jnp.bfloat16, jnp.float32
    params = pltpu.CompilerParams(vmem_limit_bytes=32 * 2**20)

    token = pl.pallas_call(
        prepare,
        out_shape=jax.ShapeDtypeStruct((8, 128), full),
        in_specs=[],
        out_specs=vmem,
        compiler_params=params,
        cost_estimate=pl.CostEstimate(flops=10_000_000_000, bytes_accessed=4_096, transcendentals=0),
        name="prepare",
    )()

    def trade(block, partner):
        return lax.ppermute(block, "row", [(d, partner(d) % n) for d in range(n)])

    def near(d):
        return d ^ 1

    def next_chip(d):
        return d + 1 if d % 2 else d - 1

    def outer(d):
        return d - 4 if d // 4 % 2 else d + 4

    def inner(d):
        return d + 4 if d // 4 % 2 else d - 4

    first = trade(basis, inner)
    second = trade(basis, outer)
    blocks = tangent_blocks.reshape(CAP // 8, 8, HALF, 128).transpose(0, 2, 1, 3).reshape(CAP * HALF, 128)
    high, low, held = pl.pallas_call(
        assemble,
        out_shape=(
            jax.ShapeDtypeStruct((LINKS, ROWS, ROWS), half),
            jax.ShapeDtypeStruct((LINKS, ROWS, ROWS), half),
            jax.ShapeDtypeStruct((ROWS, MODES), full),
        ),
        in_specs=[smem] + [vmem] * 6,
        out_specs=(vmem,) * 3,
        scratch_shapes=[
            pltpu.VMEM(((CAP + 1) * HALF, 128), full),
            pltpu.VMEM((1, CAP), jnp.int32),
            pltpu.SMEM((1, CAP), jnp.int32),
            pltpu.SemaphoreType.DMA(()),
        ],
        compiler_params=params,
        cost_estimate=pl.CostEstimate(flops=10_000_000, bytes_accessed=8_000_000, transcendentals=0),
        name="assemble",
    )(tile_count, tile_rows, tile_owner[:, 0], tile_offset, blocks, basis, token)
    beside, beyond = trade(held, near), trade(held, next_chip)

    next_sent, outer_sent, near_sent = pl.pallas_call(
        pick,
        out_shape=(jax.ShapeDtypeStruct((ROWS, MODES), full),) * 3,
        in_specs=[vmem] * 2,
        out_specs=(vmem,) * 3,
        compiler_params=params,
        cost_estimate=pl.CostEstimate(flops=0, bytes_accessed=700_000, transcendentals=0),
        name="pick",
    )(first, second)
    across = trade(outer_sent, outer) if n == 16 else trade(held, lambda d: d + n // 2)
    far_next, far_near = trade(next_sent, next_chip), trade(near_sent, near)

    total, early, weight_high, weight_low = pl.pallas_call(
        project_early,
        out_shape=(
            jax.ShapeDtypeStruct((ROWS, MODES), full),
            jax.ShapeDtypeStruct((MODES, MODES), full),
            jax.ShapeDtypeStruct((LATE, MODES, ROWS), half),
            jax.ShapeDtypeStruct((LATE, MODES, ROWS), half),
        ),
        in_specs=[vmem] * (3 + LINKS - LATE),
        out_specs=(vmem,) * 4,
        scratch_shapes=[pltpu.VMEM((ROWS, MODES), full)],
        compiler_params=params,
        cost_estimate=pl.CostEstimate(flops=20_000_000_000, bytes_accessed=2_500_000, transcendentals=0),
        name="project_early",
    )(high, low, springs.reshape(1, ROWS), held, first, second, beside, beyond)

    side = me
    for shift in (8, 4, 2, 1):
        side = side ^ (side >> shift)
    side = (side & 1).reshape(1)
    piece = jax.ShapeDtypeStruct((MODES // 2, MODES), full)
    kept, sent = pl.pallas_call(
        functools.partial(reduce_late, 1.0 / (basis.shape[0] * n)),
        out_shape=(piece, piece),
        in_specs=[smem] + [vmem] * (3 + LATE),
        out_specs=(vmem,) * 2,
        scratch_shapes=[pltpu.VMEM((MODES, MODES), full)],
        compiler_params=params,
        cost_estimate=pl.CostEstimate(flops=80_000_000, bytes_accessed=700_000, transcendentals=0),
        name="reduce_late",
    )(side, weight_high, weight_low, early, far_next, across, far_near)

    stiff_image, done = pl.pallas_call(
        project_late,
        out_shape=(jax.ShapeDtypeStruct((ROWS, MODES), full), jax.ShapeDtypeStruct((8, 128), full)),
        in_specs=[vmem] * (3 + LATE),
        out_specs=(vmem,) * 2,
        compiler_params=params,
        cost_estimate=pl.CostEstimate(flops=160_000_000, bytes_accessed=1_500_000, transcendentals=0),
        name="project_late",
    )(high, low, total, far_next, across, far_near)

    def swap(block, apart):
        return lax.ppermute(block, "row", [(d, d ^ apart) for d in range(n)])

    mine = kept + swap(sent, 1)
    mine = pl.pallas_call(
        add_after,
        out_shape=piece,
        in_specs=[vmem] * 3,
        out_specs=vmem,
        compiler_params=params,
        name="add_after",
    )(mine, swap(mine, 3), done)
    apart = 4
    while apart < n:
        mine += swap(mine, apart + 1)
        apart *= 2
    reduced = pl.pallas_call(
        join,
        out_shape=jax.ShapeDtypeStruct((MODES, MODES), full),
        in_specs=[smem, vmem, vmem],
        out_specs=vmem,
        compiler_params=params,
        cost_estimate=pl.CostEstimate(flops=0, bytes_accessed=130_000, transcendentals=0),
        name="join",
    )(side, mine, swap(mine, 1))
    return (stiff_image, reduced)


def solution(mesh):
    in_specs = (
        P(("groups", "row"), None),
        P(("groups", "row")),
        P(("groups", "row"), None),
        P(("groups", "row")),
        P(("groups", "row"), None),
        P(("groups", "row")),
        P(("groups", "row")),
    )
    out_specs = (P(("groups", "row"), None), P("groups", None))
    return jax.shard_map(shards, mesh=mesh, in_specs=in_specs, out_specs=out_specs, check_vma=False)
```

```python
import functools

import jax
import jax.numpy as jnp
from jax import lax
from jax.experimental import pallas as pl
from jax.experimental.pallas import tpu as pltpu
from jax.sharding import PartitionSpec as P

B = 64
MODES = 128
BR_DEV = 4
CAP = 128
LINKS = 8
LATE = 3
HALF = B // 2
ROWS = BR_DEV * B


def split(x):
    high = x.astype(jnp.bfloat16)
    return high, (x - high.astype(jnp.float32)).astype(jnp.bfloat16)


def dot3(a_high, a_low, b_high, b_low):
    dot = functools.partial(jnp.dot, preferred_element_type=jnp.float32)
    return dot(a_high, b_high) + (dot(a_low, b_high) + dot(a_high, b_low))


def halves():
    for r in range(BR_DEV):
        for h in range(2):
            yield pl.ds(r * B + h, HALF, stride=2), slice(r * B + h * HALF, r * B + (h + 1) * HALF)


def prepare(token_ref):
    token_ref[...] = jnp.zeros_like(token_ref)


def assemble(count_ref, rows_ref, owner_ref, offset_ref, blocks_ref, basis_ref, token_ref, high_ref, low_ref, held_ref, dense, placed, place, arrived):
    n, me = lax.axis_size("row"), lax.axis_index("row")
    away = lax.rem(owner_ref[...].reshape(1, CAP) - me + n, n)
    link = jnp.zeros_like(away)
    for k, step in enumerate(steps(n, me)):
        link = jnp.where(away == step, k, link)
    target = (link * BR_DEV + rows_ref[...].reshape(1, CAP)) * BR_DEV + offset_ref[...].reshape(1, CAP)
    slot = lax.broadcasted_iota(jnp.int32, (1, CAP), 1)
    placed[...] = jnp.where(slot < count_ref[0], target, CAP)
    copy = pltpu.make_async_copy(placed, place, arrived)
    copy.start()
    dense[...] = jnp.zeros_like(dense)
    held_ref[...] = basis_ref[...]
    copy.wait()

    @pl.loop(0, CAP // 8)
    def _(group):
        for k in range(8):
            block = blocks_ref[pl.ds(group * (8 * HALF) + k, HALF, stride=8), :]
            target = pl.ds(pl.multiple_of(place[0, group * 8 + k] * HALF, HALF), HALF)
            dense[target, :] += block

    left = lax.broadcasted_iota(jnp.int32, (HALF, 128), 1) < B

    @pl.loop(0, LINKS)
    def _(link):
        for r in range(BR_DEV):
            for pair in range(BR_DEV // 2):
                start = ((link * BR_DEV + r) * BR_DEV + 2 * pair) * HALF
                first = dense[pl.ds(pl.multiple_of(start, HALF), HALF), :]
                second = dense[pl.ds(pl.multiple_of(start + HALF, HALF), HALF), :]
                even = jnp.where(left, first, pltpu.roll(second, B, 1))
                odd = jnp.where(left, pltpu.roll(first, B, 1), second)
                for h, part in enumerate((even, odd)):
                    high, low = split(part)
                    rows = slice(r * B + h * HALF, r * B + (h + 1) * HALF)
                    high_ref[link, rows, pair * 128:(pair + 1) * 128] = high
                    low_ref[link, rows, pair * 128:(pair + 1) * 128] = low


def project_early(high_ref, low_ref, springs_ref, *refs):
    basis_refs, (total_ref, partial_ref, weight_high_ref, weight_low_ref, sorted_rows) = refs[:-5], refs[-5:]
    own_ref = basis_refs[0]
    for rows, target in halves():
        sorted_rows[target, :] = own_ref[rows, :]
    turned_high, turned_low = split(sorted_rows[...].T)
    for k in range(LATE):
        link = LINKS - LATE + k
        high, low = split(dot3(turned_high, turned_low, high_ref[link], low_ref[link]))
        weight_high_ref[k] = high
        weight_low_ref[k] = low
    total = jnp.zeros((ROWS, MODES), jnp.float32)
    for link, ref in enumerate(basis_refs):
        b_high, b_low = split(ref[...])
        total += dot3(high_ref[link], low_ref[link], b_high, b_low)
    for part in range(ROWS // MODES):
        rows = slice(part * MODES, (part + 1) * MODES)
        column = jnp.broadcast_to(springs_ref[:, rows], (MODES, MODES)).T
        total_ref[rows, :] = column * own_ref[rows, :]
    for rows, target in halves():
        total_ref[rows, :] += total[target, :]
        sorted_rows[target, :] = total_ref[rows, :]
    partial_ref[...] = dot3(turned_high, turned_low, *split(sorted_rows[...]))


def reduce_late(scale, side_ref, weight_high_ref, weight_low_ref, early_ref, *refs):
    basis_refs, (kept_ref, sent_ref, partial) = refs[:LATE], refs[LATE:]
    total = early_ref[...]
    for k, ref in enumerate(basis_refs):
        total += dot3(weight_high_ref[k], weight_low_ref[k], *split(ref[...]))
    partial[...] = total * scale
    half = MODES // 2
    kept_ref[...] = partial[pl.ds(pl.multiple_of(side_ref[0] * half, half), half), :]
    sent_ref[...] = partial[pl.ds(pl.multiple_of((1 - side_ref[0]) * half, half), half), :]


def add_after(first_ref, second_ref, done_ref, sum_ref):
    sum_ref[...] = first_ref[...] + second_ref[...]


def join(side_ref, mine_ref, other_ref, whole_ref):
    half = MODES // 2
    whole_ref[pl.ds(pl.multiple_of(side_ref[0] * half, half), half), :] = mine_ref[...]
    whole_ref[pl.ds(pl.multiple_of((1 - side_ref[0]) * half, half), half), :] = other_ref[...]


def project_late(high_ref, low_ref, total_ref, *refs):
    basis_refs, (stiff_ref, done_ref) = refs[:LATE], refs[LATE:]
    total = jnp.zeros((ROWS, MODES), jnp.float32)
    for k, ref in enumerate(basis_refs):
        b_high, b_low = split(ref[...])
        total += dot3(high_ref[LINKS - LATE + k], low_ref[LINKS - LATE + k], b_high, b_low)
    for rows, target in halves():
        stiff_ref[rows, :] = total_ref[rows, :] + total[target, :]
    done_ref[...] = jnp.zeros_like(done_ref)


def steps(n, me):
    even, even_four = me % 2 == 0, (me // 4) % 2 == 0

    def one_of(first, when_first):
        return jnp.where(when_first, first, n - first)

    return (
        0,
        one_of(n - 4, even_four),
        one_of(4, even_four),
        one_of(1, even),
        one_of(n - 1, even),
        one_of(n - 5, even),
        n // 2,
        one_of(5, even),
    )


def pick(short, first_ref, second_ref, next_ref, outer_ref, near_ref):
    outer_ref[...] = first_ref[...]
    me = lax.axis_index("row")
    straight = (me % 2 == 1) == ((me // 4) % 2 == 0)

    near_ref[...] = jnp.where(straight, second_ref[...], first_ref[...])
    if short:
        straight = jnp.logical_or(straight, jnp.logical_or(me % 4 == 0, me % 4 == 3))
    next_ref[...] = jnp.where(straight, first_ref[...], second_ref[...])


def shards(basis, springs, tangent_blocks, tile_rows, tile_owner, tile_offset, tile_count):
    n = lax.axis_size("row")
    me = lax.axis_index("row")
    smem = pl.BlockSpec(memory_space=pltpu.SMEM)
    vmem = pl.BlockSpec(memory_space=pltpu.VMEM)
    half, full = jnp.bfloat16, jnp.float32
    params = pltpu.CompilerParams(vmem_limit_bytes=32 * 2**20)

    token = pl.pallas_call(
        prepare,
        out_shape=jax.ShapeDtypeStruct((8, 128), full),
        in_specs=[],
        out_specs=vmem,
        compiler_params=params,
        cost_estimate=pl.CostEstimate(flops=10_000_000_000, bytes_accessed=4_096, transcendentals=0),
        name="prepare",
    )()

    def trade(block, partner):
        return lax.ppermute(block, "row", [(d, partner(d) % n) for d in range(n)])

    def near(d):
        return d ^ 1

    def next_chip(d):
        return d + 1 if d % 2 else d - 1

    def outer(d):
        return d - 4 if d // 4 % 2 else d + 4

    def inner(d):
        return d + 4 if d // 4 % 2 else d - 4

    first = trade(basis, inner)
    second = trade(basis, outer)
    blocks = tangent_blocks.reshape(CAP // 8, 8, HALF, 128).transpose(0, 2, 1, 3).reshape(CAP * HALF, 128)
    high, low, held = pl.pallas_call(
        assemble,
        out_shape=(
            jax.ShapeDtypeStruct((LINKS, ROWS, ROWS), half),
            jax.ShapeDtypeStruct((LINKS, ROWS, ROWS), half),
            jax.ShapeDtypeStruct((ROWS, MODES), full),
        ),
        in_specs=[smem] + [vmem] * 6,
        out_specs=(vmem,) * 3,
        scratch_shapes=[
            pltpu.VMEM(((CAP + 1) * HALF, 128), full),
            pltpu.VMEM((1, CAP), jnp.int32),
            pltpu.SMEM((1, CAP), jnp.int32),
            pltpu.SemaphoreType.DMA(()),
        ],
        compiler_params=params,
        cost_estimate=pl.CostEstimate(flops=10_000_000, bytes_accessed=8_000_000, transcendentals=0),
        name="assemble",
    )(tile_count, tile_rows, tile_owner[:, 0], tile_offset, blocks, basis, token)
    beside, beyond = trade(held, near), trade(held, next_chip)

    next_sent, outer_sent, near_sent = pl.pallas_call(
        functools.partial(pick, n == 16),
        out_shape=(jax.ShapeDtypeStruct((ROWS, MODES), full),) * 3,
        in_specs=[vmem] * 2,
        out_specs=(vmem,) * 3,
        compiler_params=params,
        cost_estimate=pl.CostEstimate(flops=0, bytes_accessed=700_000, transcendentals=0),
        name="pick",
    )(first, second)
    if n == 16:
        across = trade(outer_sent, outer)
        far_next = trade(next_sent, lambda d: {0: 7, 7: 0, 8: 15, 15: 8}.get(d, next_chip(d)))
    else:
        across = trade(held, lambda d: d + n // 2)
        far_next = trade(next_sent, next_chip)
    far_near = trade(near_sent, near)

    total, early, weight_high, weight_low = pl.pallas_call(
        project_early,
        out_shape=(
            jax.ShapeDtypeStruct((ROWS, MODES), full),
            jax.ShapeDtypeStruct((MODES, MODES), full),
            jax.ShapeDtypeStruct((LATE, MODES, ROWS), half),
            jax.ShapeDtypeStruct((LATE, MODES, ROWS), half),
        ),
        in_specs=[vmem] * (3 + LINKS - LATE),
        out_specs=(vmem,) * 4,
        scratch_shapes=[pltpu.VMEM((ROWS, MODES), full)],
        compiler_params=params,
        cost_estimate=pl.CostEstimate(flops=20_000_000_000, bytes_accessed=2_500_000, transcendentals=0),
        name="project_early",
    )(high, low, springs.reshape(1, ROWS), held, first, second, beside, beyond)

    side = me
    for shift in (8, 4, 2, 1):
        side = side ^ (side >> shift)
    side = (side & 1).reshape(1)
    piece = jax.ShapeDtypeStruct((MODES // 2, MODES), full)
    kept, sent = pl.pallas_call(
        functools.partial(reduce_late, 1.0 / (basis.shape[0] * n)),
        out_shape=(piece, piece),
        in_specs=[smem] + [vmem] * (3 + LATE),
        out_specs=(vmem,) * 2,
        scratch_shapes=[pltpu.VMEM((MODES, MODES), full)],
        compiler_params=params,
        cost_estimate=pl.CostEstimate(flops=80_000_000, bytes_accessed=700_000, transcendentals=0),
        name="reduce_late",
    )(side, weight_high, weight_low, early, far_next, across, far_near)

    stiff_image, done = pl.pallas_call(
        project_late,
        out_shape=(jax.ShapeDtypeStruct((ROWS, MODES), full), jax.ShapeDtypeStruct((8, 128), full)),
        in_specs=[vmem] * (3 + LATE),
        out_specs=(vmem,) * 2,
        compiler_params=params,
        cost_estimate=pl.CostEstimate(flops=160_000_000, bytes_accessed=1_500_000, transcendentals=0),
        name="project_late",
    )(high, low, total, far_next, across, far_near)

    def swap(block, apart):
        return lax.ppermute(block, "row", [(d, d ^ apart) for d in range(n)])

    mine = kept + swap(sent, 1)
    mine = pl.pallas_call(
        add_after,
        out_shape=piece,
        in_specs=[vmem] * 3,
        out_specs=vmem,
        compiler_params=params,
        name="add_after",
    )(mine, swap(mine, 3), done)
    apart = 4
    while apart < n:
        mine += swap(mine, apart + 1)
        apart *= 2
    reduced = pl.pallas_call(
        join,
        out_shape=jax.ShapeDtypeStruct((MODES, MODES), full),
        in_specs=[smem, vmem, vmem],
        out_specs=vmem,
        compiler_params=params,
        cost_estimate=pl.CostEstimate(flops=0, bytes_accessed=130_000, transcendentals=0),
        name="join",
    )(side, mine, swap(mine, 1))
    return (stiff_image, reduced)


def solution(mesh):
    in_specs = (
        P(("groups", "row"), None),
        P(("groups", "row")),
        P(("groups", "row"), None),
        P(("groups", "row")),
        P(("groups", "row"), None),
        P(("groups", "row")),
        P(("groups", "row")),
    )
    out_specs = (P(("groups", "row"), None), P("groups", None))
    return jax.shard_map(shards, mesh=mesh, in_specs=in_specs, out_specs=out_specs, check_vma=False)
```

```python
import functools

import jax
import jax.numpy as jnp
from jax import lax
from jax.experimental import pallas as pl
from jax.experimental.pallas import tpu as pltpu
from jax.sharding import PartitionSpec as P

B = 64
MODES = 128
BR_DEV = 4
CAP = 128
LINKS = 8
LATE = 3
HALF = B // 2
ROWS = BR_DEV * B


def split(x):
    high = x.astype(jnp.bfloat16)
    return high, (x - high.astype(jnp.float32)).astype(jnp.bfloat16)


def dot3(a_high, a_low, b_high, b_low):
    dot = functools.partial(jnp.dot, preferred_element_type=jnp.float32)
    return dot(a_high, b_high) + (dot(a_low, b_high) + dot(a_high, b_low))


def halves():
    for r in range(BR_DEV):
        for h in range(2):
            yield pl.ds(r * B + h, HALF, stride=2), slice(r * B + h * HALF, r * B + (h + 1) * HALF)


def prepare(token_ref):
    token_ref[...] = jnp.zeros_like(token_ref)


def assemble(count_ref, rows_ref, owner_ref, offset_ref, blocks_ref, basis_ref, token_ref, high_ref, low_ref, held_ref, dense, placed, place, arrived):
    n, me = lax.axis_size("row"), lax.axis_index("row")
    away = lax.rem(owner_ref[...].reshape(1, CAP) - me + n, n)
    link = jnp.zeros_like(away)
    for k, step in enumerate(steps(n, me)):
        link = jnp.where(away == step, k, link)
    target = (link * BR_DEV + rows_ref[...].reshape(1, CAP)) * BR_DEV + offset_ref[...].reshape(1, CAP)
    slot = lax.broadcasted_iota(jnp.int32, (1, CAP), 1)
    placed[...] = jnp.where(slot < count_ref[0], target, CAP)
    copy = pltpu.make_async_copy(placed, place, arrived)
    copy.start()
    dense[...] = jnp.zeros_like(dense)
    held_ref[...] = basis_ref[...]
    copy.wait()

    @pl.loop(0, CAP // 8)
    def _(group):
        for k in range(8):
            block = blocks_ref[pl.ds(group * (8 * HALF) + k, HALF, stride=8), :]
            target = pl.ds(pl.multiple_of(place[0, group * 8 + k] * HALF, HALF), HALF)
            dense[target, :] += block

    left = lax.broadcasted_iota(jnp.int32, (HALF, 128), 1) < B

    @pl.loop(0, LINKS)
    def _(link):
        for r in range(BR_DEV):
            for pair in range(BR_DEV // 2):
                start = ((link * BR_DEV + r) * BR_DEV + 2 * pair) * HALF
                first = dense[pl.ds(pl.multiple_of(start, HALF), HALF), :]
                second = dense[pl.ds(pl.multiple_of(start + HALF, HALF), HALF), :]
                even = jnp.where(left, first, pltpu.roll(second, B, 1))
                odd = jnp.where(left, pltpu.roll(first, B, 1), second)
                for h, part in enumerate((even, odd)):
                    high, low = split(part)
                    rows = slice(r * B + h * HALF, r * B + (h + 1) * HALF)
                    high_ref[link, rows, pair * 128:(pair + 1) * 128] = high
                    low_ref[link, rows, pair * 128:(pair + 1) * 128] = low


def project_early(high_ref, low_ref, springs_ref, *refs):
    basis_refs, (total_ref, partial_ref, weight_high_ref, weight_low_ref, sorted_rows) = refs[:-5], refs[-5:]
    own_ref = basis_refs[0]
    for rows, target in halves():
        sorted_rows[target, :] = own_ref[rows, :]
    turned_high, turned_low = split(sorted_rows[...].T)
    for k in range(LATE):
        link = LINKS - LATE + k
        high, low = split(dot3(turned_high, turned_low, high_ref[link], low_ref[link]))
        weight_high_ref[k] = high
        weight_low_ref[k] = low
    total = jnp.zeros((ROWS, MODES), jnp.float32)
    for link, ref in enumerate(basis_refs):
        b_high, b_low = split(ref[...])
        total += dot3(high_ref[link], low_ref[link], b_high, b_low)
    for part in range(ROWS // MODES):
        rows = slice(part * MODES, (part + 1) * MODES)
        column = jnp.broadcast_to(springs_ref[:, rows], (MODES, MODES)).T
        total_ref[rows, :] = column * own_ref[rows, :]
    for rows, target in halves():
        total_ref[rows, :] += total[target, :]
        sorted_rows[target, :] = total_ref[rows, :]
    partial_ref[...] = dot3(turned_high, turned_low, *split(sorted_rows[...]))


def reduce_late(scale, side_ref, weight_high_ref, weight_low_ref, early_ref, *refs):
    basis_refs, (kept_ref, sent_ref, partial) = refs[:LATE], refs[LATE:]
    total = early_ref[...]
    for k, ref in enumerate(basis_refs):
        total += dot3(weight_high_ref[k], weight_low_ref[k], *split(ref[...]))
    partial[...] = total * scale
    half = MODES // 2
    kept_ref[...] = partial[pl.ds(pl.multiple_of(side_ref[0] * half, half), half), :]
    sent_ref[...] = partial[pl.ds(pl.multiple_of((1 - side_ref[0]) * half, half), half), :]


def add_after(first_ref, second_ref, done_ref, sum_ref):
    sum_ref[...] = first_ref[...] + second_ref[...]


def join(side_ref, mine_ref, other_ref, whole_ref):
    half = MODES // 2
    whole_ref[pl.ds(pl.multiple_of(side_ref[0] * half, half), half), :] = mine_ref[...]
    whole_ref[pl.ds(pl.multiple_of((1 - side_ref[0]) * half, half), half), :] = other_ref[...]


def project_late(high_ref, low_ref, total_ref, *refs):
    basis_refs, (stiff_ref, done_ref) = refs[:LATE], refs[LATE:]
    total = jnp.zeros((ROWS, MODES), jnp.float32)
    for k, ref in enumerate(basis_refs):
        b_high, b_low = split(ref[...])
        total += dot3(high_ref[LINKS - LATE + k], low_ref[LINKS - LATE + k], b_high, b_low)
    for rows, target in halves():
        stiff_ref[rows, :] = total_ref[rows, :] + total[target, :]
    done_ref[...] = jnp.zeros_like(done_ref)


def steps(n, me):
    even, even_four = me % 2 == 0, (me // 4) % 2 == 0

    def one_of(first, when_first):
        return jnp.where(when_first, first, n - first)

    return (
        0,
        one_of(n - 4, even_four),
        one_of(4, even_four),
        one_of(1, even),
        one_of(n - 1, even),
        n // 2,
        one_of(n - 5, even),
        one_of(5, even),
    )


def pick(short, first_ref, second_ref, outer_ref, next_ref, near_ref):
    outer_ref[...] = first_ref[...]
    me = lax.axis_index("row")
    straight = (me % 2 == 1) == ((me // 4) % 2 == 0)

    near_ref[...] = jnp.where(straight, second_ref[...], first_ref[...])
    if short:
        straight = jnp.logical_or(straight, jnp.logical_or(me % 4 == 0, me % 4 == 3))
    next_ref[...] = jnp.where(straight, first_ref[...], second_ref[...])


def shards(basis, springs, tangent_blocks, tile_rows, tile_owner, tile_offset, tile_count):
    n = lax.axis_size("row")
    me = lax.axis_index("row")
    smem = pl.BlockSpec(memory_space=pltpu.SMEM)
    vmem = pl.BlockSpec(memory_space=pltpu.VMEM)
    half, full = jnp.bfloat16, jnp.float32
    params = pltpu.CompilerParams(vmem_limit_bytes=32 * 2**20)

    token = pl.pallas_call(
        prepare,
        out_shape=jax.ShapeDtypeStruct((8, 128), full),
        in_specs=[],
        out_specs=vmem,
        compiler_params=params,
        cost_estimate=pl.CostEstimate(flops=10_000_000_000, bytes_accessed=4_096, transcendentals=0),
        name="prepare",
    )()

    def trade(block, partner):
        return lax.ppermute(block, "row", [(d, partner(d) % n) for d in range(n)])

    def near(d):
        return d ^ 1

    def next_chip(d):
        return d + 1 if d % 2 else d - 1

    def outer(d):
        return d - 4 if d // 4 % 2 else d + 4

    def inner(d):
        return d + 4 if d // 4 % 2 else d - 4

    first = trade(basis, inner)
    second = trade(basis, outer)
    blocks = tangent_blocks.reshape(CAP // 8, 8, HALF, 128).transpose(0, 2, 1, 3).reshape(CAP * HALF, 128)
    high, low, held = pl.pallas_call(
        assemble,
        out_shape=(
            jax.ShapeDtypeStruct((LINKS, ROWS, ROWS), half),
            jax.ShapeDtypeStruct((LINKS, ROWS, ROWS), half),
            jax.ShapeDtypeStruct((ROWS, MODES), full),
        ),
        in_specs=[smem] + [vmem] * 6,
        out_specs=(vmem,) * 3,
        scratch_shapes=[
            pltpu.VMEM(((CAP + 1) * HALF, 128), full),
            pltpu.VMEM((1, CAP), jnp.int32),
            pltpu.SMEM((1, CAP), jnp.int32),
            pltpu.SemaphoreType.DMA(()),
        ],
        compiler_params=params,
        cost_estimate=pl.CostEstimate(flops=10_000_000, bytes_accessed=8_000_000, transcendentals=0),
        name="assemble",
    )(tile_count, tile_rows, tile_owner[:, 0], tile_offset, blocks, basis, token)
    beside, beyond = trade(held, near), trade(held, next_chip)

    outer_sent, next_sent, near_sent = pl.pallas_call(
        functools.partial(pick, n == 16),
        out_shape=(jax.ShapeDtypeStruct((ROWS, MODES), full),) * 3,
        in_specs=[vmem] * 2,
        out_specs=(vmem,) * 3,
        compiler_params=params,
        cost_estimate=pl.CostEstimate(flops=0, bytes_accessed=700_000, transcendentals=0),
        name="pick",
    )(first, second)
    if n == 16:
        across = trade(outer_sent, outer)
        far_next = trade(next_sent, lambda d: {0: 7, 7: 0, 8: 15, 15: 8}.get(d, next_chip(d)))
    else:
        across = trade(held, lambda d: d + n // 2)
        far_next = trade(next_sent, next_chip)
    far_near = trade(near_sent, near)

    total, early, weight_high, weight_low = pl.pallas_call(
        project_early,
        out_shape=(
            jax.ShapeDtypeStruct((ROWS, MODES), full),
            jax.ShapeDtypeStruct((MODES, MODES), full),
            jax.ShapeDtypeStruct((LATE, MODES, ROWS), half),
            jax.ShapeDtypeStruct((LATE, MODES, ROWS), half),
        ),
        in_specs=[vmem] * (3 + LINKS - LATE),
        out_specs=(vmem,) * 4,
        scratch_shapes=[pltpu.VMEM((ROWS, MODES), full)],
        compiler_params=params,
        cost_estimate=pl.CostEstimate(flops=20_000_000_000, bytes_accessed=2_500_000, transcendentals=0),
        name="project_early",
    )(high, low, springs.reshape(1, ROWS), held, first, second, beside, beyond)

    side = me
    for shift in (8, 4, 2, 1):
        side = side ^ (side >> shift)
    side = (side & 1).reshape(1)
    piece = jax.ShapeDtypeStruct((MODES // 2, MODES), full)
    kept, sent = pl.pallas_call(
        functools.partial(reduce_late, 1.0 / (basis.shape[0] * n)),
        out_shape=(piece, piece),
        in_specs=[smem] + [vmem] * (3 + LATE),
        out_specs=(vmem,) * 2,
        scratch_shapes=[pltpu.VMEM((MODES, MODES), full)],
        compiler_params=params,
        cost_estimate=pl.CostEstimate(flops=80_000_000, bytes_accessed=700_000, transcendentals=0),
        name="reduce_late",
    )(side, weight_high, weight_low, early, across, far_next, far_near)

    stiff_image, done = pl.pallas_call(
        project_late,
        out_shape=(jax.ShapeDtypeStruct((ROWS, MODES), full), jax.ShapeDtypeStruct((8, 128), full)),
        in_specs=[vmem] * (3 + LATE),
        out_specs=(vmem,) * 2,
        compiler_params=params,
        cost_estimate=pl.CostEstimate(flops=160_000_000, bytes_accessed=1_500_000, transcendentals=0),
        name="project_late",
    )(high, low, total, across, far_next, far_near)

    def swap(block, apart):
        return lax.ppermute(block, "row", [(d, d ^ apart) for d in range(n)])

    mine = kept + swap(sent, 1)
    mine = pl.pallas_call(
        add_after,
        out_shape=piece,
        in_specs=[vmem] * 3,
        out_specs=vmem,
        compiler_params=params,
        name="add_after",
    )(mine, swap(mine, 3), done)
    apart = 4
    while apart < n:
        mine += swap(mine, apart + 1)
        apart *= 2
    reduced = pl.pallas_call(
        join,
        out_shape=jax.ShapeDtypeStruct((MODES, MODES), full),
        in_specs=[smem, vmem, vmem],
        out_specs=vmem,
        compiler_params=params,
        cost_estimate=pl.CostEstimate(flops=0, bytes_accessed=130_000, transcendentals=0),
        name="join",
    )(side, mine, swap(mine, 1))
    return (stiff_image, reduced)


def solution(mesh):
    in_specs = (
        P(("groups", "row"), None),
        P(("groups", "row")),
        P(("groups", "row"), None),
        P(("groups", "row")),
        P(("groups", "row"), None),
        P(("groups", "row")),
        P(("groups", "row")),
    )
    out_specs = (P(("groups", "row"), None), P("groups", None))
    return jax.shard_map(shards, mesh=mesh, in_specs=in_specs, out_specs=out_specs, check_vma=False)
```

```python
import functools

import jax
import jax.numpy as jnp
from jax import lax
from jax.experimental import pallas as pl
from jax.experimental.pallas import tpu as pltpu
from jax.sharding import PartitionSpec as P

B = 64
MODES = 128
BR_DEV = 4
CAP = 128
LINKS = 8
LATE = 3
HALF = B // 2
ROWS = BR_DEV * B


def split(x):
    high = x.astype(jnp.bfloat16)
    return high, (x - high.astype(jnp.float32)).astype(jnp.bfloat16)


def dot3(a_high, a_low, b_high, b_low):
    dot = functools.partial(jnp.dot, preferred_element_type=jnp.float32)
    return dot(a_high, b_high) + (dot(a_low, b_high) + dot(a_high, b_low))


def halves():
    for r in range(BR_DEV):
        for h in range(2):
            yield pl.ds(r * B + h, HALF, stride=2), slice(r * B + h * HALF, r * B + (h + 1) * HALF)


def prepare(token_ref):
    token_ref[...] = jnp.zeros_like(token_ref)


def assemble(count_ref, rows_ref, owner_ref, offset_ref, blocks_ref, basis_ref, token_ref, high_ref, low_ref, held_ref, dense, placed, place, arrived):
    n, me = lax.axis_size("row"), lax.axis_index("row")
    away = lax.rem(owner_ref[...].reshape(1, CAP) - me + n, n)
    link = jnp.zeros_like(away)
    for k, step in enumerate(steps(n, me)):
        link = jnp.where(away == step, k, link)
    target = (link * BR_DEV + rows_ref[...].reshape(1, CAP)) * BR_DEV + offset_ref[...].reshape(1, CAP)
    slot = lax.broadcasted_iota(jnp.int32, (1, CAP), 1)
    placed[...] = jnp.where(slot < count_ref[0], target, CAP)
    copy = pltpu.make_async_copy(placed, place, arrived)
    copy.start()
    dense[...] = jnp.zeros_like(dense)
    held_ref[...] = basis_ref[...]
    copy.wait()

    @pl.loop(0, CAP // 8)
    def _(group):
        for k in range(8):
            block = blocks_ref[pl.ds(group * (8 * HALF) + k, HALF, stride=8), :]
            target = pl.ds(pl.multiple_of(place[0, group * 8 + k] * HALF, HALF), HALF)
            dense[target, :] += block

    left = lax.broadcasted_iota(jnp.int32, (HALF, 128), 1) < B

    @pl.loop(0, LINKS)
    def _(link):
        for r in range(BR_DEV):
            for pair in range(BR_DEV // 2):
                start = ((link * BR_DEV + r) * BR_DEV + 2 * pair) * HALF
                first = dense[pl.ds(pl.multiple_of(start, HALF), HALF), :]
                second = dense[pl.ds(pl.multiple_of(start + HALF, HALF), HALF), :]
                even = jnp.where(left, first, pltpu.roll(second, B, 1))
                odd = jnp.where(left, pltpu.roll(first, B, 1), second)
                for h, part in enumerate((even, odd)):
                    high, low = split(part)
                    rows = slice(r * B + h * HALF, r * B + (h + 1) * HALF)
                    high_ref[link, rows, pair * 128:(pair + 1) * 128] = high
                    low_ref[link, rows, pair * 128:(pair + 1) * 128] = low


def project_early(high_ref, low_ref, springs_ref, *refs):
    basis_refs, (total_ref, partial_ref, weight_high_ref, weight_low_ref, sorted_rows) = refs[:-5], refs[-5:]
    own_ref = basis_refs[0]
    for rows, target in halves():
        sorted_rows[target, :] = own_ref[rows, :]
    turned_high, turned_low = split(sorted_rows[...].T)
    for k in range(LATE):
        link = LINKS - LATE + k
        high, low = split(dot3(turned_high, turned_low, high_ref[link], low_ref[link]))
        weight_high_ref[k] = high
        weight_low_ref[k] = low
    total = jnp.zeros((ROWS, MODES), jnp.float32)
    for link, ref in enumerate(basis_refs):
        b_high, b_low = split(ref[...])
        total += dot3(high_ref[link], low_ref[link], b_high, b_low)
    for part in range(ROWS // MODES):
        rows = slice(part * MODES, (part + 1) * MODES)
        column = jnp.broadcast_to(springs_ref[:, rows], (MODES, MODES)).T
        total_ref[rows, :] = column * own_ref[rows, :]
    for rows, target in halves():
        total_ref[rows, :] += total[target, :]
        sorted_rows[target, :] = total_ref[rows, :]
    partial_ref[...] = dot3(turned_high, turned_low, *split(sorted_rows[...]))


def reduce_late(scale, side_ref, weight_high_ref, weight_low_ref, early_ref, *refs):
    basis_refs, (kept_ref, sent_ref, partial) = refs[:LATE], refs[LATE:]
    total = early_ref[...]
    for k, ref in enumerate(basis_refs):
        total += dot3(weight_high_ref[k], weight_low_ref[k], *split(ref[...]))
    partial[...] = total * scale
    half = MODES // 2
    kept_ref[...] = partial[pl.ds(pl.multiple_of(side_ref[0] * half, half), half), :]
    sent_ref[...] = partial[pl.ds(pl.multiple_of((1 - side_ref[0]) * half, half), half), :]


def add_after(first_ref, second_ref, done_ref, sum_ref):
    sum_ref[...] = first_ref[...] + second_ref[...]


def join(side_ref, mine_ref, other_ref, whole_ref):
    half = MODES // 2
    whole_ref[pl.ds(pl.multiple_of(side_ref[0] * half, half), half), :] = mine_ref[...]
    whole_ref[pl.ds(pl.multiple_of((1 - side_ref[0]) * half, half), half), :] = other_ref[...]


def project_late(high_ref, low_ref, total_ref, *refs):
    basis_refs, (stiff_ref, done_ref) = refs[:LATE], refs[LATE:]
    total = jnp.zeros((ROWS, MODES), jnp.float32)
    for k, ref in enumerate(basis_refs):
        b_high, b_low = split(ref[...])
        total += dot3(high_ref[LINKS - LATE + k], low_ref[LINKS - LATE + k], b_high, b_low)
    for rows, target in halves():
        stiff_ref[rows, :] = total_ref[rows, :] + total[target, :]
    done_ref[...] = jnp.zeros_like(done_ref)


def steps(n, me):
    even, even_four = me % 2 == 0, (me // 4) % 2 == 0

    def one_of(first, when_first):
        return jnp.where(when_first, first, n - first)

    return (
        0,
        one_of(n - 4, even_four),
        one_of(4, even_four),
        one_of(1, even),
        one_of(n - 1, even),
        n // 2,
        one_of(n - 5, even),
        one_of(5, even),
    )


def hand_on(first_ref, outer_ref):
    outer_ref[...] = first_ref[...]


def pick(short, first_ref, second_ref, next_ref, near_ref):
    me = lax.axis_index("row")
    straight = (me % 2 == 1) == ((me // 4) % 2 == 0)

    near_ref[...] = jnp.where(straight, second_ref[...], first_ref[...])
    if short:
        straight = jnp.logical_or(straight, jnp.logical_or(me % 4 == 0, me % 4 == 3))
    next_ref[...] = jnp.where(straight, first_ref[...], second_ref[...])


def shards(basis, springs, tangent_blocks, tile_rows, tile_owner, tile_offset, tile_count):
    n = lax.axis_size("row")
    me = lax.axis_index("row")
    smem = pl.BlockSpec(memory_space=pltpu.SMEM)
    vmem = pl.BlockSpec(memory_space=pltpu.VMEM)
    half, full = jnp.bfloat16, jnp.float32
    params = pltpu.CompilerParams(vmem_limit_bytes=32 * 2**20)

    token = pl.pallas_call(
        prepare,
        out_shape=jax.ShapeDtypeStruct((8, 128), full),
        in_specs=[],
        out_specs=vmem,
        compiler_params=params,
        cost_estimate=pl.CostEstimate(flops=10_000_000_000, bytes_accessed=4_096, transcendentals=0),
        name="prepare",
    )()

    def trade(block, partner):
        return lax.ppermute(block, "row", [(d, partner(d) % n) for d in range(n)])

    def near(d):
        return d ^ 1

    def next_chip(d):
        return d + 1 if d % 2 else d - 1

    def outer(d):
        return d - 4 if d // 4 % 2 else d + 4

    def inner(d):
        return d + 4 if d // 4 % 2 else d - 4

    first = trade(basis, inner)
    second = trade(basis, outer)
    blocks = tangent_blocks.reshape(CAP // 8, 8, HALF, 128).transpose(0, 2, 1, 3).reshape(CAP * HALF, 128)
    high, low, held = pl.pallas_call(
        assemble,
        out_shape=(
            jax.ShapeDtypeStruct((LINKS, ROWS, ROWS), half),
            jax.ShapeDtypeStruct((LINKS, ROWS, ROWS), half),
            jax.ShapeDtypeStruct((ROWS, MODES), full),
        ),
        in_specs=[smem] + [vmem] * 6,
        out_specs=(vmem,) * 3,
        scratch_shapes=[
            pltpu.VMEM(((CAP + 1) * HALF, 128), full),
            pltpu.VMEM((1, CAP), jnp.int32),
            pltpu.SMEM((1, CAP), jnp.int32),
            pltpu.SemaphoreType.DMA(()),
        ],
        compiler_params=params,
        cost_estimate=pl.CostEstimate(flops=10_000_000, bytes_accessed=8_000_000, transcendentals=0),
        name="assemble",
    )(tile_count, tile_rows, tile_owner[:, 0], tile_offset, blocks, basis, token)
    beside, beyond = trade(held, near), trade(held, next_chip)

    ready = pl.pallas_call(
        hand_on,
        out_shape=jax.ShapeDtypeStruct((ROWS, MODES), full),
        in_specs=[vmem],
        out_specs=vmem,
        compiler_params=params,
        cost_estimate=pl.CostEstimate(flops=5_000_000_000, bytes_accessed=300_000, transcendentals=0),
        name="hand_on",
    )(first)
    next_sent, near_sent = pl.pallas_call(
        functools.partial(pick, n == 16),
        out_shape=(jax.ShapeDtypeStruct((ROWS, MODES), full),) * 2,
        in_specs=[vmem] * 2,
        out_specs=(vmem,) * 2,
        compiler_params=params,
        cost_estimate=pl.CostEstimate(flops=0, bytes_accessed=700_000, transcendentals=0),
        name="pick",
    )(first, second)
    if n == 16:
        across = trade(ready, outer)
        far_next = trade(next_sent, lambda d: {0: 7, 7: 0, 8: 15, 15: 8}.get(d, next_chip(d)))
    else:
        across = trade(held, lambda d: d + n // 2)
        far_next = trade(next_sent, next_chip)
    far_near = trade(near_sent, near)

    total, early, weight_high, weight_low = pl.pallas_call(
        project_early,
        out_shape=(
            jax.ShapeDtypeStruct((ROWS, MODES), full),
            jax.ShapeDtypeStruct((MODES, MODES), full),
            jax.ShapeDtypeStruct((LATE, MODES, ROWS), half),
            jax.ShapeDtypeStruct((LATE, MODES, ROWS), half),
        ),
        in_specs=[vmem] * (3 + LINKS - LATE),
        out_specs=(vmem,) * 4,
        scratch_shapes=[pltpu.VMEM((ROWS, MODES), full)],
        compiler_params=params,
        cost_estimate=pl.CostEstimate(flops=20_000_000_000, bytes_accessed=2_500_000, transcendentals=0),
        name="project_early",
    )(high, low, springs.reshape(1, ROWS), held, first, second, beside, beyond)

    side = me
    for shift in (8, 4, 2, 1):
        side = side ^ (side >> shift)
    side = (side & 1).reshape(1)
    piece = jax.ShapeDtypeStruct((MODES // 2, MODES), full)
    kept, sent = pl.pallas_call(
        functools.partial(reduce_late, 1.0 / (basis.shape[0] * n)),
        out_shape=(piece, piece),
        in_specs=[smem] + [vmem] * (3 + LATE),
        out_specs=(vmem,) * 2,
        scratch_shapes=[pltpu.VMEM((MODES, MODES), full)],
        compiler_params=params,
        cost_estimate=pl.CostEstimate(flops=80_000_000, bytes_accessed=700_000, transcendentals=0),
        name="reduce_late",
    )(side, weight_high, weight_low, early, across, far_next, far_near)

    stiff_image, done = pl.pallas_call(
        project_late,
        out_shape=(jax.ShapeDtypeStruct((ROWS, MODES), full), jax.ShapeDtypeStruct((8, 128), full)),
        in_specs=[vmem] * (3 + LATE),
        out_specs=(vmem,) * 2,
        compiler_params=params,
        cost_estimate=pl.CostEstimate(flops=160_000_000, bytes_accessed=1_500_000, transcendentals=0),
        name="project_late",
    )(high, low, total, across, far_next, far_near)

    def swap(block, apart):
        return lax.ppermute(block, "row", [(d, d ^ apart) for d in range(n)])

    mine = kept + swap(sent, 1)
    mine = pl.pallas_call(
        add_after,
        out_shape=piece,
        in_specs=[vmem] * 3,
        out_specs=vmem,
        compiler_params=params,
        name="add_after",
    )(mine, swap(mine, 3), done)
    apart = 4
    while apart < n:
        mine += swap(mine, apart + 1)
        apart *= 2
    reduced = pl.pallas_call(
        join,
        out_shape=jax.ShapeDtypeStruct((MODES, MODES), full),
        in_specs=[smem, vmem, vmem],
        out_specs=vmem,
        compiler_params=params,
        cost_estimate=pl.CostEstimate(flops=0, bytes_accessed=130_000, transcendentals=0),
        name="join",
    )(side, mine, swap(mine, 1))
    return (stiff_image, reduced)


def solution(mesh):
    in_specs = (
        P(("groups", "row"), None),
        P(("groups", "row")),
        P(("groups", "row"), None),
        P(("groups", "row")),
        P(("groups", "row"), None),
        P(("groups", "row")),
        P(("groups", "row")),
    )
    out_specs = (P(("groups", "row"), None), P("groups", None))
    return jax.shard_map(shards, mesh=mesh, in_specs=in_specs, out_specs=out_specs, check_vma=False)
```

```python
import functools

import jax
import jax.numpy as jnp
from jax import lax
from jax.experimental import pallas as pl
from jax.experimental.pallas import tpu as pltpu
from jax.sharding import PartitionSpec as P

B = 64
MODES = 128
BR_DEV = 4
CAP = 128
LINKS = 8
LATE = 3
HALF = B // 2
ROWS = BR_DEV * B


def split(x):
    high = x.astype(jnp.bfloat16)
    return high, (x - high.astype(jnp.float32)).astype(jnp.bfloat16)


def dot3(a_high, a_low, b_high, b_low):
    dot = functools.partial(jnp.dot, preferred_element_type=jnp.float32)
    return dot(a_high, b_high) + (dot(a_low, b_high) + dot(a_high, b_low))


def halves():
    for r in range(BR_DEV):
        for h in range(2):
            yield pl.ds(r * B + h, HALF, stride=2), slice(r * B + h * HALF, r * B + (h + 1) * HALF)


def prepare(token_ref):
    token_ref[...] = jnp.zeros_like(token_ref)


def assemble(count_ref, rows_ref, owner_ref, offset_ref, blocks_ref, token_ref, high_ref, low_ref, dense, placed, place, arrived):
    n, me = lax.axis_size("row"), lax.axis_index("row")
    away = lax.rem(owner_ref[...].reshape(1, CAP) - me + n, n)
    link = jnp.zeros_like(away)
    for k, step in enumerate(steps(n, me)):
        link = jnp.where(away == step, k, link)
    target = (link * BR_DEV + rows_ref[...].reshape(1, CAP)) * BR_DEV + offset_ref[...].reshape(1, CAP)
    slot = lax.broadcasted_iota(jnp.int32, (1, CAP), 1)
    placed[...] = jnp.where(slot < count_ref[0], target, CAP)
    copy = pltpu.make_async_copy(placed, place, arrived)
    copy.start()
    dense[...] = jnp.zeros_like(dense)
    copy.wait()

    @pl.loop(0, CAP // 8)
    def _(group):
        for k in range(8):
            block = blocks_ref[pl.ds(group * (8 * HALF) + k, HALF, stride=8), :]
            target = pl.ds(pl.multiple_of(place[0, group * 8 + k] * HALF, HALF), HALF)
            dense[target, :] += block

    left = lax.broadcasted_iota(jnp.int32, (HALF, 128), 1) < B

    @pl.loop(0, LINKS)
    def _(link):
        for r in range(BR_DEV):
            for pair in range(BR_DEV // 2):
                start = ((link * BR_DEV + r) * BR_DEV + 2 * pair) * HALF
                first = dense[pl.ds(pl.multiple_of(start, HALF), HALF), :]
                second = dense[pl.ds(pl.multiple_of(start + HALF, HALF), HALF), :]
                even = jnp.where(left, first, pltpu.roll(second, B, 1))
                odd = jnp.where(left, pltpu.roll(first, B, 1), second)
                for h, part in enumerate((even, odd)):
                    high, low = split(part)
                    rows = slice(r * B + h * HALF, r * B + (h + 1) * HALF)
                    high_ref[link, rows, pair * 128:(pair + 1) * 128] = high
                    low_ref[link, rows, pair * 128:(pair + 1) * 128] = low


def project_early(high_ref, low_ref, springs_ref, *refs):
    basis_refs, (total_ref, partial_ref, weight_high_ref, weight_low_ref, sorted_rows) = refs[:-5], refs[-5:]
    own_ref = basis_refs[0]
    for rows, target in halves():
        sorted_rows[target, :] = own_ref[rows, :]
    turned_high, turned_low = split(sorted_rows[...].T)
    for k in range(LATE):
        link = LINKS - LATE + k
        high, low = split(dot3(turned_high, turned_low, high_ref[link], low_ref[link]))
        weight_high_ref[k] = high
        weight_low_ref[k] = low
    total = jnp.zeros((ROWS, MODES), jnp.float32)
    for link, ref in enumerate(basis_refs):
        b_high, b_low = split(ref[...])
        total += dot3(high_ref[link], low_ref[link], b_high, b_low)
    for part in range(ROWS // MODES):
        rows = slice(part * MODES, (part + 1) * MODES)
        column = jnp.broadcast_to(springs_ref[:, rows], (MODES, MODES)).T
        total_ref[rows, :] = column * own_ref[rows, :]
    for rows, target in halves():
        total_ref[rows, :] += total[target, :]
        sorted_rows[target, :] = total_ref[rows, :]
    partial_ref[...] = dot3(turned_high, turned_low, *split(sorted_rows[...]))


def reduce_late(scale, side_ref, weight_high_ref, weight_low_ref, early_ref, *refs):
    basis_refs, (kept_ref, sent_ref, partial) = refs[:LATE], refs[LATE:]
    total = early_ref[...]
    for k, ref in enumerate(basis_refs):
        total += dot3(weight_high_ref[k], weight_low_ref[k], *split(ref[...]))
    partial[...] = total * scale
    half = MODES // 2
    kept_ref[...] = partial[pl.ds(pl.multiple_of(side_ref[0] * half, half), half), :]
    sent_ref[...] = partial[pl.ds(pl.multiple_of((1 - side_ref[0]) * half, half), half), :]


def add_after(first_ref, second_ref, done_ref, sum_ref):
    sum_ref[...] = first_ref[...] + second_ref[...]


def join(side_ref, mine_ref, other_ref, whole_ref):
    half = MODES // 2
    whole_ref[pl.ds(pl.multiple_of(side_ref[0] * half, half), half), :] = mine_ref[...]
    whole_ref[pl.ds(pl.multiple_of((1 - side_ref[0]) * half, half), half), :] = other_ref[...]


def project_late(high_ref, low_ref, total_ref, *refs):
    basis_refs, (stiff_ref, done_ref) = refs[:LATE], refs[LATE:]
    total = jnp.zeros((ROWS, MODES), jnp.float32)
    for k, ref in enumerate(basis_refs):
        b_high, b_low = split(ref[...])
        total += dot3(high_ref[LINKS - LATE + k], low_ref[LINKS - LATE + k], b_high, b_low)
    for rows, target in halves():
        stiff_ref[rows, :] = total_ref[rows, :] + total[target, :]
    done_ref[...] = jnp.zeros_like(done_ref)


def steps(n, me):
    even, even_four = me % 2 == 0, (me // 4) % 2 == 0

    def one_of(first, when_first):
        return jnp.where(when_first, first, n - first)

    return (
        0,
        one_of(n - 4, even_four),
        one_of(4, even_four),
        one_of(1, even),
        one_of(n - 1, even),
        one_of(n - 5, even),
        n // 2,
        one_of(5, even),
    )


def pick(short, first_ref, second_ref, next_ref, outer_ref, near_ref):
    outer_ref[...] = first_ref[...]
    me = lax.axis_index("row")
    straight = (me % 2 == 1) == ((me // 4) % 2 == 0)

    near_ref[...] = jnp.where(straight, second_ref[...], first_ref[...])
    if short:
        straight = jnp.logical_or(straight, jnp.logical_or(me % 4 == 0, me % 4 == 3))
    next_ref[...] = jnp.where(straight, first_ref[...], second_ref[...])


def shards(basis, springs, tangent_blocks, tile_rows, tile_owner, tile_offset, tile_count):
    n = lax.axis_size("row")
    me = lax.axis_index("row")
    smem = pl.BlockSpec(memory_space=pltpu.SMEM)
    vmem = pl.BlockSpec(memory_space=pltpu.VMEM)
    half, full = jnp.bfloat16, jnp.float32
    params = pltpu.CompilerParams(vmem_limit_bytes=32 * 2**20)

    token = pl.pallas_call(
        prepare,
        out_shape=jax.ShapeDtypeStruct((8, 128), full),
        in_specs=[],
        out_specs=vmem,
        compiler_params=params,
        cost_estimate=pl.CostEstimate(flops=10_000_000_000, bytes_accessed=4_096, transcendentals=0),
        name="prepare",
    )()

    def trade(block, partner):
        return lax.ppermute(block, "row", [(d, partner(d) % n) for d in range(n)])

    def near(d):
        return d ^ 1

    def next_chip(d):
        return d + 1 if d % 2 else d - 1

    def outer(d):
        return d - 4 if d // 4 % 2 else d + 4

    def inner(d):
        return d + 4 if d // 4 % 2 else d - 4

    first = trade(basis, inner)
    second = trade(basis, outer)
    beside, beyond = trade(basis, near), trade(basis, next_chip)
    blocks = tangent_blocks.reshape(CAP // 8, 8, HALF, 128).transpose(0, 2, 1, 3).reshape(CAP * HALF, 128)
    high, low = pl.pallas_call(
        assemble,
        out_shape=(
            jax.ShapeDtypeStruct((LINKS, ROWS, ROWS), half),
            jax.ShapeDtypeStruct((LINKS, ROWS, ROWS), half),
        ),
        in_specs=[smem] + [vmem] * 5,
        out_specs=(vmem,) * 2,
        scratch_shapes=[
            pltpu.VMEM(((CAP + 1) * HALF, 128), full),
            pltpu.VMEM((1, CAP), jnp.int32),
            pltpu.SMEM((1, CAP), jnp.int32),
            pltpu.SemaphoreType.DMA(()),
        ],
        compiler_params=params,
        cost_estimate=pl.CostEstimate(flops=10_000_000, bytes_accessed=8_000_000, transcendentals=0),
        name="assemble",
    )(tile_count, tile_rows, tile_owner[:, 0], tile_offset, blocks, token)

    next_sent, outer_sent, near_sent = pl.pallas_call(
        functools.partial(pick, n == 16),
        out_shape=(jax.ShapeDtypeStruct((ROWS, MODES), full),) * 3,
        in_specs=[vmem] * 2,
        out_specs=(vmem,) * 3,
        compiler_params=params,
        cost_estimate=pl.CostEstimate(flops=0, bytes_accessed=700_000, transcendentals=0),
        name="pick",
    )(first, second)
    if n == 16:
        across = trade(outer_sent, outer)
        far_next = trade(next_sent, lambda d: {0: 7, 7: 0, 8: 15, 15: 8}.get(d, next_chip(d)))
    else:
        across = trade(basis, lambda d: d + n // 2)
        far_next = trade(next_sent, next_chip)
    far_near = trade(near_sent, near)

    total, early, weight_high, weight_low = pl.pallas_call(
        project_early,
        out_shape=(
            jax.ShapeDtypeStruct((ROWS, MODES), full),
            jax.ShapeDtypeStruct((MODES, MODES), full),
            jax.ShapeDtypeStruct((LATE, MODES, ROWS), half),
            jax.ShapeDtypeStruct((LATE, MODES, ROWS), half),
        ),
        in_specs=[vmem] * (3 + LINKS - LATE),
        out_specs=(vmem,) * 4,
        scratch_shapes=[pltpu.VMEM((ROWS, MODES), full)],
        compiler_params=params,
        cost_estimate=pl.CostEstimate(flops=20_000_000_000, bytes_accessed=2_500_000, transcendentals=0),
        name="project_early",
    )(high, low, springs.reshape(1, ROWS), basis, first, second, beside, beyond)

    side = me
    for shift in (8, 4, 2, 1):
        side = side ^ (side >> shift)
    side = (side & 1).reshape(1)
    piece = jax.ShapeDtypeStruct((MODES // 2, MODES), full)
    kept, sent = pl.pallas_call(
        functools.partial(reduce_late, 1.0 / (basis.shape[0] * n)),
        out_shape=(piece, piece),
        in_specs=[smem] + [vmem] * (3 + LATE),
        out_specs=(vmem,) * 2,
        scratch_shapes=[pltpu.VMEM((MODES, MODES), full)],
        compiler_params=params,
        cost_estimate=pl.CostEstimate(flops=80_000_000, bytes_accessed=700_000, transcendentals=0),
        name="reduce_late",
    )(side, weight_high, weight_low, early, far_next, across, far_near)

    stiff_image, done = pl.pallas_call(
        project_late,
        out_shape=(jax.ShapeDtypeStruct((ROWS, MODES), full), jax.ShapeDtypeStruct((8, 128), full)),
        in_specs=[vmem] * (3 + LATE),
        out_specs=(vmem,) * 2,
        compiler_params=params,
        cost_estimate=pl.CostEstimate(flops=160_000_000, bytes_accessed=1_500_000, transcendentals=0),
        name="project_late",
    )(high, low, total, far_next, across, far_near)

    def swap(block, apart):
        return lax.ppermute(block, "row", [(d, d ^ apart) for d in range(n)])

    mine = kept + swap(sent, 1)
    mine = pl.pallas_call(
        add_after,
        out_shape=piece,
        in_specs=[vmem] * 3,
        out_specs=vmem,
        compiler_params=params,
        name="add_after",
    )(mine, swap(mine, 3), done)
    apart = 4
    while apart < n:
        mine += swap(mine, apart + 1)
        apart *= 2
    reduced = pl.pallas_call(
        join,
        out_shape=jax.ShapeDtypeStruct((MODES, MODES), full),
        in_specs=[smem, vmem, vmem],
        out_specs=vmem,
        compiler_params=params,
        cost_estimate=pl.CostEstimate(flops=0, bytes_accessed=130_000, transcendentals=0),
        name="join",
    )(side, mine, swap(mine, 1))
    return (stiff_image, reduced)


def solution(mesh):
    in_specs = (
        P(("groups", "row"), None),
        P(("groups", "row")),
        P(("groups", "row"), None),
        P(("groups", "row")),
        P(("groups", "row"), None),
        P(("groups", "row")),
        P(("groups", "row")),
    )
    out_specs = (P(("groups", "row"), None), P("groups", None))
    return jax.shard_map(shards, mesh=mesh, in_specs=in_specs, out_specs=out_specs, check_vma=False)
```
